32 devices in a mesh: ep: 8 (over z, y), tp: 4 (over x, core).
Axes of the slice: x: 2, y: 2, z: 4, core: 2. Of those that a mesh axis runs over, the one named last changes fastest.
Arguments:
- tokens: bfloat16 [4096, 1536], P(('ep', 'tp')), may hold values from -6 to 6
- norm_gain: float32 [1536], replicated, may hold values from 0.5 to 1.5
- query_matrix: bfloat16 [1536, 1536], P(None, 'tp'), may hold values from -0.15625 to 0.15625
- key_matrix: bfloat16 [1536, 512], P(None, 'tp'), may hold values from -0.15625 to 0.15625
- value_matrix: bfloat16 [1536, 512], P(None, 'tp'), may hold values from -0.15625 to 0.15625
- out_weight: bfloat16 [1536, 1536], P('tp'), may hold values from -1.25 to 1.25
- moe_gain: float32 [1536], replicated, may hold values from 0.5 to 1.5
- router_weight: bfloat16 [1536, 40], replicated, may hold values from -0.0390625 to 0.0390625
- gate_weight: bfloat16 [40, 1536, 512], P('ep', None, 'tp'), may hold values from -0.15625 to 0.15625
- up_weight: bfloat16 [40, 1536, 512], P('ep', None, 'tp'), may hold values from -0.15625 to 0.15625
- down_weight: bfloat16 [40, 512, 1536], P('ep', 'tp'), may hold values from -2 to 2
- cotangent: bfloat16 [4096, 1536], P(('ep', 'tp')), may hold values from -6 to 6
- expert_ids: int32 [4096, 8], P(('ep', 'tp')), may hold values from 0 to 39, all different within a row; in each aligned block of 128 rows (0 to 127, 128 to 255, ...) at most 32 rows name the same one
- segments: int32 [8, 512], P('ep'), may hold values from 0 to 3, never falling along the last dimension, each value on 1 to 256 neighbouring positions
- valid_mask: int32 [8, 512], P('ep'), may hold values from 0 to 1, as said below
Outputs:
- output: bfloat16 [4096, 1536], P(('ep', 'tp'))
- input_grad: float32 [4096, 1536], P(('ep', 'tp'))
- norm_gain_grad: float32 [1536], replicated
- query_grad: float32 [1536, 1536], P(None, 'tp')
- key_grad: float32 [1536, 512], P(None, 'tp')
- value_grad: float32 [1536, 512], P(None, 'tp')
- out_grad: float32 [1536, 1536], P('tp')
- moe_gain_grad: float32 [1536], replicated
- router_grad: float32 [1536, 40], replicated
- gate_grad: float32 [40, 1536, 512], P('ep', None, 'tp')
- up_grad: float32 [40, 1536, 512], P('ep', None, 'tp')
- down_grad: float32 [40, 512, 1536], P('ep', 'tp')
The draws below stay inside these ranges and needn't reach their ends.
Inputs may be any that keep to these rules, and one draw needn't show every extreme that they name: `expert_ids`: each row names 8 different experts. Among the 128 rows of one device (aligned blocks of 128 rows) no expert is named by more than 32 rows, a bound that some block reaches. `segments`: document numbers never fall along a sequence; each document has 1 to 256 tokens, one exactly 256. `valid_mask`: in each sequence the ones form a prefix of 384 tokens or more; the first sequence has no padding.
All inputs are finite; a program needn't handle non-finite values.
Results may differ from the reference program's by a relative error of at most 0.015.
Values may be sent and summed in bfloat16 or wider, within the bound.
No kernel may reach another device: no remote copies, remote signals or barrier semaphores. Data moves between devices by JAX's collectives and lax.ppermute only.
A program may use at most 320 MiB of HBM per device.

```python
import math
import jax
import jax.numpy as jnp
import numpy as np
from jax import lax

MODEL_WIDTH = 1536
QUERY_HEADS = 24
KEY_VALUE_HEADS = 8
HEAD_SIZE_DIM = 64
FFE = 512
TOP = 8
TOK_DEV = 512
EXPERTS = 40
SEQS = 8
TOKENS = 4096
TQ = 128
CAP = 32
DOCS = 4
DOC_MOST = 256


def draw_valid_mask(key, part):
    lengths = jax.random.randint(key, (SEQS,), 3 * TOK_DEV // 4, TOK_DEV + 1)
    lengths = lengths.at[0].set(TOK_DEV)
    return (jnp.arange(TOK_DEV)[None, :] < lengths[:, None]).astype(jnp.int32)


def shard_levels(own_key, dims, pieces, least, largest):
    def one(dim, parts):
        steps = jax.random.uniform(jax.random.fold_in(jax.random.fold_in(own_key, 6), dim), (parts,), jnp.float32, least / len(pieces), largest / len(pieces))
        return jnp.repeat(jnp.exp(steps), dims[dim] // parts).reshape((-1,) + (1,) * (len(dims) - dim - 1))

    gain = one(*pieces[0])
    for cut in pieces[1:]:
        gain = gain * one(*cut)
    return gain


def split_up(amount, total, reach, lean):
    weights = [(1 << 20) // math.isqrt(grade ** lean) + 1 for grade in range(2, amount + 1)]
    spare, counts = total - reach - (amount - 1), [1] * (amount - 1)
    while spare > 0:
        free = [i for i in range(amount - 1) if counts[i] < reach]
        whole, remaining = sum([weights[i] for i in free]), spare
        for i in free:
            extra = min(reach - counts[i], max(1, remaining * weights[i] // whole), spare)
            counts[i] = counts[i] + extra
            spare = spare - extra
    return np.array([reach] + counts)


def ragged(rng, count, total, reach, lean):
    if count == 2:
        one = jax.random.randint(rng, (), max(1, total - reach), min(reach, total - 1) + 1)
        return jnp.stack([one, total - one])
    sizes = jnp.asarray(split_up(count, total, reach, lean), jnp.int32)
    couples = (count - 1) // 2
    source_of, receiver = sizes[1:1 + 2 * couples:2], sizes[2:2 + 2 * couples:2]
    room = jnp.minimum(source_of - 1, reach - receiver)
    shifted = jax.random.randint(jax.random.fold_in(rng, 1), (couples,), 0, 1 << 20) % (room + 1)
    sizes = sizes.at[1:1 + 2 * couples:2].set(source_of - shifted).at[2:2 + 2 * couples:2].set(receiver + shifted)
    return sizes[jax.random.permutation(jax.random.fold_in(rng, 2), count)]


def deal_out(stream_key, own, number, rows, amount, top, most, slope):
    sequence = jax.random.permutation(stream_key, amount)
    crowded, common = shares(amount, rows * top, most, slope, True), shares(amount, rows * top, most, slope, False)
    places = jnp.arange(amount)

    def named(tallies, turn):
        used = int((tallies > 0).sum())
        fixed = max(1, used // 4)
        moved = fixed + (places - fixed + turn * (used - fixed)) % max(1, amount - fixed)
        return jnp.zeros((amount,), jnp.int32).at[sequence[jnp.where(places < fixed, places, moved)]].set(jnp.asarray(tallies, jnp.int32))

    tallies = jnp.where(number % 4 == 0, named(crowded, number // 4), named(common, number - number // 4 - 1))
    mixed = jax.random.permutation(jax.random.fold_in(own, 3), amount)
    source_of, receiver = mixed[0:amount // 2 * 2:2], mixed[1:amount // 2 * 2:2]
    slack = jnp.minimum(tallies[source_of] - 1, most - tallies[receiver]) // 2
    slack = jnp.where((source_of == sequence[0]) | (receiver == sequence[0]) | (tallies[receiver] == 0), 0, jnp.maximum(slack, 0))
    moved = jax.random.randint(jax.random.fold_in(own, 4), (amount // 2,), 0, 1 << 20) % (slack + 1)
    tallies = tallies.at[source_of].add(-moved).at[receiver].add(moved)
    items = jnp.searchsorted(jnp.cumsum(tallies), jnp.arange(rows * top), side="right").astype(jnp.int32)
    table = items.reshape(top, rows).T
    table = table[jax.random.permutation(jax.random.fold_in(own, 1), rows)]
    turn = jax.random.randint(jax.random.fold_in(own, 2), (rows, 1), 0, top)
    return jnp.take_along_axis(table, (jnp.arange(top)[None, :] + turn) % top, axis=1)


def shares(number_of, total, reach, lean, full):
    weights = [(1 << 20) // math.isqrt(standing ** lean) + 1 for standing in range(1, number_of + 1)]
    largest = reach if full else min(reach, max(-(-total // number_of), total * weights[0] // sum(weights)))
    least = 1 if total - largest >= number_of - 1 else 0
    given, surplus = [largest] + [least] * (number_of - 1), total - largest - least * (number_of - 1)
    while surplus > 0:
        movable = [i for i in range(1, number_of) if given[i] < largest] or [i for i in range(1, number_of) if given[i] < reach]
        whole, budget = sum([weights[i] for i in movable]), surplus
        for i in movable:
            more = min(reach - given[i], max(1, budget * weights[i] // whole), surplus)
            given[i] = given[i] + more
            surplus = surplus - more
    return np.array(given)


def noise(own_key, extent, deviation, limit, shards=(), kind=jnp.bfloat16):
    drawn = jax.random.normal(own_key, extent, jnp.float32) * deviation
    if len(shards) > 0:
        drawn = shard_levels(own_key, extent, shards, -0.22, 0.18) * drawn
    return jnp.clip(drawn, min=-limit, max=limit).astype(kind)


def setup_inputs(seed: int = 0) -> dict:
    arg_keys = jax.random.split(jax.random.key(seed), 16)
    tokens = noise(arg_keys[0], (TOKENS, MODEL_WIDTH), 1.0, 6.0, ((0, 32),))
    norm_gain = jnp.clip(1.0 + 0.1 * jax.random.normal(arg_keys[1], (MODEL_WIDTH,), jnp.float32), 0.5, 1.5)
    query_matrix = noise(arg_keys[2], (MODEL_WIDTH, QUERY_HEADS * HEAD_SIZE_DIM), MODEL_WIDTH ** -0.5, 0.15625, ((1, 4),))
    key_matrix = noise(arg_keys[3], (MODEL_WIDTH, KEY_VALUE_HEADS * HEAD_SIZE_DIM), MODEL_WIDTH ** -0.5, 0.15625, ((1, 4),))
    value_matrix = noise(arg_keys[4], (MODEL_WIDTH, KEY_VALUE_HEADS * HEAD_SIZE_DIM), MODEL_WIDTH ** -0.5, 0.15625, ((1, 4),))
    out_weight = noise(arg_keys[5], (QUERY_HEADS * HEAD_SIZE_DIM, MODEL_WIDTH), (max(1, QUERY_HEADS * HEAD_SIZE_DIM // 64)) ** -0.5, 1.25, ((0, 4),))
    moe_gain = jnp.clip(1.0 + 0.1 * jax.random.normal(arg_keys[6], (MODEL_WIDTH,), jnp.float32), 0.5, 1.5)
    router_weight = noise(arg_keys[7], (MODEL_WIDTH, EXPERTS), (16 * MODEL_WIDTH) ** -0.5, 0.0390625)
    gate_weight = noise(arg_keys[8], (EXPERTS, MODEL_WIDTH, FFE), MODEL_WIDTH ** -0.5, 0.15625, ((0, 8), (2, 4)))
    up_weight = noise(arg_keys[9], (EXPERTS, MODEL_WIDTH, FFE), MODEL_WIDTH ** -0.5, 0.15625, ((0, 8), (2, 4)))
    down_weight = noise(arg_keys[10], (EXPERTS, FFE, MODEL_WIDTH), (max(1, FFE // 64)) ** -0.5, 2.0, ((0, 8), (1, 4)))
    cotangent = noise(arg_keys[11], (TOKENS, MODEL_WIDTH), 1.0, 6.0, ((0, 32),))
    expert_ids_keys = jax.random.split(jax.random.fold_in(arg_keys[12], 1), TOKENS // TQ)
    expert_ids_turns = jax.random.permutation(jax.random.fold_in(arg_keys[12], 3), TOKENS // TQ)
    expert_ids = jax.vmap(lambda own, number: deal_out(jax.random.fold_in(arg_keys[12], 2), own, number, TQ, EXPERTS, TOP, CAP, 2))(expert_ids_keys, expert_ids_turns).reshape((TOKENS, TOP))
    segments = jax.vmap(lambda own: jnp.searchsorted(jnp.cumsum(ragged(own, DOCS, TOK_DEV, DOC_MOST, 1)), jnp.arange(TOK_DEV), side="right"))(jax.random.split(arg_keys[13], SEQS)).reshape((SEQS, TOK_DEV)).astype(jnp.int32)
    valid_mask = draw_valid_mask(jax.random.fold_in(arg_keys[15], 71), 0)
    return dict(tokens=tokens, norm_gain=norm_gain, query_matrix=query_matrix, key_matrix=key_matrix, value_matrix=value_matrix, out_weight=out_weight, moe_gain=moe_gain, router_weight=router_weight, gate_weight=gate_weight, up_weight=up_weight, down_weight=down_weight, cotangent=cotangent, expert_ids=expert_ids, segments=segments, valid_mask=valid_mask)


@jax.custom_vjp
def lower_precision(v):
    return lax.optimization_barrier(v.astype(jnp.bfloat16)).astype(jnp.float32)

@jax.custom_vjp
def lower_precision_backward(v):
    return v

def low_keep(v):
    return (lower_precision(v), None)

def low_pass(kept, grad):
    return (grad,)

def back_keep(v):
    return (v, None)

def back_low(kept, grad):
    return (lower_precision(grad),)
lower_precision.defvjp(low_keep, low_pass)
lower_precision_backward.defvjp(back_keep, back_low)
EPS = 1e-06
HIGH_PRECISION = lax.Precision.HIGHEST

def rms_norm(activation, gain_vec):
    factor = lax.rsqrt(lax.optimization_barrier(jnp.mean(activation * activation, axis=-1, keepdims=True)) + EPS)
    return activation * factor * gain_vec

def rotate(vectors, cos_table, sin_table):
    half_size = vectors.shape[-1] // 2
    first_half = vectors[..., :half_size]
    second_half = vectors[..., half_size:]
    return jnp.concatenate([first_half * cos_table - second_half * sin_table, second_half * cos_table + first_half * sin_table], axis=-1)

def angle_tables(span_length, head_size):
    half_size = head_size // 2
    inverse = jnp.exp(-math.log(10000.0) * jnp.arange(half_size, dtype=jnp.float32) * 2.0 / head_size)
    angles = jnp.arange(span_length, dtype=jnp.float32)[:, None] * inverse[None, :]
    return (jnp.cos(angles), jnp.sin(angles))

def swiglu(gate_val, up_val):
    return jax.nn.silu(gate_val) * up_val

def attend(normalized_sequence, segment_row, live_row, query_matrix, key_matrix, value_matrix):
    span_length = normalized_sequence.shape[0]
    group_factor = QUERY_HEADS // KEY_VALUE_HEADS
    query_unrotated = lower_precision_backward(jnp.dot(normalized_sequence, query_matrix, precision=HIGH_PRECISION)).reshape(span_length, KEY_VALUE_HEADS, group_factor, HEAD_SIZE_DIM)
    key_unrotated = lower_precision_backward(jnp.dot(normalized_sequence, key_matrix, precision=HIGH_PRECISION)).reshape(span_length, KEY_VALUE_HEADS, HEAD_SIZE_DIM)
    value_vectors = lower_precision(lower_precision_backward(jnp.dot(normalized_sequence, value_matrix, precision=HIGH_PRECISION))).reshape(span_length, KEY_VALUE_HEADS, HEAD_SIZE_DIM)
    cos_table, sin_table = angle_tables(span_length, HEAD_SIZE_DIM)
    query_val = lower_precision(rotate(query_unrotated, cos_table[:, None, None, :], sin_table[:, None, None, :]))
    key_val = lower_precision(rotate(key_unrotated, cos_table[:, None, :], sin_table[:, None, :]))
    scores = lower_precision_backward(jnp.einsum('qgrd,kgd->grqk', query_val, key_val, precision=HIGH_PRECISION) * (1.0 / math.sqrt(HEAD_SIZE_DIM)))
    places = jnp.arange(span_length)
    allowed = (segment_row[:, None] == segment_row[None, :]) & (places[None, :] <= places[:, None]) & ((live_row[None, :] > 0) | (places[None, :] == places[:, None]))
    scores = jnp.where(allowed[None, None], scores, -1e+30)
    probs = lower_precision(jax.nn.softmax(scores, axis=-1))
    mixed = jnp.einsum('grqk,kgd->qgrd', probs, value_vectors, precision=HIGH_PRECISION).reshape(span_length, QUERY_HEADS * HEAD_SIZE_DIM)
    return lower_precision(lower_precision_backward(mixed))

def reference(tokens, norm_gain, query_matrix, key_matrix, value_matrix, out_weight, moe_gain, router_weight, gate_weight, up_weight, down_weight, cotangent, expert_ids, segments, valid_mask):
    seq_count = segments.shape[0]
    seq_len = segments.shape[1]
    chosen = lax.optimization_barrier(jnp.sum(jax.nn.one_hot(expert_ids, EXPERTS, dtype=jnp.float32), axis=1)) * valid_mask.reshape(-1, 1).astype(jnp.float32)

    def forward(x_in, gain_one, wq_in, wk_in, wv_in, wo_in, gain_two, wr_in, wg_in, wu_in, wd_in):
        normed = lower_precision(rms_norm(x_in, gain_one))

        def one_sequence(packed):
            return attend(packed[0], packed[1], packed[2], wq_in, wk_in, wv_in)
        mixed = lax.map(jax.checkpoint(one_sequence), (normed.reshape(seq_count, seq_len, -1), segments, valid_mask))
        branch = lower_precision_backward(jnp.dot(mixed.reshape(-1, QUERY_HEADS * HEAD_SIZE_DIM), wo_in, precision=HIGH_PRECISION))
        middle = x_in + branch
        moe_in = lower_precision(rms_norm(middle, gain_two))
        router = jax.nn.softmax(jnp.dot(moe_in, wr_in, precision=HIGH_PRECISION), axis=-1)
        combine = chosen * router

        def one_expert(running, packed):
            gate_w, up_w, down_w, column = packed
            copied = lower_precision_backward(moe_in)
            gate_val = lower_precision_backward(jnp.dot(copied, gate_w, precision=HIGH_PRECISION))
            up_val = lower_precision_backward(jnp.dot(copied, up_w, precision=HIGH_PRECISION))
            hidden = lower_precision(swiglu(gate_val, up_val))
            result = lower_precision(lower_precision_backward(jnp.dot(hidden, down_w, precision=HIGH_PRECISION)))
            return (running + column[:, None] * result, None)
        expert_sum, _ = lax.scan(jax.checkpoint(one_expert), jnp.zeros_like(middle), (wg_in, wu_in, wd_in, combine.T))
        return middle + expert_sum
    floats = tuple((array_in.astype(jnp.float32) for array_in in (tokens, norm_gain, query_matrix, key_matrix, value_matrix, out_weight, moe_gain, router_weight, gate_weight, up_weight, down_weight)))
    output, pullback = jax.vjp(forward, *floats)
    grads = pullback(cotangent.astype(jnp.float32))
    return (output.astype(jnp.bfloat16), grads[0], grads[1], grads[2], grads[3], grads[4], grads[5], grads[6], grads[7], grads[8], grads[9], grads[10])
```

```python
import math

import jax
import jax.numpy as jnp
from jax import lax
from jax.sharding import PartitionSpec as P

HEAD_SIZE_DIM = 64


EPS = 1e-06
HIGH_PRECISION = lax.Precision.HIGHEST


def rms_norm(activation, gain_vec):
    factor = lax.rsqrt(jnp.mean(activation * activation, axis=-1, keepdims=True) + EPS)
    return activation * factor * gain_vec


def rotate(vectors, cos_table, sin_table):
    half_size = vectors.shape[-1] // 2
    first_half = vectors[..., :half_size]
    second_half = vectors[..., half_size:]
    return jnp.concatenate(
        [
            first_half * cos_table - second_half * sin_table,
            second_half * cos_table + first_half * sin_table,
        ],
        axis=-1,
    )


def angle_tables(span_length, head_size):
    half_size = head_size // 2
    inverse = jnp.exp(
        -math.log(10000.0) * jnp.arange(half_size, dtype=jnp.float32) * 2.0 / head_size
    )
    angles = jnp.arange(span_length, dtype=jnp.float32)[:, None] * inverse[None, :]
    return (jnp.cos(angles), jnp.sin(angles))


def swiglu(gate_val, up_val):
    return jax.nn.silu(gate_val) * up_val


def softmax_rows(logits):
    return jax.nn.softmax(logits, axis=-1)


def block_mask(segment_row, live_row, offset, height):
    span_length = segment_row.shape[0]
    key_places = jnp.arange(span_length)
    query_places = offset + jnp.arange(height)
    same_doc = segment_row[:, None] == segment_row[None, :]
    causal = key_places[None, :] <= query_places[:, None]
    usable = (live_row[None, :] > 0) | (key_places[None, :] == query_places[:, None])
    return same_doc & causal & usable


def block_scores(query_block, key_val, allowed, factor):
    scores = (
        jnp.einsum("qgrd,kgd->grqk", query_block, key_val, preferred_element_type=jnp.float32)
        * factor
    )
    return jnp.where(allowed[None, None], scores, -1e30)


def group_rows(boxes):
    return lax.all_gather(boxes, "tp", axis=0, tiled=True)


def dispatch_rows(boxes):
    return lax.all_to_all(boxes, "ep", split_axis=1, concat_axis=1, tiled=True)


def return_rows(boxes):
    return lax.all_to_all(boxes, "ep", split_axis=1, concat_axis=1, tiled=True)


def local(
    tokens,
    norm_gain,
    query_matrix,
    key_matrix,
    value_matrix,
    out_weight,
    moe_gain,
    router_weight,
    gate_weight,
    up_weight,
    down_weight,
    cotangent,
    expert_ids,
    segments,
    valid_mask,
):
    quarter = tokens.shape[0]
    width = tokens.shape[1]
    groups = lax.axis_size("tp")
    owners = lax.axis_size("ep")
    my_part = lax.axis_index("tp")
    seq_len = quarter * groups
    head_size = HEAD_SIZE_DIM
    kv_heads = key_matrix.shape[1] // head_size
    q_heads = query_matrix.shape[1] // head_size
    group_factor = q_heads // kv_heads
    local_experts = gate_weight.shape[0]
    experts_all = router_weight.shape[1]
    chosen_count = expert_ids.shape[1]
    slots = max(8, 3 * quarter * chosen_count // (2 * experts_all) // 8 * 8)
    factor = 1.0 / math.sqrt(head_size)
    segment_row = segments[0]
    live_row = valid_mask[0]
    x_float = tokens.astype(jnp.float32)
    normed = rms_norm(x_float, norm_gain).astype(jnp.bfloat16)
    normed_all = lax.all_gather(normed, "tp", axis=0, tiled=True)
    query_unrotated = jnp.dot(normed_all, query_matrix, preferred_element_type=jnp.float32).reshape(
        seq_len, kv_heads, group_factor, head_size
    )
    key_unrotated = jnp.dot(normed_all, key_matrix, preferred_element_type=jnp.float32).reshape(
        seq_len, kv_heads, head_size
    )
    value_vectors = (
        jnp.dot(normed_all, value_matrix, preferred_element_type=jnp.float32)
        .astype(jnp.bfloat16)
        .reshape(seq_len, kv_heads, head_size)
    )
    cos_table, sin_table = angle_tables(seq_len, head_size)
    cos_query = cos_table[:, None, None, :]
    sin_query = sin_table[:, None, None, :]
    cos_key = cos_table[:, None, :]
    sin_key = sin_table[:, None, :]
    query_val = rotate(query_unrotated, cos_query, sin_query).astype(jnp.bfloat16)
    key_val = rotate(key_unrotated, cos_key, sin_key).astype(jnp.bfloat16)
    height = min(512, seq_len)
    offset = 0
    allowed = block_mask(segment_row, live_row, offset, height)
    scores = block_scores(query_val, key_val, allowed, factor)
    peak = jnp.max(scores, axis=-1, keepdims=True)
    expo = jnp.exp(scores - peak)
    denom = jnp.sum(expo, axis=-1, keepdims=True)
    weights = (expo / denom).astype(jnp.bfloat16)
    mixed = jnp.einsum("grqk,kgd->qgrd", weights, value_vectors, preferred_element_type=jnp.float32)
    outputs = mixed.reshape(height, q_heads * head_size)
    log_sums = [peak + jnp.log(denom)]
    attended = outputs.astype(jnp.bfloat16)
    branch = lax.psum_scatter(
        jnp.dot(attended, out_weight, preferred_element_type=jnp.float32),
        "tp",
        scatter_dimension=0,
        tiled=True,
    )
    middle = x_float + branch
    moe_in = rms_norm(middle, moe_gain).astype(jnp.bfloat16)
    logits = jnp.dot(moe_in, router_weight, preferred_element_type=jnp.float32)
    router = softmax_rows(logits)
    my_valid = lax.dynamic_slice_in_dim(live_row, my_part * quarter, quarter, 0)
    valid_float = my_valid.astype(jnp.float32)
    picked = jnp.take_along_axis(router, expert_ids, axis=1) * valid_float[:, None]
    flat_ids = expert_ids.reshape(-1)
    flat_live = jnp.repeat(my_valid, chosen_count)
    named = (expert_ids[:, :, None] == jnp.arange(experts_all)[None, None, :]).astype(jnp.float32)
    chosen = (jnp.sum(named, axis=1) * valid_float[:, None]).astype(jnp.bfloat16)
    before = (jnp.arange(quarter)[None, :] < jnp.arange(quarter)[:, None]).astype(jnp.bfloat16)
    earlier = jnp.dot(before, chosen, preferred_element_type=jnp.float32)
    slot_of = jnp.sum(named * earlier[:, None, :], axis=2).astype(jnp.int32).reshape(-1)
    target = jnp.where(flat_live > 0, flat_ids, experts_all)
    safe_target = jnp.minimum(target, experts_all - 1)

    def pack(row_block):
        boxes = jnp.zeros((experts_all, slots, width), jnp.bfloat16)
        boxes = boxes.at[target, slot_of].set(row_block, mode="drop")
        return boxes.reshape(1, owners, local_experts * slots, width)

    def unpack(boxes):
        flat_boxes = boxes.reshape(experts_all, slots, width)
        taken = flat_boxes[safe_target, slot_of]
        taken = jnp.where(flat_live[:, None] > 0, taken, jnp.zeros_like(taken))
        return taken.reshape(quarter, chosen_count, width)

    sent = pack(jnp.repeat(moe_in, chosen_count, axis=0))
    full_gate, full_up, full_down = (gate_weight, up_weight, down_weight)
    arrived = group_rows(dispatch_rows(sent))
    expert_rows = arrived.reshape(groups, owners, local_experts, slots, width)
    gate_val = jnp.einsum(
        "tsecd,edf->tsecf", expert_rows, gate_weight, preferred_element_type=jnp.float32
    )
    up_val = jnp.einsum(
        "tsecd,edf->tsecf", expert_rows, up_weight, preferred_element_type=jnp.float32
    )
    hidden = swiglu(gate_val, up_val).astype(jnp.bfloat16)
    result = jnp.einsum("tsecf,efd->tsecd", hidden, down_weight, preferred_element_type=jnp.float32)
    finished = lax.psum_scatter(
        result.reshape(1 * lax.axis_size("tp"), owners, local_experts * slots, width).astype(
            jnp.bfloat16
        ),
        "tp",
        scatter_dimension=0,
        tiled=True,
    )
    returned = return_rows(finished)
    result_rows = unpack(returned).astype(jnp.float32)
    output = (middle + jnp.sum(picked[:, :, None] * result_rows, axis=1)).astype(jnp.bfloat16)
    grad_out = cotangent.astype(jnp.float32)
    grad_picked = jnp.einsum("tkd,td->tk", result_rows, grad_out, precision=HIGH_PRECISION)
    onehot_float = (expert_ids[:, :, None] == jnp.arange(experts_all)[None, None, :]).astype(
        jnp.float32
    )
    grad_router = jnp.sum(onehot_float * (grad_picked * valid_float[:, None])[:, :, None], axis=1)
    _, soft_back = jax.vjp(softmax_rows, logits)
    grad_logits = soft_back(grad_router)[0]
    grad_result = (
        (picked[:, :, None] * grad_out[:, None, :])
        .astype(jnp.bfloat16)
        .reshape(quarter * chosen_count, width)
    )
    grad_sent = pack(grad_result)
    grad_arrived = group_rows(dispatch_rows(grad_sent))
    grad_rows = grad_arrived.reshape(groups, owners, local_experts, slots, width)
    gate_all = jnp.einsum(
        "tsecd,edf->tsecf", expert_rows, full_gate, preferred_element_type=jnp.float32
    )
    up_all = jnp.einsum(
        "tsecd,edf->tsecf", expert_rows, full_up, preferred_element_type=jnp.float32
    )
    hidden_all, swiglu_back = jax.vjp(swiglu, gate_all, up_all)
    hidden_low = hidden_all.astype(jnp.bfloat16)
    grad_hidden = jnp.einsum(
        "tsecd,efd->tsecf", grad_rows, full_down, preferred_element_type=jnp.float32
    )
    grad_gate_f, grad_up_f = swiglu_back(grad_hidden)
    grad_gate_rows = grad_gate_f.astype(jnp.bfloat16)
    grad_up_rows = grad_up_f.astype(jnp.bfloat16)
    down_grad = jnp.einsum(
        "tsecf,tsecd->efd", hidden_low, grad_rows, preferred_element_type=jnp.float32
    )
    gate_grad = jnp.einsum(
        "tsecd,tsecf->edf", expert_rows, grad_gate_rows, preferred_element_type=jnp.float32
    )
    up_grad = jnp.einsum(
        "tsecd,tsecf->edf", expert_rows, grad_up_rows, preferred_element_type=jnp.float32
    )
    summed = jnp.einsum(
        "tsecf,edf->tsecd", grad_gate_rows, gate_weight, preferred_element_type=jnp.float32
    )
    summed = summed + jnp.einsum(
        "tsecf,edf->tsecd", grad_up_rows, up_weight, preferred_element_type=jnp.float32
    )
    grad_finished = lax.psum_scatter(
        summed.reshape(1 * lax.axis_size("tp"), owners, local_experts * slots, width).astype(
            jnp.bfloat16
        ),
        "tp",
        scatter_dimension=0,
        tiled=True,
    )
    grad_returned = return_rows(grad_finished)
    grad_copies = unpack(grad_returned).astype(jnp.float32)
    router_float = router_weight.astype(jnp.float32)
    grad_moe_in = jnp.sum(grad_copies, axis=1) + jnp.dot(
        grad_logits, router_float.T, precision=HIGH_PRECISION
    )
    router_grad = jnp.dot(moe_in.astype(jnp.float32).T, grad_logits, precision=HIGH_PRECISION)
    _, norm_two_back = jax.vjp(rms_norm, middle, moe_gain)
    grad_mid_norm, moe_gain_grad = norm_two_back(grad_moe_in)
    grad_middle = grad_out + grad_mid_norm
    grad_branch = lax.all_gather(grad_middle.astype(jnp.bfloat16), "tp", axis=0, tiled=True)
    out_grad = jnp.einsum("sh,sd->hd", attended, grad_branch, preferred_element_type=jnp.float32)
    grad_attended = jnp.einsum(
        "sd,hd->sh", grad_branch, out_weight, preferred_element_type=jnp.float32
    ).astype(jnp.bfloat16)
    grad_attended = grad_attended.reshape(seq_len, kv_heads, group_factor, head_size)
    query_parts = []
    key_total = jnp.zeros((seq_len, kv_heads, head_size), jnp.float32)
    value_total = jnp.zeros((seq_len, kv_heads, head_size), jnp.float32)
    for block_no, offset in enumerate(range(0, seq_len, height)):
        allowed = block_mask(segment_row, live_row, offset, height)
        scores = block_scores(query_val, key_val, allowed, factor)
        probs = jnp.where(allowed[None, None], jnp.exp(scores - log_sums[block_no]), 0.0)
        grad_probs = jnp.einsum(
            "qgrd,kgd->grqk", grad_attended, value_vectors, preferred_element_type=jnp.float32
        )
        centre = jnp.sum(probs * grad_probs, axis=-1, keepdims=True)
        grad_scores = (probs * (grad_probs - centre)).astype(jnp.bfloat16)
        query_parts.append(
            jnp.einsum("grqk,kgd->qgrd", grad_scores, key_val, preferred_element_type=jnp.float32)
            * factor
        )
        key_total = (
            jnp.einsum("grqk,qgrd->kgd", grad_scores, query_val, preferred_element_type=jnp.float32)
            * factor
        )
        value_total = jnp.einsum(
            "grqk,qgrd->kgd",
            probs.astype(jnp.bfloat16),
            grad_attended,
            preferred_element_type=jnp.float32,
        )
    grad_query_rot = query_parts[0]
    _, query_back = jax.vjp(lambda vectors: rotate(vectors, cos_query, sin_query), query_unrotated)
    _, key_back = jax.vjp(lambda vectors: rotate(vectors, cos_key, sin_key), key_unrotated)
    grad_q_pre = (
        query_back(grad_query_rot)[0].astype(jnp.bfloat16).reshape(seq_len, q_heads * head_size)
    )
    grad_k_pre = key_back(key_total)[0].astype(jnp.bfloat16).reshape(seq_len, kv_heads * head_size)
    grad_value = value_total.astype(jnp.bfloat16).reshape(seq_len, kv_heads * head_size)
    query_grad = jnp.einsum("sd,sh->dh", normed_all, grad_q_pre, preferred_element_type=jnp.float32)
    key_grad = jnp.einsum("sd,sh->dh", normed_all, grad_k_pre, preferred_element_type=jnp.float32)
    value_grad = jnp.einsum("sd,sh->dh", normed_all, grad_value, preferred_element_type=jnp.float32)
    summed = jnp.einsum("sh,dh->sd", grad_q_pre, query_matrix, preferred_element_type=jnp.float32)
    summed = summed + jnp.einsum(
        "sh,dh->sd", grad_k_pre, key_matrix, preferred_element_type=jnp.float32
    )
    summed = summed + jnp.einsum(
        "sh,dh->sd", grad_value, value_matrix, preferred_element_type=jnp.float32
    )
    grad_normed = lax.psum_scatter(
        summed.astype(jnp.bfloat16), "tp", scatter_dimension=0, tiled=True
    ).astype(jnp.float32)
    _, norm_one_back = jax.vjp(rms_norm, x_float, norm_gain)
    grad_x_norm, norm_gain_grad = norm_one_back(grad_normed)
    input_grad = grad_middle + grad_x_norm
    query_grad, key_grad, value_grad, out_grad = lax.psum(
        (query_grad, key_grad, value_grad, out_grad), "ep"
    )
    norm_gain_grad, moe_gain_grad, router_grad = lax.psum(
        (norm_gain_grad, moe_gain_grad, router_grad), ("ep", "tp")
    )
    return (
        output,
        input_grad,
        norm_gain_grad,
        query_grad,
        key_grad,
        value_grad,
        out_grad,
        moe_gain_grad,
        router_grad,
        gate_grad,
        up_grad,
        down_grad,
    )


def solution(mesh):
    in_specs = (
        P(("ep", "tp"), None),
        P(),
        P(None, "tp"),
        P(None, "tp"),
        P(None, "tp"),
        P("tp", None),
        P(),
        P(),
        P("ep", None, "tp"),
        P("ep", None, "tp"),
        P("ep", "tp", None),
        P(("ep", "tp"), None),
        P(("ep", "tp"), None),
        P("ep", None),
        P("ep", None),
    )
    out_specs = (
        P(("ep", "tp"), None),
        P(("ep", "tp"), None),
        P(),
        P(None, "tp"),
        P(None, "tp"),
        P(None, "tp"),
        P("tp", None),
        P(),
        P(),
        P("ep", None, "tp"),
        P("ep", None, "tp"),
        P("ep", "tp", None),
    )
    return jax.shard_map(local, mesh=mesh, in_specs=in_specs, out_specs=out_specs, check_vma=False)
```

```python
import math

import jax
import jax.numpy as jnp
from jax import lax
from jax.experimental import pallas as pl
from jax.experimental.pallas import tpu as pltpu
from jax.sharding import PartitionSpec as P

HEAD_SIZE_DIM = 64


EPS = 1e-06
HIGH_PRECISION = lax.Precision.HIGHEST


def rms_norm(activation, gain_vec):
    factor = lax.rsqrt(jnp.mean(activation * activation, axis=-1, keepdims=True) + EPS)
    return activation * factor * gain_vec


def rotate(vectors, cos_table, sin_table):
    half_size = vectors.shape[-1] // 2
    first_half = vectors[..., :half_size]
    second_half = vectors[..., half_size:]
    return jnp.concatenate(
        [
            first_half * cos_table - second_half * sin_table,
            second_half * cos_table + first_half * sin_table,
        ],
        axis=-1,
    )


def angle_tables(span_length, head_size):
    half_size = head_size // 2
    inverse = jnp.exp(
        -math.log(10000.0) * jnp.arange(half_size, dtype=jnp.float32) * 2.0 / head_size
    )
    angles = jnp.arange(span_length, dtype=jnp.float32)[:, None] * inverse[None, :]
    return (jnp.cos(angles), jnp.sin(angles))


def swiglu(gate_val, up_val):
    return jax.nn.silu(gate_val) * up_val


def softmax_rows(logits):
    return jax.nn.softmax(logits, axis=-1)


def block_mask(segment_row, live_row, offset, height):
    span_length = segment_row.shape[0]
    key_places = jnp.arange(span_length)
    query_places = offset + jnp.arange(height)
    same_doc = segment_row[:, None] == segment_row[None, :]
    causal = key_places[None, :] <= query_places[:, None]
    usable = (live_row[None, :] > 0) | (key_places[None, :] == query_places[:, None])
    return same_doc & causal & usable


def block_scores(query_block, key_val, allowed, factor):
    scores = (
        jnp.einsum("qgrd,kgd->grqk", query_block, key_val, preferred_element_type=jnp.float32)
        * factor
    )
    return jnp.where(allowed[None, None], scores, -1e30)


def group_rows(boxes):
    return lax.all_gather(boxes, "tp", axis=0, tiled=True)


def dispatch_rows(boxes):
    return lax.all_to_all(boxes, "ep", split_axis=1, concat_axis=1, tiled=True)


def return_rows(boxes):
    return lax.all_to_all(boxes, "ep", split_axis=1, concat_axis=1, tiled=True)


def swap_core(value):
    return lax.ppermute(value, "tp", [(i, i ^ 1) for i in range(4)])


def swap_x(value):
    return lax.ppermute(value, "tp", [(i, i ^ 2) for i in range(4)])


def swap_y(value):
    owners = lax.axis_size("ep")
    return lax.ppermute(value, "ep", [(i, i ^ 1) for i in range(owners)])


def shift_z(value, step):
    owners = lax.axis_size("ep")
    return lax.ppermute(value, "ep", [(i, (i + 2 * step) % owners) for i in range(owners)])


def gather_tp(value):
    if lax.axis_size("tp") != 4:
        return lax.all_gather(value, "tp", axis=0, tiled=True)
    me = lax.axis_index("tp")
    other = swap_core(value)
    across = swap_x(value)
    across_other = swap_core(across)
    rows = value.shape[0]
    full = jnp.zeros((4 * rows,) + value.shape[1:], value.dtype)
    for part, flip in ((value, 0), (other, 1), (across, 2), (across_other, 3)):
        full = lax.dynamic_update_slice_in_dim(full, part, (me ^ flip) * rows, 0)
    return full


def scatter_tp(value, core_dtype):
    if lax.axis_size("tp") != 4:
        return lax.psum_scatter(value, "tp", scatter_dimension=0, tiled=True).astype(jnp.float32)
    me = lax.axis_index("tp")
    core, across = me % 2, me // 2
    boxes = value.reshape((2, 2, value.shape[0] // 4) + value.shape[1:])
    leave = lax.dynamic_index_in_dim(boxes, 1 - core, 1, keepdims=False).astype(core_dtype)
    stay = lax.dynamic_index_in_dim(boxes, core, 1, keepdims=False)
    both = stay.astype(jnp.float32) + swap_core(leave).astype(jnp.float32)
    mine = lax.dynamic_index_in_dim(both, across, 0, keepdims=False)
    theirs = lax.dynamic_index_in_dim(both, 1 - across, 0, keepdims=False)
    return mine + swap_x(theirs.astype(jnp.bfloat16)).astype(jnp.float32)


def gather_column(value):
    half = value.shape[0] // 2
    across = swap_x(value)
    along = swap_y(value)
    first = swap_y(across[:half])
    last = swap_x(along[half:])
    pieces = (value, across, along, first, last)
    return pieces + tuple(swap_core(piece) for piece in pieces)


def gather_planes(value):
    planes = lax.axis_size("ep") // 2
    chunks = [gather_column(value)]
    for _ in range(1, planes):
        value = shift_z(value, 1)
        chunks.append(gather_column(value))
    return chunks


def add_low(left, right):
    return (left.astype(jnp.float32) + right.astype(jnp.float32)).astype(jnp.bfloat16)


def reduce_plane(own_core, other_core, step):
    size = own_core.shape[0] // 4
    arrived = swap_core(other_core)
    part = lambda i: add_low(own_core[i * size : (i + 1) * size], arrived[i * size : (i + 1) * size])
    from_x = swap_x(part(2))
    from_y = swap_y(part(3))
    first = add_low(part(0), from_x)
    last = add_low(part(1), from_y)
    half = size // 2
    first_sum = add_low(first[:half], swap_y(first[half:]))
    last_sum = add_low(last[:half], swap_x(last[half:]))
    total = jnp.concatenate([first_sum, last_sum], axis=0)
    return shift_z(total, -step) if step else total


def butterfly_sum(value):
    value = value + swap_core(value)
    value = value + swap_x(value)
    value = value + swap_y(value)
    total = value
    for step in range(1, lax.axis_size("ep") // 2):
        total = total + shift_z(value, step)
    return total


FIRST_HALF = (0, 4, 1, 5)
LAST_HALF = (2, 3, 6, 7)
NT = (((1,), (1,)), ((), ()))
TN = (((0,), (0,)), ((), ()))


def dot_f32(left, right, dims=None):
    if dims is None:
        return jnp.dot(left, right, preferred_element_type=jnp.float32)
    return lax.dot_general(left, right, dims, preferred_element_type=jnp.float32)


def pick(index, table):
    out = table[0]
    for i in range(1, len(table)):
        out = jnp.where(index == i, table[i], out)
    return out


def expert_kernel(sizes, *refs):
    experts, slots, blocks, rows, routed = sizes
    x_parts, g_parts = refs[:10], refs[10:20]
    slot_ref, router_ref, gate_ref, up_ref, down_ref = refs[20:25]
    own_ref, other_ref, xr_out, gr_out, dgu_ref, wh_ref, rg_ref = refs[25:32]
    xs, gs, xr, gr, wgu, wd, back, picks, probs, weight, d_weight = refs[32:43]
    x_sem, g_sem, w_sem, out_sem = refs[43:47]
    units = wd.shape[1]
    half = rows // 2
    total = experts * slots
    depth = blocks * slots
    starts = []
    for parts, scratch, sem in ((x_parts, xs, x_sem), (g_parts, gs, g_sem)):
        for i, part in enumerate(parts):
            side, place = i // 5, i % 5
            block = side * 4 + min(place, 3)
            offset = block * rows + (half if place == 4 else 0)
            starts.append((part, scratch.at[pl.ds(offset, part.shape[0])], sem.at[block]))
    for source, target, sem in starts[:10]:
        pltpu.make_async_copy(source, target, sem).start()
    for source, target, sem in starts[10:]:
        pltpu.make_async_copy(source, target, sem).start()
    for e in range(experts):
        pltpu.make_async_copy(gate_ref.at[e], wgu.at[e, :, pl.ds(0, units)], w_sem.at[0, e]).start()
        pltpu.make_async_copy(up_ref.at[e], wgu.at[e, :, pl.ds(units, units)], w_sem.at[1, e]).start()
        pltpu.make_async_copy(down_ref.at[e], wd.at[e], w_sem.at[2, e]).start()
    rg_ref[...] = jnp.zeros_like(rg_ref)

    def block_rows(b):
        return pl.ds(pl.multiple_of(b * rows, rows), rows)

    def slot_rows(b):
        return pl.ds(pl.multiple_of(b * slots, slots), slots)

    def expand(table):
        return jnp.concatenate(
            [jnp.broadcast_to(table[e : e + 1, :], (slots, rows)) for e in range(experts)], axis=0
        )

    place = jnp.concatenate(
        [lax.broadcasted_iota(jnp.int32, (slots, rows), 0)] * experts, axis=0
    ).astype(jnp.float32)

    def gather_x(b, carry):
        pltpu.make_async_copy(xs.at[block_rows(b)], xs.at[block_rows(b)], x_sem.at[b]).wait()
        x_block = xs[block_rows(b), :]
        logits = dot_f32(router_ref[...], x_block, NT)
        lane = lax.broadcasted_iota(jnp.int32, logits.shape, 0)
        logits = jnp.where(lane < routed, logits, -1e30)
        expo = jnp.exp(logits - jnp.max(logits, axis=0, keepdims=True))
        prob = expo / jnp.sum(expo, axis=0, keepdims=True)
        probs[b] = prob
        hit = expand(slot_ref[b]) == place
        chosen = jnp.sum(jnp.where(hit, expand(prob), 0.0), axis=1, keepdims=True)
        chosen = jnp.broadcast_to(chosen, (total, rows))
        one = hit.astype(jnp.float32).astype(jnp.bfloat16)
        picks[b] = one
        taken = dot_f32(one, x_block).astype(jnp.bfloat16)
        for e in range(experts):
            xr[e, slot_rows(b), :] = taken[e * slots : (e + 1) * slots]
            weight[e, slot_rows(b), :] = chosen[e * slots : (e + 1) * slots]
        back[b, pl.ds(total, router_ref.shape[0]), :] = router_ref[...]
        return carry

    def gather_g(b, carry):
        pltpu.make_async_copy(gs.at[block_rows(b)], gs.at[block_rows(b)], g_sem.at[b]).wait()
        taken = dot_f32(picks[b], gs[block_rows(b), :]).astype(jnp.bfloat16)
        for e in range(experts):
            gr[e, slot_rows(b), :] = taken[e * slots : (e + 1) * slots]
        return carry

    lax.fori_loop(0, blocks, gather_x, 0)
    pltpu.make_async_copy(xr, xr_out, out_sem.at[0]).start()
    lax.fori_loop(0, blocks, gather_g, 0)
    pltpu.make_async_copy(gr, gr_out, out_sem.at[1]).start()

    def one_expert(e, carry):
        pltpu.make_async_copy(wgu.at[e, :, pl.ds(0, units)], wgu.at[e, :, pl.ds(0, units)], w_sem.at[0, e]).wait()
        pltpu.make_async_copy(wgu.at[e, :, pl.ds(units, units)], wgu.at[e, :, pl.ds(units, units)], w_sem.at[1, e]).wait()
        pltpu.make_async_copy(wd.at[e], wd.at[e], w_sem.at[2, e]).wait()
        both = dot_f32(xr[e], wgu[e])
        gate, up = both[:, :units], both[:, units:]
        back_hidden = dot_f32(gr[e], wd[e], NT)
        sig = 1.0 / (1.0 + jnp.exp(-gate))
        silu = gate * sig
        hidden = silu * up
        d_weight[e] = jnp.broadcast_to(
            jnp.sum(hidden.astype(jnp.bfloat16).astype(jnp.float32) * back_hidden, axis=1, keepdims=True),
            (depth, rows),
        )
        share = weight[e]
        d_hidden = share * back_hidden
        d_gate = d_hidden * up * (sig * (1.0 + gate * (1.0 - sig)))
        d_up = d_hidden * silu
        d_both = jnp.concatenate([d_gate, d_up], axis=1).astype(jnp.bfloat16)
        dgu_ref[e] = d_both
        wh_ref[e] = (share * hidden).astype(jnp.bfloat16)
        d_rows = dot_f32(d_both, wgu[e], NT).astype(jnp.bfloat16)
        for b in range(blocks):
            back[b, pl.ds(pl.multiple_of(e * slots, slots), slots), :] = d_rows[b * slots : (b + 1) * slots]
        return carry

    lax.fori_loop(0, experts, one_expert, 0)

    def scatter(b, carry):
        one = picks[b]
        d_slot = jnp.concatenate([d_weight[e, slot_rows(b), :] for e in range(experts)], axis=0)
        spread = one.astype(jnp.float32) * d_slot
        d_prob = jnp.concatenate(
            [jnp.sum(spread[e * slots : (e + 1) * slots], axis=0, keepdims=True) for e in range(experts)]
            + [jnp.zeros((router_ref.shape[0] - experts, rows), jnp.float32)],
            axis=0,
        )
        prob = probs[b]
        centre = jnp.sum(prob * d_prob, axis=0, keepdims=True)
        d_logits = (prob * (d_prob - centre)).astype(jnp.bfloat16)
        rg_ref[...] += dot_f32(d_logits, xs[block_rows(b), :])
        result = dot_f32(jnp.concatenate([one, d_logits], axis=0), back[b], TN).astype(jnp.bfloat16)
        kind = b % 4
        first = pl.ds(pl.multiple_of(pick(kind, FIRST_HALF) * half, half), half)
        last = pl.ds(pl.multiple_of(pick(kind, LAST_HALF) * half, half), half)

        @pl.when(b < 4)
        def _():
            own_ref[first, :] = result[:half]
            own_ref[last, :] = result[half:]

        @pl.when(b >= 4)
        def _():
            other_ref[first, :] = result[:half]
            other_ref[last, :] = result[half:]

        return carry

    lax.fori_loop(0, blocks, scatter, 0)
    pltpu.make_async_copy(xr, xr_out, out_sem.at[0]).wait()
    pltpu.make_async_copy(gr, gr_out, out_sem.at[1]).wait()


def expert_call(x_parts, g_parts, slot, router_rows, gate_weight, up_weight, down_weight, routed, slots):
    blocks = 8
    rows, width = x_parts[0].shape
    experts, _, units = gate_weight.shape
    depth = blocks * slots
    padded = router_rows.shape[0]
    low, full = jnp.bfloat16, jnp.float32
    any_spec = pl.BlockSpec(memory_space=pl.ANY)
    vmem_spec = pl.BlockSpec(memory_space=pltpu.VMEM)
    return pl.pallas_call(
        lambda *refs: expert_kernel((experts, slots, blocks, rows, routed), *refs),
        out_shape=(
            jax.ShapeDtypeStruct((4 * rows, width), low),
            jax.ShapeDtypeStruct((4 * rows, width), low),
            jax.ShapeDtypeStruct((experts, depth, width), low),
            jax.ShapeDtypeStruct((experts, depth, width), low),
            jax.ShapeDtypeStruct((experts, depth, 2 * units), low),
            jax.ShapeDtypeStruct((experts, depth, units), low),
            jax.ShapeDtypeStruct((padded, width), full),
        ),
        in_specs=[any_spec] * 20 + [vmem_spec] * 2 + [any_spec] * 3,
        out_specs=(vmem_spec, vmem_spec, any_spec, any_spec, vmem_spec, vmem_spec, vmem_spec),
        scratch_shapes=[
            pltpu.VMEM((blocks * rows, width), low),
            pltpu.VMEM((blocks * rows, width), low),
            pltpu.VMEM((experts, depth, width), low),
            pltpu.VMEM((experts, depth, width), low),
            pltpu.VMEM((experts, width, 2 * units), low),
            pltpu.VMEM((experts, units, width), low),
            pltpu.VMEM((blocks, experts * slots + padded, width), low),
            pltpu.VMEM((blocks, experts * slots, rows), low),
            pltpu.VMEM((blocks, padded, rows), full),
            pltpu.VMEM((experts, depth, rows), full),
            pltpu.VMEM((experts, depth, rows), full),
            pltpu.SemaphoreType.DMA((blocks,)),
            pltpu.SemaphoreType.DMA((blocks,)),
            pltpu.SemaphoreType.DMA((3, experts)),
            pltpu.SemaphoreType.DMA((2,)),
        ],
        compiler_params=pltpu.CompilerParams(vmem_limit_bytes=50 * 2**20),
        cost_estimate=pl.CostEstimate(
            flops=2 * experts * depth * width * units * 5, bytes_accessed=24 * 2**20, transcendentals=0
        ),
        name="expert_chunk",
    )(*x_parts, *g_parts, slot, router_rows, gate_weight, up_weight, down_weight)


def output_kernel(sizes, wh_ref, slot_ref, down_ref, own_ref, other_ref, rows_ref):
    experts, slots, blocks, rows = sizes
    half = rows // 2

    def one_expert(e, carry):
        result = dot_f32(wh_ref[e], down_ref[e]).astype(jnp.bfloat16)
        for b in range(blocks):
            rows_ref[b, pl.ds(pl.multiple_of(e * slots, slots), slots), :] = result[b * slots : (b + 1) * slots]
        return carry

    lax.fori_loop(0, experts, one_expert, 0)
    place = lax.broadcasted_iota(jnp.int32, (slots, rows), 0).astype(jnp.float32)

    def scatter(b, carry):
        table = slot_ref[b]
        one = jnp.concatenate(
            [(table[e : e + 1, :] == place).astype(jnp.float32) for e in range(experts)], axis=0
        ).astype(jnp.bfloat16)
        result = dot_f32(one, rows_ref[b], TN).astype(jnp.bfloat16)
        kind = b % 4
        first = pl.ds(pl.multiple_of(pick(kind, FIRST_HALF) * half, half), half)
        last = pl.ds(pl.multiple_of(pick(kind, LAST_HALF) * half, half), half)

        @pl.when(b < 4)
        def _():
            own_ref[first, :] = result[:half]
            own_ref[last, :] = result[half:]

        @pl.when(b >= 4)
        def _():
            other_ref[first, :] = result[:half]
            other_ref[last, :] = result[half:]

        return carry

    lax.fori_loop(0, blocks, scatter, 0)


def output_call(weighted, slot, down_weight, slots):
    experts, depth, units = weighted.shape
    width = down_weight.shape[2]
    blocks, _, rows = slot.shape
    vmem_spec = pl.BlockSpec(memory_space=pltpu.VMEM)
    return pl.pallas_call(
        lambda *refs: output_kernel((experts, slots, blocks, rows), *refs),
        out_shape=(jax.ShapeDtypeStruct((4 * rows, width), jnp.bfloat16),) * 2,
        in_specs=[vmem_spec] * 3,
        out_specs=(vmem_spec,) * 2,
        scratch_shapes=[pltpu.VMEM((blocks, experts * slots, width), jnp.bfloat16)],
        compiler_params=pltpu.CompilerParams(vmem_limit_bytes=40 * 2**20),
        cost_estimate=pl.CostEstimate(
            flops=2 * experts * depth * width * units * 3, bytes_accessed=6 * 2**20, transcendentals=0
        ),
        name="output_chunk",
    )(weighted, slot, down_weight)


def weight_kernel(count, *refs):
    xr, gr, dgu, wh = (refs[i * count : (i + 1) * count] for i in range(4))
    gate_ref, up_ref, down_ref = refs[4 * count :]
    units = gate_ref.shape[2]
    both = sum(dot_f32(x[0], d[0], TN) for x, d in zip(xr, dgu))
    gate_ref[0] = both[:, :units]
    up_ref[0] = both[:, units:]
    down_ref[0] = sum(dot_f32(h[0], g[0], TN) for h, g in zip(wh, gr))


def weight_call(xr, gr, dgu, wh):
    count = len(xr)
    experts, depth, width = xr[0].shape
    units = wh[0].shape[2]
    spec = lambda array: pl.BlockSpec((1,) + array.shape[1:], lambda e: (e, 0, 0))
    operands = [*xr, *gr, *dgu, *wh]
    up_like = jax.ShapeDtypeStruct((experts, width, units), jnp.float32)
    down_like = jax.ShapeDtypeStruct((experts, units, width), jnp.float32)
    return pl.pallas_call(
        lambda *refs: weight_kernel(count, *refs),
        grid=(experts,),
        out_shape=(up_like, up_like, down_like),
        in_specs=[spec(a) for a in operands],
        out_specs=(spec(up_like), spec(up_like), spec(down_like)),
        compiler_params=pltpu.CompilerParams(vmem_limit_bytes=50 * 2**20),
        cost_estimate=pl.CostEstimate(
            flops=2 * experts * depth * count * width * units * 3,
            bytes_accessed=45 * 2**20,
            transcendentals=0,
        ),
        name="expert_weights",
    )(*operands)


def gathered_experts(
    moe_in, router_weight, gate_weight, up_weight, down_weight, cotangent, expert_ids, my_valid, slots
):
    rows = moe_in.shape[0]
    local_experts = gate_weight.shape[0]
    experts_all = router_weight.shape[1]
    owner = lax.axis_index("ep")
    planes = lax.axis_size("ep") // 2
    ids = jnp.where(my_valid[:, None] > 0, expert_ids, -1).T[None]
    for swap in (swap_x, swap_y, swap_core):
        ids = jnp.concatenate([ids, swap(ids)], axis=0)
    ids = jnp.stack([ids] + [shift_z(ids, step) for step in range(1, planes)])
    mine = owner * local_experts + jnp.arange(local_experts)
    named = jnp.any(ids[:, :, None] == mine[None, None, :, None, None], axis=-2)
    before = (jnp.arange(rows)[:, None] < jnp.arange(rows)[None, :]).astype(jnp.bfloat16)
    earlier = jnp.dot(named.astype(jnp.bfloat16), before, preferred_element_type=jnp.float32)
    slot = jnp.where(named, earlier, -1.0)
    slot = jnp.pad(slot, ((0, 0), (0, 0), (0, -local_experts % 8), (0, 0)), constant_values=-1.0)
    padded = -(-experts_all // 16) * 16
    router_rows = jnp.roll(router_weight.T, -owner * local_experts, axis=0)
    router_rows = jnp.pad(router_rows, ((0, padded - experts_all), (0, 0)))
    g_chunks = gather_planes(cotangent)
    x_chunks = gather_planes(moe_in)
    kept, d_input = [], 0.0
    for i in range(planes):
        own, other, *rest = expert_call(
            x_chunks[i], g_chunks[i], slot[i], router_rows, gate_weight, up_weight, down_weight, experts_all, slots
        )
        kept.append(rest)
        d_input = d_input + reduce_plane(own, other, i).astype(jnp.float32)
    xr, gr, dgu, wh, router_parts = zip(*kept)
    expert_sum = 0.0
    for i in range(planes):
        own, other = output_call(wh[i], slot[i], down_weight, slots)
        expert_sum = expert_sum + reduce_plane(own, other, i).astype(jnp.float32)
    gate_grad, up_grad, down_grad = weight_call(xr, gr, dgu, wh)
    router_part = jnp.roll(sum(router_parts)[:experts_all], owner * local_experts, axis=0)
    return expert_sum, d_input, router_part, gate_grad, up_grad, down_grad


def routed_experts(
    moe_in, router_weight, gate_weight, up_weight, down_weight, cotangent, expert_ids, my_valid, slots
):
    quarter, width = moe_in.shape
    owners, groups = lax.axis_size("ep"), lax.axis_size("tp")
    local_experts = gate_weight.shape[0]
    experts_all = router_weight.shape[1]
    chosen_count = expert_ids.shape[1]
    logits = jnp.dot(moe_in, router_weight, preferred_element_type=jnp.float32)
    router = softmax_rows(logits)
    valid_float = my_valid.astype(jnp.float32)
    picked = jnp.take_along_axis(router, expert_ids, axis=1) * valid_float[:, None]
    flat_ids = expert_ids.reshape(-1)
    flat_live = jnp.repeat(my_valid, chosen_count)
    named = (expert_ids[:, :, None] == jnp.arange(experts_all)[None, None, :]).astype(jnp.float32)
    chosen = (jnp.sum(named, axis=1) * valid_float[:, None]).astype(jnp.bfloat16)
    before = (jnp.arange(quarter)[None, :] < jnp.arange(quarter)[:, None]).astype(jnp.bfloat16)
    earlier = jnp.dot(before, chosen, preferred_element_type=jnp.float32)
    slot_of = jnp.sum(named * earlier[:, None, :], axis=2).astype(jnp.int32).reshape(-1)
    target = jnp.where(flat_live > 0, flat_ids, experts_all)
    safe_target = jnp.minimum(target, experts_all - 1)

    def pack(row_block):
        boxes = jnp.zeros((experts_all, slots, width), jnp.bfloat16)
        boxes = boxes.at[target, slot_of].set(row_block, mode="drop")
        return boxes.reshape(1, owners, local_experts * slots, width)

    def unpack(boxes):
        flat_boxes = boxes.reshape(experts_all, slots, width)
        taken = flat_boxes[safe_target, slot_of]
        taken = jnp.where(flat_live[:, None] > 0, taken, jnp.zeros_like(taken))
        return taken.reshape(quarter, chosen_count, width)

    sent = pack(jnp.repeat(moe_in, chosen_count, axis=0))
    arrived = group_rows(dispatch_rows(sent))
    expert_rows = arrived.reshape(groups, owners, local_experts, slots, width)
    gate_val = jnp.einsum(
        "tsecd,edf->tsecf", expert_rows, gate_weight, preferred_element_type=jnp.float32
    )
    up_val = jnp.einsum(
        "tsecd,edf->tsecf", expert_rows, up_weight, preferred_element_type=jnp.float32
    )
    hidden = swiglu(gate_val, up_val).astype(jnp.bfloat16)
    result = jnp.einsum("tsecf,efd->tsecd", hidden, down_weight, preferred_element_type=jnp.float32)
    finished = lax.psum_scatter(
        result.reshape(1 * lax.axis_size("tp"), owners, local_experts * slots, width).astype(
            jnp.bfloat16
        ),
        "tp",
        scatter_dimension=0,
        tiled=True,
    )
    returned = return_rows(finished)
    result_rows = unpack(returned).astype(jnp.float32)
    expert_sum = jnp.sum(picked[:, :, None] * result_rows, axis=1)
    grad_out = cotangent.astype(jnp.float32)
    grad_picked = jnp.einsum("tkd,td->tk", result_rows, grad_out, precision=HIGH_PRECISION)
    onehot_float = (expert_ids[:, :, None] == jnp.arange(experts_all)[None, None, :]).astype(
        jnp.float32
    )
    grad_router = jnp.sum(onehot_float * (grad_picked * valid_float[:, None])[:, :, None], axis=1)
    _, soft_back = jax.vjp(softmax_rows, logits)
    grad_logits = soft_back(grad_router)[0]
    grad_result = (
        (picked[:, :, None] * grad_out[:, None, :])
        .astype(jnp.bfloat16)
        .reshape(quarter * chosen_count, width)
    )
    grad_sent = pack(grad_result)
    grad_arrived = group_rows(dispatch_rows(grad_sent))
    grad_rows = grad_arrived.reshape(groups, owners, local_experts, slots, width)
    gate_all = jnp.einsum(
        "tsecd,edf->tsecf", expert_rows, gate_weight, preferred_element_type=jnp.float32
    )
    up_all = jnp.einsum(
        "tsecd,edf->tsecf", expert_rows, up_weight, preferred_element_type=jnp.float32
    )
    hidden_all, swiglu_back = jax.vjp(swiglu, gate_all, up_all)
    hidden_low = hidden_all.astype(jnp.bfloat16)
    grad_hidden = jnp.einsum(
        "tsecd,efd->tsecf", grad_rows, down_weight, preferred_element_type=jnp.float32
    )
    grad_gate_f, grad_up_f = swiglu_back(grad_hidden)
    grad_gate_rows = grad_gate_f.astype(jnp.bfloat16)
    grad_up_rows = grad_up_f.astype(jnp.bfloat16)
    down_grad = jnp.einsum(
        "tsecf,tsecd->efd", hidden_low, grad_rows, preferred_element_type=jnp.float32
    )
    gate_grad = jnp.einsum(
        "tsecd,tsecf->edf", expert_rows, grad_gate_rows, preferred_element_type=jnp.float32
    )
    up_grad = jnp.einsum(
        "tsecd,tsecf->edf", expert_rows, grad_up_rows, preferred_element_type=jnp.float32
    )
    summed = jnp.einsum(
        "tsecf,edf->tsecd", grad_gate_rows, gate_weight, preferred_element_type=jnp.float32
    )
    summed = summed + jnp.einsum(
        "tsecf,edf->tsecd", grad_up_rows, up_weight, preferred_element_type=jnp.float32
    )
    grad_finished = lax.psum_scatter(
        summed.reshape(1 * lax.axis_size("tp"), owners, local_experts * slots, width).astype(
            jnp.bfloat16
        ),
        "tp",
        scatter_dimension=0,
        tiled=True,
    )
    grad_returned = return_rows(grad_finished)
    grad_copies = unpack(grad_returned).astype(jnp.float32)
    router_float = router_weight.astype(jnp.float32)
    grad_moe_in = jnp.sum(grad_copies, axis=1) + jnp.dot(
        grad_logits, router_float.T, precision=HIGH_PRECISION
    )
    router_part = jnp.dot(
        grad_logits.T, moe_in.astype(jnp.float32), precision=HIGH_PRECISION
    )
    return expert_sum, grad_moe_in, router_part, gate_grad, up_grad, down_grad


def local(
    tokens,
    norm_gain,
    query_matrix,
    key_matrix,
    value_matrix,
    out_weight,
    moe_gain,
    router_weight,
    gate_weight,
    up_weight,
    down_weight,
    cotangent,
    expert_ids,
    segments,
    valid_mask,
):
    quarter = tokens.shape[0]
    width = tokens.shape[1]
    groups = lax.axis_size("tp")
    owners = lax.axis_size("ep")
    my_part = lax.axis_index("tp")
    seq_len = quarter * groups
    head_size = HEAD_SIZE_DIM
    kv_heads = key_matrix.shape[1] // head_size
    q_heads = query_matrix.shape[1] // head_size
    group_factor = q_heads // kv_heads
    local_experts = gate_weight.shape[0]
    experts_all = router_weight.shape[1]
    chosen_count = expert_ids.shape[1]
    slots = max(8, 3 * quarter * chosen_count // (2 * experts_all) // 8 * 8)
    factor = 1.0 / math.sqrt(head_size)
    segment_row = segments[0]
    live_row = valid_mask[0]
    x_float = tokens.astype(jnp.float32)
    normed = rms_norm(x_float, norm_gain).astype(jnp.bfloat16)
    normed_all = gather_tp(normed)
    query_unrotated = jnp.dot(normed_all, query_matrix, preferred_element_type=jnp.float32).reshape(
        seq_len, kv_heads, group_factor, head_size
    )
    key_unrotated = jnp.dot(normed_all, key_matrix, preferred_element_type=jnp.float32).reshape(
        seq_len, kv_heads, head_size
    )
    value_vectors = (
        jnp.dot(normed_all, value_matrix, preferred_element_type=jnp.float32)
        .astype(jnp.bfloat16)
        .reshape(seq_len, kv_heads, head_size)
    )
    cos_table, sin_table = angle_tables(seq_len, head_size)
    cos_query = cos_table[:, None, None, :]
    sin_query = sin_table[:, None, None, :]
    cos_key = cos_table[:, None, :]
    sin_key = sin_table[:, None, :]
    query_val = rotate(query_unrotated, cos_query, sin_query).astype(jnp.bfloat16)
    key_val = rotate(key_unrotated, cos_key, sin_key).astype(jnp.bfloat16)
    height = min(512, seq_len)
    offset = 0
    allowed = block_mask(segment_row, live_row, offset, height)
    scores = block_scores(query_val, key_val, allowed, factor)
    peak = jnp.max(scores, axis=-1, keepdims=True)
    expo = jnp.exp(scores - peak)
    denom = jnp.sum(expo, axis=-1, keepdims=True)
    weights = (expo / denom).astype(jnp.bfloat16)
    mixed = jnp.einsum("grqk,kgd->qgrd", weights, value_vectors, preferred_element_type=jnp.float32)
    outputs = mixed.reshape(height, q_heads * head_size)
    log_sums = [peak + jnp.log(denom)]
    attended = outputs.astype(jnp.bfloat16)
    branch = scatter_tp(
        jnp.dot(attended, out_weight, preferred_element_type=jnp.float32), jnp.float32
    )
    middle = x_float + branch
    moe_in = rms_norm(middle, moe_gain).astype(jnp.bfloat16)
    my_valid = lax.dynamic_slice_in_dim(live_row, my_part * quarter, quarter, 0)
    gathers = groups == 4 and owners % 2 == 0 and local_experts * slots >= quarter
    if gathers:
        expert_sum, grad_moe_in, router_part, gate_grad, up_grad, down_grad = gathered_experts(
            moe_in, router_weight, gate_weight, up_weight, down_weight, cotangent, expert_ids, my_valid, slots
        )
    else:
        expert_sum, grad_moe_in, router_part, gate_grad, up_grad, down_grad = routed_experts(
            moe_in, router_weight, gate_weight, up_weight, down_weight, cotangent, expert_ids, my_valid, slots
        )
    grad_out = cotangent.astype(jnp.float32)
    output = (middle + expert_sum).astype(jnp.bfloat16)
    _, norm_two_back = jax.vjp(rms_norm, middle, moe_gain)
    grad_mid_norm, moe_gain_grad = norm_two_back(grad_moe_in)
    grad_middle = grad_out + grad_mid_norm
    grad_branch = gather_tp(grad_middle.astype(jnp.bfloat16))
    out_grad = jnp.einsum("sh,sd->hd", attended, grad_branch, preferred_element_type=jnp.float32)
    grad_attended = jnp.einsum(
        "sd,hd->sh", grad_branch, out_weight, preferred_element_type=jnp.float32
    ).astype(jnp.bfloat16)
    grad_attended = grad_attended.reshape(seq_len, kv_heads, group_factor, head_size)
    query_parts = []
    key_total = jnp.zeros((seq_len, kv_heads, head_size), jnp.float32)
    value_total = jnp.zeros((seq_len, kv_heads, head_size), jnp.float32)
    for block_no, offset in enumerate(range(0, seq_len, height)):
        allowed = block_mask(segment_row, live_row, offset, height)
        scores = block_scores(query_val, key_val, allowed, factor)
        probs = jnp.where(allowed[None, None], jnp.exp(scores - log_sums[block_no]), 0.0)
        grad_probs = jnp.einsum(
            "qgrd,kgd->grqk", grad_attended, value_vectors, preferred_element_type=jnp.float32
        )
        centre = jnp.sum(probs * grad_probs, axis=-1, keepdims=True)
        grad_scores = (probs * (grad_probs - centre)).astype(jnp.bfloat16)
        query_parts.append(
            jnp.einsum("grqk,kgd->qgrd", grad_scores, key_val, preferred_element_type=jnp.float32)
            * factor
        )
        key_total = (
            jnp.einsum("grqk,qgrd->kgd", grad_scores, query_val, preferred_element_type=jnp.float32)
            * factor
        )
        value_total = jnp.einsum(
            "grqk,qgrd->kgd",
            probs.astype(jnp.bfloat16),
            grad_attended,
            preferred_element_type=jnp.float32,
        )
    grad_query_rot = query_parts[0]
    _, query_back = jax.vjp(lambda vectors: rotate(vectors, cos_query, sin_query), query_unrotated)
    _, key_back = jax.vjp(lambda vectors: rotate(vectors, cos_key, sin_key), key_unrotated)
    grad_q_pre = (
        query_back(grad_query_rot)[0].astype(jnp.bfloat16).reshape(seq_len, q_heads * head_size)
    )
    grad_k_pre = key_back(key_total)[0].astype(jnp.bfloat16).reshape(seq_len, kv_heads * head_size)
    grad_value = value_total.astype(jnp.bfloat16).reshape(seq_len, kv_heads * head_size)
    query_grad = jnp.einsum("sd,sh->dh", normed_all, grad_q_pre, preferred_element_type=jnp.float32)
    key_grad = jnp.einsum("sd,sh->dh", normed_all, grad_k_pre, preferred_element_type=jnp.float32)
    value_grad = jnp.einsum("sd,sh->dh", normed_all, grad_value, preferred_element_type=jnp.float32)
    summed = jnp.einsum("sh,dh->sd", grad_q_pre, query_matrix, preferred_element_type=jnp.float32)
    summed = summed + jnp.einsum(
        "sh,dh->sd", grad_k_pre, key_matrix, preferred_element_type=jnp.float32
    )
    summed = summed + jnp.einsum(
        "sh,dh->sd", grad_value, value_matrix, preferred_element_type=jnp.float32
    )
    grad_normed = scatter_tp(summed, jnp.bfloat16)
    _, norm_one_back = jax.vjp(rms_norm, x_float, norm_gain)
    grad_x_norm, norm_gain_grad = norm_one_back(grad_normed)
    input_grad = grad_middle + grad_x_norm
    weights = jnp.concatenate(
        [part.astype(jnp.bfloat16) for part in (query_grad, key_grad, value_grad)], axis=1
    )
    weights = lax.psum(weights, "ep").astype(jnp.float32)
    query_grad, key_grad, value_grad = jnp.split(
        weights, (query_grad.shape[1], query_grad.shape[1] + key_grad.shape[1]), axis=1
    )
    out_grad = lax.psum(out_grad.astype(jnp.bfloat16), "ep").astype(jnp.float32)
    small = jnp.concatenate([router_part, moe_gain_grad[None]], axis=0)
    if gathers:
        small, norm_gain_grad = butterfly_sum(small), butterfly_sum(norm_gain_grad[None])[0]
    else:
        small, norm_gain_grad = lax.psum((small, norm_gain_grad), ("ep", "tp"))
    router_grad, moe_gain_grad = small[:experts_all].T, small[experts_all]
    return (
        output,
        input_grad,
        norm_gain_grad,
        query_grad,
        key_grad,
        value_grad,
        out_grad,
        moe_gain_grad,
        router_grad,
        gate_grad,
        up_grad,
        down_grad,
    )


def solution(mesh):
    in_specs = (
        P(("ep", "tp"), None),
        P(),
        P(None, "tp"),
        P(None, "tp"),
        P(None, "tp"),
        P("tp", None),
        P(),
        P(),
        P("ep", None, "tp"),
        P("ep", None, "tp"),
        P("ep", "tp", None),
        P(("ep", "tp"), None),
        P(("ep", "tp"), None),
        P("ep", None),
        P("ep", None),
    )
    out_specs = (
        P(("ep", "tp"), None),
        P(("ep", "tp"), None),
        P(),
        P(None, "tp"),
        P(None, "tp"),
        P(None, "tp"),
        P("tp", None),
        P(),
        P(),
        P("ep", None, "tp"),
        P("ep", None, "tp"),
        P("ep", "tp", None),
    )
    return jax.shard_map(local, mesh=mesh, in_specs=in_specs, out_specs=out_specs, check_vma=False)
```

```python
import math

import jax
import jax.numpy as jnp
from jax import lax
from jax.experimental import pallas as pl
from jax.experimental.pallas import tpu as pltpu
from jax.sharding import PartitionSpec as P

HEAD_SIZE_DIM = 64


EPS = 1e-06
HIGH_PRECISION = lax.Precision.HIGHEST


def rms_norm(activation, gain_vec):
    factor = lax.rsqrt(jnp.mean(activation * activation, axis=-1, keepdims=True) + EPS)
    return activation * factor * gain_vec


def rotate(vectors, cos_table, sin_table):
    half_size = vectors.shape[-1] // 2
    first_half = vectors[..., :half_size]
    second_half = vectors[..., half_size:]
    return jnp.concatenate(
        [
            first_half * cos_table - second_half * sin_table,
            second_half * cos_table + first_half * sin_table,
        ],
        axis=-1,
    )


def angle_tables(span_length, head_size):
    half_size = head_size // 2
    inverse = jnp.exp(
        -math.log(10000.0) * jnp.arange(half_size, dtype=jnp.float32) * 2.0 / head_size
    )
    angles = jnp.arange(span_length, dtype=jnp.float32)[:, None] * inverse[None, :]
    return (jnp.cos(angles), jnp.sin(angles))


def swiglu(gate_val, up_val):
    return jax.nn.silu(gate_val) * up_val


def softmax_rows(logits):
    return jax.nn.softmax(logits, axis=-1)


def block_mask(segment_row, live_row, offset, height):
    span_length = segment_row.shape[0]
    key_places = jnp.arange(span_length)
    query_places = offset + jnp.arange(height)
    same_doc = segment_row[:, None] == segment_row[None, :]
    causal = key_places[None, :] <= query_places[:, None]
    usable = (live_row[None, :] > 0) | (key_places[None, :] == query_places[:, None])
    return same_doc & causal & usable


def block_scores(query_block, key_val, allowed, factor):
    scores = (
        jnp.einsum("qgrd,kgd->grqk", query_block, key_val, preferred_element_type=jnp.float32)
        * factor
    )
    return jnp.where(allowed[None, None], scores, -1e30)


def group_rows(boxes):
    return lax.all_gather(boxes, "tp", axis=0, tiled=True)


def dispatch_rows(boxes):
    return lax.all_to_all(boxes, "ep", split_axis=1, concat_axis=1, tiled=True)


def return_rows(boxes):
    return lax.all_to_all(boxes, "ep", split_axis=1, concat_axis=1, tiled=True)


def local_routed(
    tokens,
    norm_gain,
    query_matrix,
    key_matrix,
    value_matrix,
    out_weight,
    moe_gain,
    router_weight,
    gate_weight,
    up_weight,
    down_weight,
    cotangent,
    expert_ids,
    segments,
    valid_mask,
):
    quarter = tokens.shape[0]
    width = tokens.shape[1]
    groups = lax.axis_size("tp")
    owners = lax.axis_size("ep")
    my_part = lax.axis_index("tp")
    seq_len = quarter * groups
    head_size = HEAD_SIZE_DIM
    kv_heads = key_matrix.shape[1] // head_size
    q_heads = query_matrix.shape[1] // head_size
    group_factor = q_heads // kv_heads
    local_experts = gate_weight.shape[0]
    experts_all = router_weight.shape[1]
    chosen_count = expert_ids.shape[1]
    slots = max(8, 3 * quarter * chosen_count // (2 * experts_all) // 8 * 8)
    factor = 1.0 / math.sqrt(head_size)
    segment_row = segments[0]
    live_row = valid_mask[0]
    x_float = tokens.astype(jnp.float32)
    normed = rms_norm(x_float, norm_gain).astype(jnp.bfloat16)
    normed_all = lax.all_gather(normed, "tp", axis=0, tiled=True)
    query_unrotated = jnp.dot(normed_all, query_matrix, preferred_element_type=jnp.float32).reshape(
        seq_len, kv_heads, group_factor, head_size
    )
    key_unrotated = jnp.dot(normed_all, key_matrix, preferred_element_type=jnp.float32).reshape(
        seq_len, kv_heads, head_size
    )
    value_vectors = (
        jnp.dot(normed_all, value_matrix, preferred_element_type=jnp.float32)
        .astype(jnp.bfloat16)
        .reshape(seq_len, kv_heads, head_size)
    )
    cos_table, sin_table = angle_tables(seq_len, head_size)
    cos_query = cos_table[:, None, None, :]
    sin_query = sin_table[:, None, None, :]
    cos_key = cos_table[:, None, :]
    sin_key = sin_table[:, None, :]
    query_val = rotate(query_unrotated, cos_query, sin_query).astype(jnp.bfloat16)
    key_val = rotate(key_unrotated, cos_key, sin_key).astype(jnp.bfloat16)
    height = min(512, seq_len)
    offset = 0
    allowed = block_mask(segment_row, live_row, offset, height)
    scores = block_scores(query_val, key_val, allowed, factor)
    peak = jnp.max(scores, axis=-1, keepdims=True)
    expo = jnp.exp(scores - peak)
    denom = jnp.sum(expo, axis=-1, keepdims=True)
    weights = (expo / denom).astype(jnp.bfloat16)
    mixed = jnp.einsum("grqk,kgd->qgrd", weights, value_vectors, preferred_element_type=jnp.float32)
    outputs = mixed.reshape(height, q_heads * head_size)
    log_sums = [peak + jnp.log(denom)]
    attended = outputs.astype(jnp.bfloat16)
    branch = lax.psum_scatter(
        jnp.dot(attended, out_weight, preferred_element_type=jnp.float32),
        "tp",
        scatter_dimension=0,
        tiled=True,
    )
    middle = x_float + branch
    moe_in = rms_norm(middle, moe_gain).astype(jnp.bfloat16)
    logits = jnp.dot(moe_in, router_weight, preferred_element_type=jnp.float32)
    router = softmax_rows(logits)
    my_valid = lax.dynamic_slice_in_dim(live_row, my_part * quarter, quarter, 0)
    valid_float = my_valid.astype(jnp.float32)
    picked = jnp.take_along_axis(router, expert_ids, axis=1) * valid_float[:, None]
    flat_ids = expert_ids.reshape(-1)
    flat_live = jnp.repeat(my_valid, chosen_count)
    named = (expert_ids[:, :, None] == jnp.arange(experts_all)[None, None, :]).astype(jnp.float32)
    chosen = (jnp.sum(named, axis=1) * valid_float[:, None]).astype(jnp.bfloat16)
    before = (jnp.arange(quarter)[None, :] < jnp.arange(quarter)[:, None]).astype(jnp.bfloat16)
    earlier = jnp.dot(before, chosen, preferred_element_type=jnp.float32)
    slot_of = jnp.sum(named * earlier[:, None, :], axis=2).astype(jnp.int32).reshape(-1)
    target = jnp.where(flat_live > 0, flat_ids, experts_all)
    safe_target = jnp.minimum(target, experts_all - 1)

    def pack(row_block):
        boxes = jnp.zeros((experts_all, slots, width), jnp.bfloat16)
        boxes = boxes.at[target, slot_of].set(row_block, mode="drop")
        return boxes.reshape(1, owners, local_experts * slots, width)

    def unpack(boxes):
        flat_boxes = boxes.reshape(experts_all, slots, width)
        taken = flat_boxes[safe_target, slot_of]
        taken = jnp.where(flat_live[:, None] > 0, taken, jnp.zeros_like(taken))
        return taken.reshape(quarter, chosen_count, width)

    sent = pack(jnp.repeat(moe_in, chosen_count, axis=0))
    full_gate, full_up, full_down = (gate_weight, up_weight, down_weight)
    arrived = group_rows(dispatch_rows(sent))
    expert_rows = arrived.reshape(groups, owners, local_experts, slots, width)
    gate_val = jnp.einsum(
        "tsecd,edf->tsecf", expert_rows, gate_weight, preferred_element_type=jnp.float32
    )
    up_val = jnp.einsum(
        "tsecd,edf->tsecf", expert_rows, up_weight, preferred_element_type=jnp.float32
    )
    hidden = swiglu(gate_val, up_val).astype(jnp.bfloat16)
    result = jnp.einsum("tsecf,efd->tsecd", hidden, down_weight, preferred_element_type=jnp.float32)
    finished = lax.psum_scatter(
        result.reshape(1 * lax.axis_size("tp"), owners, local_experts * slots, width).astype(
            jnp.bfloat16
        ),
        "tp",
        scatter_dimension=0,
        tiled=True,
    )
    returned = return_rows(finished)
    result_rows = unpack(returned).astype(jnp.float32)
    output = (middle + jnp.sum(picked[:, :, None] * result_rows, axis=1)).astype(jnp.bfloat16)
    grad_out = cotangent.astype(jnp.float32)
    grad_picked = jnp.einsum("tkd,td->tk", result_rows, grad_out, precision=HIGH_PRECISION)
    onehot_float = (expert_ids[:, :, None] == jnp.arange(experts_all)[None, None, :]).astype(
        jnp.float32
    )
    grad_router = jnp.sum(onehot_float * (grad_picked * valid_float[:, None])[:, :, None], axis=1)
    _, soft_back = jax.vjp(softmax_rows, logits)
    grad_logits = soft_back(grad_router)[0]
    grad_result = (
        (picked[:, :, None] * grad_out[:, None, :])
        .astype(jnp.bfloat16)
        .reshape(quarter * chosen_count, width)
    )
    grad_sent = pack(grad_result)
    grad_arrived = group_rows(dispatch_rows(grad_sent))
    grad_rows = grad_arrived.reshape(groups, owners, local_experts, slots, width)
    gate_all = jnp.einsum(
        "tsecd,edf->tsecf", expert_rows, full_gate, preferred_element_type=jnp.float32
    )
    up_all = jnp.einsum(
        "tsecd,edf->tsecf", expert_rows, full_up, preferred_element_type=jnp.float32
    )
    hidden_all, swiglu_back = jax.vjp(swiglu, gate_all, up_all)
    hidden_low = hidden_all.astype(jnp.bfloat16)
    grad_hidden = jnp.einsum(
        "tsecd,efd->tsecf", grad_rows, full_down, preferred_element_type=jnp.float32
    )
    grad_gate_f, grad_up_f = swiglu_back(grad_hidden)
    grad_gate_rows = grad_gate_f.astype(jnp.bfloat16)
    grad_up_rows = grad_up_f.astype(jnp.bfloat16)
    down_grad = jnp.einsum(
        "tsecf,tsecd->efd", hidden_low, grad_rows, preferred_element_type=jnp.float32
    )
    gate_grad = jnp.einsum(
        "tsecd,tsecf->edf", expert_rows, grad_gate_rows, preferred_element_type=jnp.float32
    )
    up_grad = jnp.einsum(
        "tsecd,tsecf->edf", expert_rows, grad_up_rows, preferred_element_type=jnp.float32
    )
    summed = jnp.einsum(
        "tsecf,edf->tsecd", grad_gate_rows, gate_weight, preferred_element_type=jnp.float32
    )
    summed = summed + jnp.einsum(
        "tsecf,edf->tsecd", grad_up_rows, up_weight, preferred_element_type=jnp.float32
    )
    grad_finished = lax.psum_scatter(
        summed.reshape(1 * lax.axis_size("tp"), owners, local_experts * slots, width).astype(
            jnp.bfloat16
        ),
        "tp",
        scatter_dimension=0,
        tiled=True,
    )
    grad_returned = return_rows(grad_finished)
    grad_copies = unpack(grad_returned).astype(jnp.float32)
    router_float = router_weight.astype(jnp.float32)
    grad_moe_in = jnp.sum(grad_copies, axis=1) + jnp.dot(
        grad_logits, router_float.T, precision=HIGH_PRECISION
    )
    router_grad = jnp.dot(moe_in.astype(jnp.float32).T, grad_logits, precision=HIGH_PRECISION)
    _, norm_two_back = jax.vjp(rms_norm, middle, moe_gain)
    grad_mid_norm, moe_gain_grad = norm_two_back(grad_moe_in)
    grad_middle = grad_out + grad_mid_norm
    grad_branch = lax.all_gather(grad_middle.astype(jnp.bfloat16), "tp", axis=0, tiled=True)
    out_grad = jnp.einsum("sh,sd->hd", attended, grad_branch, preferred_element_type=jnp.float32)
    grad_attended = jnp.einsum(
        "sd,hd->sh", grad_branch, out_weight, preferred_element_type=jnp.float32
    ).astype(jnp.bfloat16)
    grad_attended = grad_attended.reshape(seq_len, kv_heads, group_factor, head_size)
    query_parts = []
    key_total = jnp.zeros((seq_len, kv_heads, head_size), jnp.float32)
    value_total = jnp.zeros((seq_len, kv_heads, head_size), jnp.float32)
    for block_no, offset in enumerate(range(0, seq_len, height)):
        allowed = block_mask(segment_row, live_row, offset, height)
        scores = block_scores(query_val, key_val, allowed, factor)
        probs = jnp.where(allowed[None, None], jnp.exp(scores - log_sums[block_no]), 0.0)
        grad_probs = jnp.einsum(
            "qgrd,kgd->grqk", grad_attended, value_vectors, preferred_element_type=jnp.float32
        )
        centre = jnp.sum(probs * grad_probs, axis=-1, keepdims=True)
        grad_scores = (probs * (grad_probs - centre)).astype(jnp.bfloat16)
        query_parts.append(
            jnp.einsum("grqk,kgd->qgrd", grad_scores, key_val, preferred_element_type=jnp.float32)
            * factor
        )
        key_total = (
            jnp.einsum("grqk,qgrd->kgd", grad_scores, query_val, preferred_element_type=jnp.float32)
            * factor
        )
        value_total = jnp.einsum(
            "grqk,qgrd->kgd",
            probs.astype(jnp.bfloat16),
            grad_attended,
            preferred_element_type=jnp.float32,
        )
    grad_query_rot = query_parts[0]
    _, query_back = jax.vjp(lambda vectors: rotate(vectors, cos_query, sin_query), query_unrotated)
    _, key_back = jax.vjp(lambda vectors: rotate(vectors, cos_key, sin_key), key_unrotated)
    grad_q_pre = (
        query_back(grad_query_rot)[0].astype(jnp.bfloat16).reshape(seq_len, q_heads * head_size)
    )
    grad_k_pre = key_back(key_total)[0].astype(jnp.bfloat16).reshape(seq_len, kv_heads * head_size)
    grad_value = value_total.astype(jnp.bfloat16).reshape(seq_len, kv_heads * head_size)
    query_grad = jnp.einsum("sd,sh->dh", normed_all, grad_q_pre, preferred_element_type=jnp.float32)
    key_grad = jnp.einsum("sd,sh->dh", normed_all, grad_k_pre, preferred_element_type=jnp.float32)
    value_grad = jnp.einsum("sd,sh->dh", normed_all, grad_value, preferred_element_type=jnp.float32)
    summed = jnp.einsum("sh,dh->sd", grad_q_pre, query_matrix, preferred_element_type=jnp.float32)
    summed = summed + jnp.einsum(
        "sh,dh->sd", grad_k_pre, key_matrix, preferred_element_type=jnp.float32
    )
    summed = summed + jnp.einsum(
        "sh,dh->sd", grad_value, value_matrix, preferred_element_type=jnp.float32
    )
    grad_normed = lax.psum_scatter(
        summed.astype(jnp.bfloat16), "tp", scatter_dimension=0, tiled=True
    ).astype(jnp.float32)
    _, norm_one_back = jax.vjp(rms_norm, x_float, norm_gain)
    grad_x_norm, norm_gain_grad = norm_one_back(grad_normed)
    input_grad = grad_middle + grad_x_norm
    query_grad, key_grad, value_grad, out_grad = lax.psum(
        (query_grad, key_grad, value_grad, out_grad), "ep"
    )
    norm_gain_grad, moe_gain_grad, router_grad = lax.psum(
        (norm_gain_grad, moe_gain_grad, router_grad), ("ep", "tp")
    )
    return (
        output,
        input_grad,
        norm_gain_grad,
        query_grad,
        key_grad,
        value_grad,
        out_grad,
        moe_gain_grad,
        router_grad,
        gate_grad,
        up_grad,
        down_grad,
    )


def swap_core(value):
    return lax.ppermute(value, "tp", [(i, i ^ 1) for i in range(4)])


def swap_x(value):
    return lax.ppermute(value, "tp", [(i, i ^ 2) for i in range(4)])


def swap_y(value):
    owners = lax.axis_size("ep")
    return lax.ppermute(value, "ep", [(i, i ^ 1) for i in range(owners)])


def shift_z(value, step):
    owners = lax.axis_size("ep")
    return lax.ppermute(value, "ep", [(i, (i + 2 * step) % owners) for i in range(owners)])


def after(value, *others):
    return lax.optimization_barrier((value,) + others)[0]


def add_low(left, right):
    return (left.astype(jnp.float32) + right.astype(jnp.float32)).astype(jnp.bfloat16)


def gather_pieces(value):
    across = swap_x(value)
    other = swap_core(value)
    return value, other, across, swap_core(across)


def gather_tp(value):
    me = lax.axis_index("tp")
    rows = value.shape[0]
    full = jnp.zeros((4 * rows,) + value.shape[1:], value.dtype)
    for flip, part in enumerate(gather_pieces(value)):
        full = lax.dynamic_update_slice_in_dim(full, part, (me ^ flip) * rows, 0)
    return full


def scatter_tp(value, core_dtype):
    me = lax.axis_index("tp")
    core, across = me % 2, me // 2
    boxes = value.reshape((2, 2, value.shape[0] // 4) + value.shape[1:])
    leave = lax.dynamic_index_in_dim(boxes, 1 - core, 1, keepdims=False).astype(core_dtype)
    stay = lax.dynamic_index_in_dim(boxes, core, 1, keepdims=False)
    both = stay.astype(jnp.float32) + swap_core(leave).astype(jnp.float32)
    mine = lax.dynamic_index_in_dim(both, across, 0, keepdims=False)
    theirs = lax.dynamic_index_in_dim(both, 1 - across, 0, keepdims=False).astype(jnp.bfloat16)
    return mine + swap_x(theirs).astype(jnp.float32), theirs


def reduce_first(own_core, other_core):
    return own_core, swap_core(other_core)


def reduce_sends(boxes):
    own_core, arrived = boxes
    return add_low(own_core[2], arrived[2]), add_low(own_core[3], arrived[3])


def reduce_second(boxes, from_x, from_y):
    own_core, arrived = boxes
    half = own_core.shape[1] // 2
    parts = []
    for part, extra in ((0, from_x), (1, from_y)):
        for rows in (slice(0, half), slice(half, 2 * half)):
            total = own_core[part, rows].astype(jnp.float32) + arrived[part, rows].astype(jnp.float32)
            parts.append((total + extra[rows].astype(jnp.float32)).astype(jnp.bfloat16))
    return parts


def join_kernel(first_ref, from_y_ref, last_ref, from_x_ref, out_ref):
    half = first_ref.shape[0]
    out_ref[:half] = add_low(first_ref[...], from_y_ref[...])
    out_ref[half:] = add_low(last_ref[...], from_x_ref[...])


def reduce_home(first, from_y, last, from_x, steps):
    count = len(steps)
    half, width = first.shape[0] // count, first.shape[1]
    total = []
    for i in range(count):
        half_spec = pl.BlockSpec((half, width), lambda j, i=i: (i, 0))
        total.append(
            pl.pallas_call(
                join_kernel,
                grid=(1,),
                in_specs=[half_spec] * 4,
                out_specs=pl.BlockSpec((2 * half, width), lambda j: (0, 0)),
                out_shape=jax.ShapeDtypeStruct((2 * half, width), first.dtype),
                name="join_halves",
            )(first, from_y, last, from_x)
        )
    return [shift_z(total[i], -step) if step else total[i] for i, step in enumerate(steps)]


def butterfly_sum(value):
    value = value + swap_core(value)
    value = value + swap_x(value)
    value = value + swap_y(value)
    value = value + shift_z(value, 2)
    owners = lax.axis_size("ep")
    return value + lax.ppermute(value, "ep", [(i, i ^ 2) for i in range(owners)])


def planes_of(boxes):
    planes = boxes.shape[0]
    plane = lax.axis_index("ep") // 2
    return [lax.dynamic_index_in_dim(boxes, (plane + i) % planes, 0, keepdims=False) for i in range(planes)]


def send_planes(parts):
    return [shift_z(part.astype(jnp.bfloat16), i) for i, part in enumerate(parts) if i]


def add_all(first, others):
    return first.astype(jnp.float32) + sum(part.astype(jnp.float32) for part in others)


def spread_planes(value):
    planes = lax.axis_size("ep") // 2
    return [value] + [shift_z(value, i) for i in range(1, planes)]


def join_planes(parts):
    planes, plane = len(parts), lax.axis_index("ep") // 2
    full = jnp.zeros((planes,) + parts[0].shape, parts[0].dtype)
    for i, part in enumerate(parts):
        full = lax.dynamic_update_index_in_dim(full, part, (plane - i) % planes, 0)
    return full


def sides_of(boxes):
    y = lax.axis_index("ep") % 2
    return [lax.dynamic_index_in_dim(boxes, i, 0, keepdims=False) for i in (y, 1 - y)]


def join_sides(own, other):
    y = lax.axis_index("ep") % 2
    full = jnp.zeros((2,) + own.shape, own.dtype)
    full = lax.dynamic_update_index_in_dim(full, own, y, 0)
    return lax.dynamic_update_index_in_dim(full, other, 1 - y, 0)


FIRST_HALF = ((0, 0), (2, 0), (0, 1), (2, 1))
LAST_HALF = ((1, 0), (1, 1), (3, 0), (3, 1))
NT = (((1,), (1,)), ((), ()))
TN = (((0,), (0,)), ((), ()))


def dot_f32(left, right, dims=None):
    if dims is None:
        return jnp.dot(left, right, preferred_element_type=jnp.float32)
    return lax.dot_general(left, right, dims, preferred_element_type=jnp.float32)


def store_halves(own_ref, other_ref, block, plane, result):
    half = result.shape[0] // 2
    count = own_ref.shape[1] // (2 * half)
    for i in range(4):
        (part_a, place_a), (part_b, place_b) = FIRST_HALF[i], LAST_HALF[i]
        first = pl.ds((place_a * count + plane) * half, half)
        last = pl.ds((place_b * count + plane) * half, half)
        for side, ref in enumerate((own_ref, other_ref)):

            @pl.when(block == side * 4 + i)
            def _(ref=ref, first=first, last=last, part_a=part_a, part_b=part_b):
                ref[part_a, first, :] = result[:half]
                ref[part_b, last, :] = result[half:]


def expert_kernel(sizes, *refs):
    experts, slots, blocks, rows, routed = sizes
    x_parts, g_ref = refs[:8], refs[8]
    base_ref, order_ref, router_ref, gate_ref, up_ref, down_ref = refs[9:15]
    own_ref, other_ref, xr_out, gr_out, dgu_ref, wh_ref, rg_ref, picks = refs[15:23]
    xs, gs, xr, gr, wgu, wd, back, probs, weight, d_weight, table = refs[23:34]
    x_sem, g_sem, w_sem, out_sem = refs[34:38]
    width = xs.shape[1]
    units = wd.shape[1]
    total = experts * slots
    depth = blocks * slots
    for b in range(blocks):
        source = pl.ds(pl.multiple_of(order_ref[b] * rows, rows), rows)
        pltpu.make_async_copy(x_parts[b], xs.at[pl.ds(b * rows, rows)], x_sem.at[b]).start()
        pltpu.make_async_copy(g_ref.at[source], gs.at[pl.ds(b * rows, rows)], g_sem.at[b]).start()
    for e in range(experts):
        pltpu.make_async_copy(gate_ref.at[e], wgu.at[e, :, pl.ds(0, units)], w_sem.at[0, e]).start()
        pltpu.make_async_copy(up_ref.at[e], wgu.at[e, :, pl.ds(units, units)], w_sem.at[1, e]).start()
        pltpu.make_async_copy(down_ref.at[e], wd.at[e], w_sem.at[2, e]).start()
    rg_ref[...] = jnp.zeros_like(rg_ref)

    def block_rows(b):
        return pl.ds(pl.multiple_of(b * rows, rows), rows)

    def slot_rows(b):
        return pl.ds(pl.multiple_of(b * slots, slots), slots)

    def expand(values):
        return jnp.concatenate([jnp.broadcast_to(values[e], (slots, rows)) for e in range(experts)], axis=0)

    place = jnp.concatenate(
        [lax.broadcasted_iota(jnp.int32, (slots, rows), 0)] * experts, axis=0
    ).astype(jnp.float32)

    def gather_x(b, carry):
        pltpu.make_async_copy(xs.at[block_rows(b)], xs.at[block_rows(b)], x_sem.at[b]).wait()
        pltpu.make_async_copy(gs.at[block_rows(b)], gs.at[block_rows(b)], g_sem.at[b]).wait()
        x_block = xs[block_rows(b), :]
        logits = dot_f32(router_ref[...], x_block, NT)
        lane = lax.broadcasted_iota(jnp.int32, logits.shape, 0)
        logits = jnp.where(lane < routed, logits, -1e30)
        expo = jnp.exp(logits - jnp.max(logits, axis=0, keepdims=True))
        prob = expo / jnp.sum(expo, axis=0, keepdims=True)
        probs[b] = prob
        table[...] = gs[block_rows(b), width:].astype(jnp.float32).T
        hit = expand([table[pl.ds(base_ref[0] + e, 1), :] for e in range(experts)]) == place
        prob_rows = expand([prob[e : e + 1, :] for e in range(experts)])
        chosen = jnp.sum(jnp.where(hit, prob_rows, 0.0), axis=1, keepdims=True)
        chosen = jnp.broadcast_to(chosen, (total, rows))
        one = hit.astype(jnp.float32).astype(jnp.bfloat16)
        picks[b] = one
        taken = dot_f32(one, x_block).astype(jnp.bfloat16)
        for e in range(experts):
            xr[e, slot_rows(b), :] = taken[e * slots : (e + 1) * slots]
            weight[e, slot_rows(b), :] = chosen[e * slots : (e + 1) * slots]
        back[b, pl.ds(total, router_ref.shape[0]), :] = router_ref[...]
        return carry

    def gather_g(b, carry):
        taken = dot_f32(picks[b], gs[block_rows(b), :width]).astype(jnp.bfloat16)
        for e in range(experts):
            gr[e, slot_rows(b), :] = taken[e * slots : (e + 1) * slots]
        return carry

    lax.fori_loop(0, blocks, gather_x, 0)
    pltpu.make_async_copy(xr, xr_out, out_sem.at[0]).start()
    lax.fori_loop(0, blocks, gather_g, 0)
    pltpu.make_async_copy(gr, gr_out, out_sem.at[1]).start()

    def one_expert(e, carry):
        low, high = pl.ds(0, units), pl.ds(units, units)
        pltpu.make_async_copy(wgu.at[e, :, low], wgu.at[e, :, low], w_sem.at[0, e]).wait()
        pltpu.make_async_copy(wgu.at[e, :, high], wgu.at[e, :, high], w_sem.at[1, e]).wait()
        pltpu.make_async_copy(wd.at[e], wd.at[e], w_sem.at[2, e]).wait()
        both = dot_f32(xr[e], wgu[e])
        gate, up = both[:, :units], both[:, units:]
        back_hidden = dot_f32(gr[e], wd[e], NT)
        sig = 1.0 / (1.0 + jnp.exp(-gate))
        silu = gate * sig
        hidden = silu * up
        product = hidden.astype(jnp.bfloat16).astype(jnp.float32) * back_hidden
        d_weight[e] = jnp.broadcast_to(jnp.sum(product, axis=1, keepdims=True), (depth, rows))
        share = weight[e]
        d_hidden = share * back_hidden
        d_gate = d_hidden * up * (sig * (1.0 + gate * (1.0 - sig)))
        d_up = d_hidden * silu
        d_both = jnp.concatenate([d_gate, d_up], axis=1).astype(jnp.bfloat16)
        dgu_ref[e] = d_both
        wh_ref[e] = (share * hidden).astype(jnp.bfloat16)
        d_rows = dot_f32(d_both, wgu[e], NT).astype(jnp.bfloat16)
        for b in range(blocks):
            back[b, slot_rows(e), :] = d_rows[b * slots : (b + 1) * slots]
        return carry

    lax.fori_loop(0, experts, one_expert, 0)

    def scatter(b, carry):
        one = picks[b]
        d_slot = jnp.concatenate([d_weight[e, slot_rows(b), :] for e in range(experts)], axis=0)
        spread = one.astype(jnp.float32) * d_slot
        d_prob = jnp.concatenate(
            [jnp.sum(spread[e * slots : (e + 1) * slots], axis=0, keepdims=True) for e in range(experts)]
            + [jnp.zeros((router_ref.shape[0] - experts, rows), jnp.float32)],
            axis=0,
        )
        prob = probs[b]
        centre = jnp.sum(prob * d_prob, axis=0, keepdims=True)
        d_logits = (prob * (d_prob - centre)).astype(jnp.bfloat16)
        rg_ref[...] += dot_f32(d_logits, xs[block_rows(b), :])
        result = dot_f32(jnp.concatenate([one, d_logits], axis=0), back[b], TN).astype(jnp.bfloat16)
        store_halves(own_ref, other_ref, b, 0, result)
        return carry

    lax.fori_loop(0, blocks, scatter, 0)
    pltpu.make_async_copy(xr, xr_out, out_sem.at[0]).wait()
    pltpu.make_async_copy(gr, gr_out, out_sem.at[1]).wait()


def expert_call(x_parts, g_all, base, order, router_rows, gate_weight, up_weight, down_weight, routed, slots):
    blocks = len(x_parts)
    rows, width = x_parts[0].shape
    experts, _, units = gate_weight.shape
    depth = blocks * slots
    padded = router_rows.shape[0]
    extra = g_all.shape[1] - width
    low, full = jnp.bfloat16, jnp.float32
    any_spec = pl.BlockSpec(memory_space=pl.ANY)
    vmem_spec = pl.BlockSpec(memory_space=pltpu.VMEM)
    smem_spec = pl.BlockSpec(memory_space=pltpu.SMEM)
    return pl.pallas_call(
        lambda *refs: expert_kernel((experts, slots, blocks, rows, routed), *refs),
        out_shape=(
            jax.ShapeDtypeStruct((4, rows, width), low),
            jax.ShapeDtypeStruct((4, rows, width), low),
            jax.ShapeDtypeStruct((experts, depth, width), low),
            jax.ShapeDtypeStruct((experts, depth, width), low),
            jax.ShapeDtypeStruct((experts, depth, 2 * units), low),
            jax.ShapeDtypeStruct((experts, depth, units), low),
            jax.ShapeDtypeStruct((padded, width), full),
            jax.ShapeDtypeStruct((blocks, experts * slots, rows), low),
        ),
        in_specs=[any_spec] * 9 + [smem_spec, smem_spec, vmem_spec] + [any_spec] * 3,
        out_specs=(vmem_spec, vmem_spec, any_spec, any_spec) + (vmem_spec,) * 4,
        scratch_shapes=[
            pltpu.VMEM((blocks * rows, width), low),
            pltpu.VMEM((blocks * rows, width + extra), low),
            pltpu.VMEM((experts, depth, width), low),
            pltpu.VMEM((experts, depth, width), low),
            pltpu.VMEM((experts, width, 2 * units), low),
            pltpu.VMEM((experts, units, width), low),
            pltpu.VMEM((blocks, experts * slots + padded, width), low),
            pltpu.VMEM((blocks, padded, rows), full),
            pltpu.VMEM((experts, depth, rows), full),
            pltpu.VMEM((experts, depth, rows), full),
            pltpu.VMEM((extra, rows), full),
            pltpu.SemaphoreType.DMA((blocks,)),
            pltpu.SemaphoreType.DMA((blocks,)),
            pltpu.SemaphoreType.DMA((3, experts)),
            pltpu.SemaphoreType.DMA((2,)),
        ],
        compiler_params=pltpu.CompilerParams(vmem_limit_bytes=50 * 2**20),
        cost_estimate=pl.CostEstimate(
            flops=2 * experts * depth * width * units * 40, bytes_accessed=60 * 2**20, transcendentals=0
        ),
        name="expert_chunk",
    )(*x_parts, g_all, base, order, router_rows, gate_weight, up_weight, down_weight)


def output_kernel(sizes, *refs):
    experts, slots, blocks, planes = sizes
    weighted, picks = refs[:planes], refs[planes : 2 * planes]
    down_ref, own_ref, other_ref, rows_ref = refs[2 * planes :]
    for plane in range(planes):

        def one_expert(e, carry, plane=plane):
            result = dot_f32(weighted[plane][e], down_ref[e]).astype(jnp.bfloat16)
            for b in range(blocks):
                rows_ref[b, pl.ds(pl.multiple_of(e * slots, slots), slots), :] = result[b * slots : (b + 1) * slots]
            return carry

        lax.fori_loop(0, experts, one_expert, 0)

        def scatter(b, carry, plane=plane):
            result = dot_f32(picks[plane][b], rows_ref[b], TN).astype(jnp.bfloat16)
            store_halves(own_ref, other_ref, b, plane, result)
            return carry

        lax.fori_loop(0, blocks, scatter, 0)


def output_call(weighted, picks, down_weight):
    planes = len(weighted)
    experts, depth, units = weighted[0].shape
    width = down_weight.shape[2]
    blocks, total, rows = picks[0].shape
    boxes = jax.ShapeDtypeStruct((4, planes * rows, width), jnp.bfloat16)
    vmem_spec = pl.BlockSpec(memory_space=pltpu.VMEM)
    return pl.pallas_call(
        lambda *refs: output_kernel((experts, total // experts, blocks, planes), *refs),
        in_specs=[vmem_spec] * (2 * planes + 1),
        out_specs=(vmem_spec,) * 2,
        out_shape=(boxes, boxes),
        scratch_shapes=[pltpu.VMEM((blocks, total, width), jnp.bfloat16)],
        compiler_params=pltpu.CompilerParams(vmem_limit_bytes=40 * 2**20),
        cost_estimate=pl.CostEstimate(
            flops=2 * planes * experts * depth * width * units * 12,
            bytes_accessed=planes * 18 * 2**20,
            transcendentals=0,
        ),
        name="expert_output",
    )(*weighted, *picks, down_weight)


def weight_kernel(count, *refs):
    xr, gr, dgu, wh = (refs[i * count : (i + 1) * count] for i in range(4))
    gate_ref, up_ref, down_ref = refs[4 * count :]
    units = gate_ref.shape[2]
    both = sum(dot_f32(x[0], d[0], TN) for x, d in zip(xr, dgu))
    gate_ref[0] = both[:, :units]
    up_ref[0] = both[:, units:]
    down_ref[0] = sum(dot_f32(h[0], g[0], TN) for h, g in zip(wh, gr))


def weight_call(xr, gr, dgu, wh):
    count = len(xr)
    experts, depth, width = xr[0].shape
    units = wh[0].shape[2]
    spec = lambda array: pl.BlockSpec((1,) + array.shape[1:], lambda e: (e, 0, 0))
    operands = [*xr, *gr, *dgu, *wh]
    up_like = jax.ShapeDtypeStruct((experts, width, units), jnp.float32)
    down_like = jax.ShapeDtypeStruct((experts, units, width), jnp.float32)
    return pl.pallas_call(
        lambda *refs: weight_kernel(count, *refs),
        grid=(experts,),
        out_shape=(up_like, up_like, down_like),
        in_specs=[spec(a) for a in operands],
        out_specs=(spec(up_like), spec(up_like), spec(down_like)),
        compiler_params=pltpu.CompilerParams(vmem_limit_bytes=50 * 2**20),
        cost_estimate=pl.CostEstimate(
            flops=2 * experts * depth * count * width * units * 3,
            bytes_accessed=60 * 2**20,
            transcendentals=0,
        ),
        name="expert_weights",
    )(*operands)


def swap_halves(values, half):
    lane = lax.broadcasted_iota(jnp.int32, values.shape, 1)
    size = values.shape[1]
    return jnp.where(
        lane % (2 * half) < half, pltpu.roll(values, size - half, 1), pltpu.roll(values, half, 1)
    )


def attention_back_kernel(sizes, *refs):
    group_factor, head_size = sizes
    parts, me_ref = refs[:4], refs[4]
    att_ref, q_ref, k_ref, v_ref, normed_ref, wo_ref, wq_ref, wk_ref, wv_ref = refs[5:14]
    cos_ref, sin_ref, column_ref, row_ref, live_ref = refs[14:19]
    weights_ref, out_ref, stay_ref, leave_ref = refs[19:23]
    branch, back, d_q, d_k, d_v, d_all, sem = refs[23:30]
    rows = parts[0].shape[0]
    seq_len = branch.shape[0]
    factor = 1.0 / math.sqrt(head_size)
    me = me_ref[0]

    def place(flip):
        return pl.ds(pl.multiple_of((me ^ flip) * rows, rows), rows)

    for flip, part in enumerate(parts):
        pltpu.make_async_copy(part, branch.at[place(flip)], sem.at[flip]).start()
    for flip, part in enumerate(parts):
        pltpu.make_async_copy(part, branch.at[place(flip)], sem.at[flip]).wait()
    back[...] = dot_f32(branch[...], wo_ref[...], NT).astype(jnp.bfloat16)
    out_ref[...] = dot_f32(att_ref[...], branch[...], TN).astype(jnp.bfloat16)
    d_k[...] = jnp.zeros_like(d_k)
    d_v[...] = jnp.zeros_like(d_v)
    step = seq_len // 2
    for start in (0, step):
        keys = start + step
        shape = (step, keys)
        query_place = start + lax.broadcasted_iota(jnp.int32, shape, 0)
        key_place = lax.broadcasted_iota(jnp.int32, shape, 1)
        same = column_ref[start : start + step, :] == row_ref[:, :keys]
        usable = (live_ref[:, :keys] > 0) | (key_place == query_place)
        allowed = same & (key_place <= query_place) & usable
        for head in range(q_ref.shape[1] // head_size):
            group = head // group_factor
            mine = slice(head * head_size, (head + 1) * head_size)
            shared = slice(group * head_size, (group + 1) * head_size)
            query = q_ref[start : start + step, mine]
            key, value = k_ref[:keys, shared], v_ref[:keys, shared]
            d_out = back[start : start + step, mine]
            scores = jnp.where(allowed, dot_f32(query, key, NT) * factor, -1e30)
            expo = jnp.exp(scores - jnp.max(scores, axis=1, keepdims=True))
            probs = expo * (1.0 / jnp.sum(expo, axis=1, keepdims=True))
            d_probs = dot_f32(d_out, value, NT)
            centre = jnp.sum(probs * d_probs, axis=1, keepdims=True)
            d_scores = (probs * (d_probs - centre)).astype(jnp.bfloat16)
            d_q[start : start + step, mine] = dot_f32(d_scores, key) * factor
            d_k[:keys, shared] += dot_f32(d_scores, query, TN) * factor
            d_v[:keys, shared] += dot_f32(probs.astype(jnp.bfloat16), d_out, TN)
    pair = 2 * head_size
    q_width = q_ref.shape[1]
    kv_width = k_ref.shape[1]
    for source, count, offset in ((d_q, q_width // pair, 0), (d_k, kv_width // pair, q_width)):
        for i in range(count):
            turned = source[:, i * pair : (i + 1) * pair]
            flat = turned * cos_ref[...] + swap_halves(turned, head_size // 2) * sin_ref[...]
            d_all[:, offset + i * pair : offset + (i + 1) * pair] = flat.astype(jnp.bfloat16)
    d_all[:, q_width + kv_width :] = d_v[...].astype(jnp.bfloat16)
    width = normed_ref.shape[1]
    for i in range(4):
        features = slice(i * width // 4, (i + 1) * width // 4)
        weights_ref[features, :] = dot_f32(normed_ref[:, features], d_all[...], TN).astype(jnp.bfloat16)
    for flip in range(4):
        values = d_all[place(flip), :]
        total = dot_f32(values[:, :q_width], wq_ref[...], NT)
        total += dot_f32(values[:, q_width : q_width + kv_width], wk_ref[...], NT)
        total += dot_f32(values[:, q_width + kv_width :], wv_ref[...], NT)
        if flip % 2:
            leave_ref[flip // 2] = total.astype(jnp.bfloat16)
        else:
            stay_ref[flip // 2] = total


def attention_back_call(parts, attended, query, key, value, normed, wo, wq, wk, wv, cos, sin, segments, live, factor):
    rows, width = parts[0].shape
    seq_len, q_width = query.shape
    kv_width = key.shape[1]
    me = lax.axis_index("tp").astype(jnp.int32)[None]
    low, full = jnp.bfloat16, jnp.float32
    any_spec = pl.BlockSpec(memory_space=pl.ANY)
    vmem_spec = pl.BlockSpec(memory_space=pltpu.VMEM)
    cos_pair = jnp.tile(cos, (1, 4))
    sin_pair = jnp.tile(jnp.concatenate([sin, -sin], axis=1), (1, 2))
    return pl.pallas_call(
        lambda *refs: attention_back_kernel((factor, HEAD_SIZE_DIM), *refs),
        out_shape=(
            jax.ShapeDtypeStruct((width, q_width + 2 * kv_width), low),
            jax.ShapeDtypeStruct((q_width, width), low),
            jax.ShapeDtypeStruct((2, rows, width), full),
            jax.ShapeDtypeStruct((2, rows, width), low),
        ),
        in_specs=[any_spec] * 4 + [pl.BlockSpec(memory_space=pltpu.SMEM)] + [vmem_spec] * 14,
        out_specs=(vmem_spec,) * 4,
        scratch_shapes=[
            pltpu.VMEM((seq_len, width), low),
            pltpu.VMEM((seq_len, q_width), low),
            pltpu.VMEM((seq_len, q_width), full),
            pltpu.VMEM((seq_len, kv_width), full),
            pltpu.VMEM((seq_len, kv_width), full),
            pltpu.VMEM((seq_len, q_width + 2 * kv_width), low),
            pltpu.SemaphoreType.DMA((4,)),
        ],
        compiler_params=pltpu.CompilerParams(vmem_limit_bytes=48 * 2**20),
        cost_estimate=pl.CostEstimate(
            flops=2 * seq_len * width * (2 * q_width + 4 * kv_width) * 2 * 6,
            bytes_accessed=60 * 2**20,
            transcendentals=0,
        ),
        name="attention_back",
    )(
        *parts, me, attended, query, key, value, normed, wo, wq, wk, wv, cos_pair, sin_pair,
        segments.reshape(-1, 1), segments.reshape(1, -1), live.reshape(1, -1),
    )


def local_gathered(
    tokens,
    norm_gain,
    query_matrix,
    key_matrix,
    value_matrix,
    out_weight,
    moe_gain,
    router_weight,
    gate_weight,
    up_weight,
    down_weight,
    cotangent,
    expert_ids,
    segments,
    valid_mask,
):
    quarter = tokens.shape[0]
    width = tokens.shape[1]
    groups = lax.axis_size("tp")
    owners = lax.axis_size("ep")
    my_part = lax.axis_index("tp")
    seq_len = quarter * groups
    head_size = HEAD_SIZE_DIM
    kv_heads = key_matrix.shape[1] // head_size
    q_heads = query_matrix.shape[1] // head_size
    group_factor = q_heads // kv_heads
    local_experts = gate_weight.shape[0]
    experts_all = router_weight.shape[1]
    chosen_count = expert_ids.shape[1]
    slots = max(8, 3 * quarter * chosen_count // (2 * experts_all) // 8 * 8)
    factor = 1.0 / math.sqrt(head_size)
    segment_row = segments[0]
    live_row = valid_mask[0]
    x_float = tokens.astype(jnp.float32)
    planes = owners // 2
    owner = lax.axis_index("ep")
    my_valid = lax.dynamic_slice_in_dim(live_row, my_part * quarter, quarter, 0)
    padded = -(-experts_all // 16) * 16
    named = jnp.any(expert_ids[:, :, None] == jnp.arange(padded)[None, None, :], axis=1) & (my_valid[:, None] > 0)
    before = (jnp.arange(quarter)[None, :] < jnp.arange(quarter)[:, None]).astype(jnp.bfloat16)
    earlier = jnp.dot(before, named.astype(jnp.bfloat16), preferred_element_type=jnp.float32)
    slot = jnp.where(named, earlier, -1.0).astype(jnp.bfloat16)
    slot = jnp.pad(slot, ((0, 0), (0, -padded % 128)), constant_values=-1.0)
    sent = jnp.concatenate([cotangent, slot], axis=1)
    g_all = lax.all_gather(sent, ("ep", "tp"), axis=0, tiled=True)
    router_rows = jnp.roll(router_weight.T, -owner * local_experts, axis=0)
    router_rows = jnp.pad(router_rows, ((0, padded - experts_all), (0, 0)))
    base = (owner * local_experts).astype(jnp.int32)[None]
    step = jnp.arange(planes)[:, None]
    flip_y = jnp.array([0, 0, 1, 1, 0, 0, 1, 1])[None, :]
    flip_tp = jnp.array([0, 2, 0, 2, 1, 3, 1, 3])[None, :]
    order = (((owner // 2 - step) % planes) * 2 + (owner % 2 ^ flip_y)) * 4 + (my_part ^ flip_tp)
    order = order.astype(jnp.int32)
    tokens_all = gather_tp(tokens)
    normed_all = rms_norm(tokens_all.astype(jnp.float32), norm_gain).astype(jnp.bfloat16)
    query_unrotated = jnp.dot(normed_all, query_matrix, preferred_element_type=jnp.float32).reshape(
        seq_len, kv_heads, group_factor, head_size
    )
    key_unrotated = jnp.dot(normed_all, key_matrix, preferred_element_type=jnp.float32).reshape(
        seq_len, kv_heads, head_size
    )
    value_vectors = (
        jnp.dot(normed_all, value_matrix, preferred_element_type=jnp.float32)
        .astype(jnp.bfloat16)
        .reshape(seq_len, kv_heads, head_size)
    )
    cos_table, sin_table = angle_tables(seq_len, head_size)
    cos_query = cos_table[:, None, None, :]
    sin_query = sin_table[:, None, None, :]
    cos_key = cos_table[:, None, :]
    sin_key = sin_table[:, None, :]
    query_val = rotate(query_unrotated, cos_query, sin_query).astype(jnp.bfloat16)
    key_val = rotate(key_unrotated, cos_key, sin_key).astype(jnp.bfloat16)
    height = min(512, seq_len)
    offset = 0
    allowed = block_mask(segment_row, live_row, offset, height)
    scores = block_scores(query_val, key_val, allowed, factor)
    peak = jnp.max(scores, axis=-1, keepdims=True)
    expo = jnp.exp(scores - peak)
    denom = jnp.sum(expo, axis=-1, keepdims=True)
    weights = (expo / denom).astype(jnp.bfloat16)
    mixed = jnp.einsum("grqk,kgd->qgrd", weights, value_vectors, preferred_element_type=jnp.float32)
    outputs = mixed.reshape(height, q_heads * head_size)
    log_sums = [peak + jnp.log(denom)]
    attended = outputs.astype(jnp.bfloat16)
    branch, _ = scatter_tp(
        jnp.dot(attended, out_weight, preferred_element_type=jnp.float32), jnp.float32
    )
    middle = x_float + branch
    moe_in = rms_norm(middle, moe_gain).astype(jnp.bfloat16)
    column, x_chunks = moe_in, []
    for i in range(planes):
        column = shift_z(column, 1) if i else column
        across, along = swap_x(column), swap_y(column)
        diagonal = swap_x(along) if i % 2 else swap_y(across)
        parts = (column, across, along, diagonal)
        x_chunks.append(parts + tuple(swap_core(part) for part in parts))
    kept, boxes, sends, halves = [], [], [], []

    def second(i):
        first, first_sent, last, last_sent = reduce_second(boxes[i], swap_x(sends[i][0]), swap_y(sends[i][1]))
        halves.append((first, swap_y(first_sent), last, swap_x(last_sent)))
        return first_sent, last_sent

    for i in range(planes):
        ready = [part for chunk in x_chunks for part in chunk[1:3]] if i == 0 else []
        if i >= 2:
            sends.append(reduce_sends(boxes[i - 2]))
            ready += [*sends[i - 2]]
        if i >= 3:
            ready += second(i - 3)
        own, other, *rest = expert_call(
            x_chunks[i], g_all, base, order[i], after(router_rows, *ready),
            gate_weight, up_weight, down_weight, experts_all, slots,
        )
        kept.append(rest)
        boxes.append(reduce_first(own, other))
    xr, gr, dgu, wh, router_parts, picks = zip(*kept)
    pairs = planes
    grad_parts = []
    for i in range(planes):
        if i >= len(sends):
            sends.append(reduce_sends(boxes[i]))
        if i == planes - 1:
            own, other = output_call((after(wh[0], *sends[i]),) + wh[1:], picks, down_weight)
        if i >= len(halves):
            sent_on = second(i)
        if i == planes - 1:
            out_boxes = [reduce_first(own, after(other, *sent_on))]
        grad_parts += reduce_home(*halves[i], (i,))
    grad_moe_in = sum(part.astype(jnp.float32) for part in grad_parts)
    router_part = jnp.roll(sum(router_parts)[:experts_all], owner * local_experts, axis=0)
    grad_out = cotangent.astype(jnp.float32)
    _, norm_two_back = jax.vjp(rms_norm, middle, moe_gain)
    grad_mid_norm, moe_gain_grad = norm_two_back(grad_moe_in)
    grad_middle = grad_out + grad_mid_norm
    branch_parts = gather_pieces(grad_middle.astype(jnp.bfloat16))
    out_sends = [reduce_sends(box) for box in out_boxes]
    branch_parts, out_sends = lax.optimization_barrier((branch_parts, out_sends))
    out_from = [(swap_x(to_x), swap_y(to_y)) for to_x, to_y in out_sends]
    flat = lambda array: array.reshape(seq_len, -1)
    weights, out_grad, stay, leave = attention_back_call(
        branch_parts, attended, flat(query_val), flat(key_val), flat(value_vectors), normed_all,
        out_weight, query_matrix, key_matrix, value_matrix, cos_table, sin_table, segment_row, live_row, group_factor,
    )
    out_grad = lax.psum(out_grad, "ep")
    weights, leave, out_from = lax.optimization_barrier((weights, leave, out_from))
    cut = weights.shape[0] * 2 // 3
    columns = weights.shape[1]
    upper_own, upper_leave = sides_of(weights[:cut].reshape(2, planes, -1, columns))
    lower_parts = planes_of(weights[cut:].reshape(planes, 2, -1, columns))
    upper_came = swap_y(upper_leave)
    lower_came = send_planes(lower_parts)
    both = stay + swap_core(leave).astype(jnp.float32)
    across_came = swap_x(both[1].astype(jnp.bfloat16))
    out_second = [reduce_second(box, *came) for box, came in zip(out_boxes, out_from)]
    gate_grad, up_grad, down_grad = weight_call(xr, gr, (after(dgu[0], leave),) + dgu[1:], wh)
    upper_parts = planes_of(add_low(upper_own, upper_came))
    lower_own, lower_leave = sides_of(add_all(lower_parts[0], lower_came).astype(jnp.bfloat16))
    upper_parts, lower_leave, across_came, out_second, down_grad = lax.optimization_barrier(
        (upper_parts, lower_leave, across_came, out_second, down_grad)
    )
    upper_came = send_planes(upper_parts)
    lower_came = swap_y(lower_leave)
    out_third = [(first, swap_y(first_sent), last, swap_x(last_sent)) for first, first_sent, last, last_sent in out_second]
    grad_normed = both[0] + across_came.astype(jnp.float32)
    _, norm_one_back = jax.vjp(rms_norm, x_float, norm_gain)
    grad_x_norm, norm_gain_grad = norm_one_back(grad_normed)
    input_grad = grad_middle + grad_x_norm
    small = jnp.concatenate([router_part, moe_gain_grad[None], norm_gain_grad[None]], axis=0)
    upper_sum = add_all(upper_parts[0], upper_came).astype(jnp.bfloat16)
    lower_sum = add_low(lower_own, lower_came)
    upper_sum, lower_sum, out_third, small = lax.optimization_barrier((upper_sum, lower_sum, out_third, small))
    out_parts = []
    for i, third in enumerate(out_third):
        out_parts += reduce_home(*third, tuple(range(i * pairs, (i + 1) * pairs)))
    upper_came = spread_planes(upper_sum)
    lower_came = swap_y(lower_sum)
    small = small + swap_core(small)
    small = small + swap_x(small)
    upper_half, lower_half = join_planes(upper_came), join_sides(lower_sum, lower_came)
    upper_half, lower_half, small, out_parts = lax.optimization_barrier((upper_half, lower_half, small, out_parts))
    upper_came = swap_y(upper_half)
    lower_came = spread_planes(lower_half)
    output = (middle + sum(part.astype(jnp.float32) for part in out_parts)).astype(jnp.bfloat16)
    small = small + swap_y(small)
    small = small + shift_z(small, 2)
    small = small + lax.ppermute(small, "ep", [(i, i ^ 2) for i in range(owners)])
    out_grad = after(out_grad, small).astype(jnp.float32)
    upper = join_sides(upper_half, upper_came).reshape(cut, columns)
    lower = join_planes(lower_came).reshape(-1, columns)
    weights = jnp.concatenate([upper, lower], axis=0).astype(jnp.float32)
    q_width, kv_width = query_matrix.shape[1], key_matrix.shape[1]
    query_grad, key_grad, value_grad = jnp.split(weights, (q_width, q_width + kv_width), axis=1)
    router_grad, moe_gain_grad, norm_gain_grad = small[:experts_all].T, small[experts_all], small[experts_all + 1]
    return (
        output,
        input_grad,
        norm_gain_grad,
        query_grad,
        key_grad,
        value_grad,
        out_grad,
        moe_gain_grad,
        router_grad,
        gate_grad,
        up_grad,
        down_grad,
    )


def local(*operands):
    tokens, router_weight, gate_weight, expert_ids = operands[0], operands[7], operands[8], operands[12]
    quarter, experts_all = tokens.shape[0], router_weight.shape[1]
    slots = max(8, 3 * quarter * expert_ids.shape[1] // (2 * experts_all) // 8 * 8)
    gathers = lax.axis_size("tp") == 4 and lax.axis_size("ep") == 8 and gate_weight.shape[0] * slots >= quarter
    return (local_gathered if gathers else local_routed)(*operands)


def solution(mesh):
    in_specs = (
        P(("ep", "tp"), None),
        P(),
        P(None, "tp"),
        P(None, "tp"),
        P(None, "tp"),
        P("tp", None),
        P(),
        P(),
        P("ep", None, "tp"),
        P("ep", None, "tp"),
        P("ep", "tp", None),
        P(("ep", "tp"), None),
        P(("ep", "tp"), None),
        P("ep", None),
        P("ep", None),
    )
    out_specs = (
        P(("ep", "tp"), None),
        P(("ep", "tp"), None),
        P(),
        P(None, "tp"),
        P(None, "tp"),
        P(None, "tp"),
        P("tp", None),
        P(),
        P(),
        P("ep", None, "tp"),
        P("ep", None, "tp"),
        P("ep", "tp", None),
    )
    return jax.shard_map(local, mesh=mesh, in_specs=in_specs, out_specs=out_specs, check_vma=False)
```

```python
import math

import jax
import jax.numpy as jnp
from jax import lax
from jax.experimental import pallas as pl
from jax.experimental.pallas import tpu as pltpu
from jax.sharding import PartitionSpec as P

HEAD_SIZE_DIM = 64


EPS = 1e-06
HIGH_PRECISION = lax.Precision.HIGHEST


def rms_norm(activation, gain_vec):
    factor = lax.rsqrt(jnp.mean(activation * activation, axis=-1, keepdims=True) + EPS)
    return activation * factor * gain_vec


def rotate(vectors, cos_table, sin_table):
    half_size = vectors.shape[-1] // 2
    first_half = vectors[..., :half_size]
    second_half = vectors[..., half_size:]
    return jnp.concatenate(
        [
            first_half * cos_table - second_half * sin_table,
            second_half * cos_table + first_half * sin_table,
        ],
        axis=-1,
    )


def angle_tables(span_length, head_size):
    half_size = head_size // 2
    inverse = jnp.exp(
        -math.log(10000.0) * jnp.arange(half_size, dtype=jnp.float32) * 2.0 / head_size
    )
    angles = jnp.arange(span_length, dtype=jnp.float32)[:, None] * inverse[None, :]
    return (jnp.cos(angles), jnp.sin(angles))


def swiglu(gate_val, up_val):
    return jax.nn.silu(gate_val) * up_val


def softmax_rows(logits):
    return jax.nn.softmax(logits, axis=-1)


def block_mask(segment_row, live_row, offset, height):
    span_length = segment_row.shape[0]
    key_places = jnp.arange(span_length)
    query_places = offset + jnp.arange(height)
    same_doc = segment_row[:, None] == segment_row[None, :]
    causal = key_places[None, :] <= query_places[:, None]
    usable = (live_row[None, :] > 0) | (key_places[None, :] == query_places[:, None])
    return same_doc & causal & usable


def block_scores(query_block, key_val, allowed, factor):
    scores = (
        jnp.einsum("qgrd,kgd->grqk", query_block, key_val, preferred_element_type=jnp.float32)
        * factor
    )
    return jnp.where(allowed[None, None], scores, -1e30)


def group_rows(boxes):
    return lax.all_gather(boxes, "tp", axis=0, tiled=True)


def dispatch_rows(boxes):
    return lax.all_to_all(boxes, "ep", split_axis=1, concat_axis=1, tiled=True)


def return_rows(boxes):
    return lax.all_to_all(boxes, "ep", split_axis=1, concat_axis=1, tiled=True)


def local_routed(
    tokens,
    norm_gain,
    query_matrix,
    key_matrix,
    value_matrix,
    out_weight,
    moe_gain,
    router_weight,
    gate_weight,
    up_weight,
    down_weight,
    cotangent,
    expert_ids,
    segments,
    valid_mask,
):
    quarter = tokens.shape[0]
    width = tokens.shape[1]
    groups = lax.axis_size("tp")
    owners = lax.axis_size("ep")
    my_part = lax.axis_index("tp")
    seq_len = quarter * groups
    head_size = HEAD_SIZE_DIM
    kv_heads = key_matrix.shape[1] // head_size
    q_heads = query_matrix.shape[1] // head_size
    group_factor = q_heads // kv_heads
    local_experts = gate_weight.shape[0]
    experts_all = router_weight.shape[1]
    chosen_count = expert_ids.shape[1]
    slots = max(8, 3 * quarter * chosen_count // (2 * experts_all) // 8 * 8)
    factor = 1.0 / math.sqrt(head_size)
    segment_row = segments[0]
    live_row = valid_mask[0]
    x_float = tokens.astype(jnp.float32)
    normed = rms_norm(x_float, norm_gain).astype(jnp.bfloat16)
    normed_all = lax.all_gather(normed, "tp", axis=0, tiled=True)
    query_unrotated = jnp.dot(normed_all, query_matrix, preferred_element_type=jnp.float32).reshape(
        seq_len, kv_heads, group_factor, head_size
    )
    key_unrotated = jnp.dot(normed_all, key_matrix, preferred_element_type=jnp.float32).reshape(
        seq_len, kv_heads, head_size
    )
    value_vectors = (
        jnp.dot(normed_all, value_matrix, preferred_element_type=jnp.float32)
        .astype(jnp.bfloat16)
        .reshape(seq_len, kv_heads, head_size)
    )
    cos_table, sin_table = angle_tables(seq_len, head_size)
    cos_query = cos_table[:, None, None, :]
    sin_query = sin_table[:, None, None, :]
    cos_key = cos_table[:, None, :]
    sin_key = sin_table[:, None, :]
    query_val = rotate(query_unrotated, cos_query, sin_query).astype(jnp.bfloat16)
    key_val = rotate(key_unrotated, cos_key, sin_key).astype(jnp.bfloat16)
    height = min(512, seq_len)
    offset = 0
    allowed = block_mask(segment_row, live_row, offset, height)
    scores = block_scores(query_val, key_val, allowed, factor)
    peak = jnp.max(scores, axis=-1, keepdims=True)
    expo = jnp.exp(scores - peak)
    denom = jnp.sum(expo, axis=-1, keepdims=True)
    weights = (expo / denom).astype(jnp.bfloat16)
    mixed = jnp.einsum("grqk,kgd->qgrd", weights, value_vectors, preferred_element_type=jnp.float32)
    outputs = mixed.reshape(height, q_heads * head_size)
    log_sums = [peak + jnp.log(denom)]
    attended = outputs.astype(jnp.bfloat16)
    branch = lax.psum_scatter(
        jnp.dot(attended, out_weight, preferred_element_type=jnp.float32),
        "tp",
        scatter_dimension=0,
        tiled=True,
    )
    middle = x_float + branch
    moe_in = rms_norm(middle, moe_gain).astype(jnp.bfloat16)
    logits = jnp.dot(moe_in, router_weight, preferred_element_type=jnp.float32)
    router = softmax_rows(logits)
    my_valid = lax.dynamic_slice_in_dim(live_row, my_part * quarter, quarter, 0)
    valid_float = my_valid.astype(jnp.float32)
    picked = jnp.take_along_axis(router, expert_ids, axis=1) * valid_float[:, None]
    flat_ids = expert_ids.reshape(-1)
    flat_live = jnp.repeat(my_valid, chosen_count)
    named = (expert_ids[:, :, None] == jnp.arange(experts_all)[None, None, :]).astype(jnp.float32)
    chosen = (jnp.sum(named, axis=1) * valid_float[:, None]).astype(jnp.bfloat16)
    before = (jnp.arange(quarter)[None, :] < jnp.arange(quarter)[:, None]).astype(jnp.bfloat16)
    earlier = jnp.dot(before, chosen, preferred_element_type=jnp.float32)
    slot_of = jnp.sum(named * earlier[:, None, :], axis=2).astype(jnp.int32).reshape(-1)
    target = jnp.where(flat_live > 0, flat_ids, experts_all)
    safe_target = jnp.minimum(target, experts_all - 1)

    def pack(row_block):
        boxes = jnp.zeros((experts_all, slots, width), jnp.bfloat16)
        boxes = boxes.at[target, slot_of].set(row_block, mode="drop")
        return boxes.reshape(1, owners, local_experts * slots, width)

    def unpack(boxes):
        flat_boxes = boxes.reshape(experts_all, slots, width)
        taken = flat_boxes[safe_target, slot_of]
        taken = jnp.where(flat_live[:, None] > 0, taken, jnp.zeros_like(taken))
        return taken.reshape(quarter, chosen_count, width)

    sent = pack(jnp.repeat(moe_in, chosen_count, axis=0))
    full_gate, full_up, full_down = (gate_weight, up_weight, down_weight)
    arrived = group_rows(dispatch_rows(sent))
    expert_rows = arrived.reshape(groups, owners, local_experts, slots, width)
    gate_val = jnp.einsum(
        "tsecd,edf->tsecf", expert_rows, gate_weight, preferred_element_type=jnp.float32
    )
    up_val = jnp.einsum(
        "tsecd,edf->tsecf", expert_rows, up_weight, preferred_element_type=jnp.float32
    )
    hidden = swiglu(gate_val, up_val).astype(jnp.bfloat16)
    result = jnp.einsum("tsecf,efd->tsecd", hidden, down_weight, preferred_element_type=jnp.float32)
    finished = lax.psum_scatter(
        result.reshape(1 * lax.axis_size("tp"), owners, local_experts * slots, width).astype(
            jnp.bfloat16
        ),
        "tp",
        scatter_dimension=0,
        tiled=True,
    )
    returned = return_rows(finished)
    result_rows = unpack(returned).astype(jnp.float32)
    output = (middle + jnp.sum(picked[:, :, None] * result_rows, axis=1)).astype(jnp.bfloat16)
    grad_out = cotangent.astype(jnp.float32)
    grad_picked = jnp.einsum("tkd,td->tk", result_rows, grad_out, precision=HIGH_PRECISION)
    onehot_float = (expert_ids[:, :, None] == jnp.arange(experts_all)[None, None, :]).astype(
        jnp.float32
    )
    grad_router = jnp.sum(onehot_float * (grad_picked * valid_float[:, None])[:, :, None], axis=1)
    _, soft_back = jax.vjp(softmax_rows, logits)
    grad_logits = soft_back(grad_router)[0]
    grad_result = (
        (picked[:, :, None] * grad_out[:, None, :])
        .astype(jnp.bfloat16)
        .reshape(quarter * chosen_count, width)
    )
    grad_sent = pack(grad_result)
    grad_arrived = group_rows(dispatch_rows(grad_sent))
    grad_rows = grad_arrived.reshape(groups, owners, local_experts, slots, width)
    gate_all = jnp.einsum(
        "tsecd,edf->tsecf", expert_rows, full_gate, preferred_element_type=jnp.float32
    )
    up_all = jnp.einsum(
        "tsecd,edf->tsecf", expert_rows, full_up, preferred_element_type=jnp.float32
    )
    hidden_all, swiglu_back = jax.vjp(swiglu, gate_all, up_all)
    hidden_low = hidden_all.astype(jnp.bfloat16)
    grad_hidden = jnp.einsum(
        "tsecd,efd->tsecf", grad_rows, full_down, preferred_element_type=jnp.float32
    )
    grad_gate_f, grad_up_f = swiglu_back(grad_hidden)
    grad_gate_rows = grad_gate_f.astype(jnp.bfloat16)
    grad_up_rows = grad_up_f.astype(jnp.bfloat16)
    down_grad = jnp.einsum(
        "tsecf,tsecd->efd", hidden_low, grad_rows, preferred_element_type=jnp.float32
    )
    gate_grad = jnp.einsum(
        "tsecd,tsecf->edf", expert_rows, grad_gate_rows, preferred_element_type=jnp.float32
    )
    up_grad = jnp.einsum(
        "tsecd,tsecf->edf", expert_rows, grad_up_rows, preferred_element_type=jnp.float32
    )
    summed = jnp.einsum(
        "tsecf,edf->tsecd", grad_gate_rows, gate_weight, preferred_element_type=jnp.float32
    )
    summed = summed + jnp.einsum(
        "tsecf,edf->tsecd", grad_up_rows, up_weight, preferred_element_type=jnp.float32
    )
    grad_finished = lax.psum_scatter(
        summed.reshape(1 * lax.axis_size("tp"), owners, local_experts * slots, width).astype(
            jnp.bfloat16
        ),
        "tp",
        scatter_dimension=0,
        tiled=True,
    )
    grad_returned = return_rows(grad_finished)
    grad_copies = unpack(grad_returned).astype(jnp.float32)
    router_float = router_weight.astype(jnp.float32)
    grad_moe_in = jnp.sum(grad_copies, axis=1) + jnp.dot(
        grad_logits, router_float.T, precision=HIGH_PRECISION
    )
    router_grad = jnp.dot(moe_in.astype(jnp.float32).T, grad_logits, precision=HIGH_PRECISION)
    _, norm_two_back = jax.vjp(rms_norm, middle, moe_gain)
    grad_mid_norm, moe_gain_grad = norm_two_back(grad_moe_in)
    grad_middle = grad_out + grad_mid_norm
    grad_branch = lax.all_gather(grad_middle.astype(jnp.bfloat16), "tp", axis=0, tiled=True)
    out_grad = jnp.einsum("sh,sd->hd", attended, grad_branch, preferred_element_type=jnp.float32)
    grad_attended = jnp.einsum(
        "sd,hd->sh", grad_branch, out_weight, preferred_element_type=jnp.float32
    ).astype(jnp.bfloat16)
    grad_attended = grad_attended.reshape(seq_len, kv_heads, group_factor, head_size)
    query_parts = []
    key_total = jnp.zeros((seq_len, kv_heads, head_size), jnp.float32)
    value_total = jnp.zeros((seq_len, kv_heads, head_size), jnp.float32)
    for block_no, offset in enumerate(range(0, seq_len, height)):
        allowed = block_mask(segment_row, live_row, offset, height)
        scores = block_scores(query_val, key_val, allowed, factor)
        probs = jnp.where(allowed[None, None], jnp.exp(scores - log_sums[block_no]), 0.0)
        grad_probs = jnp.einsum(
            "qgrd,kgd->grqk", grad_attended, value_vectors, preferred_element_type=jnp.float32
        )
        centre = jnp.sum(probs * grad_probs, axis=-1, keepdims=True)
        grad_scores = (probs * (grad_probs - centre)).astype(jnp.bfloat16)
        query_parts.append(
            jnp.einsum("grqk,kgd->qgrd", grad_scores, key_val, preferred_element_type=jnp.float32)
            * factor
        )
        key_total = (
            jnp.einsum("grqk,qgrd->kgd", grad_scores, query_val, preferred_element_type=jnp.float32)
            * factor
        )
        value_total = jnp.einsum(
            "grqk,qgrd->kgd",
            probs.astype(jnp.bfloat16),
            grad_attended,
            preferred_element_type=jnp.float32,
        )
    grad_query_rot = query_parts[0]
    _, query_back = jax.vjp(lambda vectors: rotate(vectors, cos_query, sin_query), query_unrotated)
    _, key_back = jax.vjp(lambda vectors: rotate(vectors, cos_key, sin_key), key_unrotated)
    grad_q_pre = (
        query_back(grad_query_rot)[0].astype(jnp.bfloat16).reshape(seq_len, q_heads * head_size)
    )
    grad_k_pre = key_back(key_total)[0].astype(jnp.bfloat16).reshape(seq_len, kv_heads * head_size)
    grad_value = value_total.astype(jnp.bfloat16).reshape(seq_len, kv_heads * head_size)
    query_grad = jnp.einsum("sd,sh->dh", normed_all, grad_q_pre, preferred_element_type=jnp.float32)
    key_grad = jnp.einsum("sd,sh->dh", normed_all, grad_k_pre, preferred_element_type=jnp.float32)
    value_grad = jnp.einsum("sd,sh->dh", normed_all, grad_value, preferred_element_type=jnp.float32)
    summed = jnp.einsum("sh,dh->sd", grad_q_pre, query_matrix, preferred_element_type=jnp.float32)
    summed = summed + jnp.einsum(
        "sh,dh->sd", grad_k_pre, key_matrix, preferred_element_type=jnp.float32
    )
    summed = summed + jnp.einsum(
        "sh,dh->sd", grad_value, value_matrix, preferred_element_type=jnp.float32
    )
    grad_normed = lax.psum_scatter(
        summed.astype(jnp.bfloat16), "tp", scatter_dimension=0, tiled=True
    ).astype(jnp.float32)
    _, norm_one_back = jax.vjp(rms_norm, x_float, norm_gain)
    grad_x_norm, norm_gain_grad = norm_one_back(grad_normed)
    input_grad = grad_middle + grad_x_norm
    query_grad, key_grad, value_grad, out_grad = lax.psum(
        (query_grad, key_grad, value_grad, out_grad), "ep"
    )
    norm_gain_grad, moe_gain_grad, router_grad = lax.psum(
        (norm_gain_grad, moe_gain_grad, router_grad), ("ep", "tp")
    )
    return (
        output,
        input_grad,
        norm_gain_grad,
        query_grad,
        key_grad,
        value_grad,
        out_grad,
        moe_gain_grad,
        router_grad,
        gate_grad,
        up_grad,
        down_grad,
    )


def swap_core(value):
    return lax.ppermute(value, "tp", [(i, i ^ 1) for i in range(4)])


def swap_x(value):
    return lax.ppermute(value, "tp", [(i, i ^ 2) for i in range(4)])


def swap_y(value):
    owners = lax.axis_size("ep")
    return lax.ppermute(value, "ep", [(i, i ^ 1) for i in range(owners)])


def shift_z(value, step):
    owners = lax.axis_size("ep")
    return lax.ppermute(value, "ep", [(i, (i + 2 * step) % owners) for i in range(owners)])


def after(value, *others):
    return lax.optimization_barrier((value,) + others)[0]


def add_low(left, right):
    return (left.astype(jnp.float32) + right.astype(jnp.float32)).astype(jnp.bfloat16)


def gather_pieces(value):
    across = swap_x(value)
    other = swap_core(value)
    return value, other, across, swap_core(across)


def gather_tp(value):
    me = lax.axis_index("tp")
    rows = value.shape[0]
    full = jnp.zeros((4 * rows,) + value.shape[1:], value.dtype)
    for flip, part in enumerate(gather_pieces(value)):
        full = lax.dynamic_update_slice_in_dim(full, part, (me ^ flip) * rows, 0)
    return full


def scatter_tp(value, core_dtype):
    me = lax.axis_index("tp")
    core, across = me % 2, me // 2
    boxes = value.reshape((2, 2, value.shape[0] // 4) + value.shape[1:])
    leave = lax.dynamic_index_in_dim(boxes, 1 - core, 1, keepdims=False).astype(core_dtype)
    stay = lax.dynamic_index_in_dim(boxes, core, 1, keepdims=False)
    both = stay.astype(jnp.float32) + swap_core(leave).astype(jnp.float32)
    mine = lax.dynamic_index_in_dim(both, across, 0, keepdims=False)
    theirs = lax.dynamic_index_in_dim(both, 1 - across, 0, keepdims=False).astype(jnp.bfloat16)
    return mine + swap_x(theirs).astype(jnp.float32), theirs


def reduce_first(own_core, other_core):
    return own_core, swap_core(other_core)


def reduce_sends(boxes):
    own_core, arrived = boxes
    return add_low(own_core[2], arrived[2]), add_low(own_core[3], arrived[3])


def reduce_second(boxes, from_x, from_y):
    own_core, arrived = boxes
    half = own_core.shape[1] // 2
    parts = []
    for part, extra in ((0, from_x), (1, from_y)):
        for rows in (slice(0, half), slice(half, 2 * half)):
            total = own_core[part, rows].astype(jnp.float32) + arrived[part, rows].astype(jnp.float32)
            parts.append((total + extra[rows].astype(jnp.float32)).astype(jnp.bfloat16))
    return parts


def join_kernel(first_ref, from_y_ref, last_ref, from_x_ref, out_ref):
    half = first_ref.shape[0]
    out_ref[:half] = add_low(first_ref[...], from_y_ref[...])
    out_ref[half:] = add_low(last_ref[...], from_x_ref[...])


def reduce_home(first, from_y, last, from_x):
    half, width = first.shape
    half_spec = pl.BlockSpec((half, width), lambda j: (0, 0))
    return pl.pallas_call(
        join_kernel,
        grid=(1,),
        in_specs=[half_spec] * 4,
        out_specs=pl.BlockSpec((2 * half, width), lambda j: (0, 0)),
        out_shape=jax.ShapeDtypeStruct((2 * half, width), first.dtype),
        name="join_halves",
    )(first, from_y, last, from_x)


def butterfly_sum(value):
    value = value + swap_core(value)
    value = value + swap_x(value)
    value = value + swap_y(value)
    value = value + shift_z(value, 2)
    owners = lax.axis_size("ep")
    return value + lax.ppermute(value, "ep", [(i, i ^ 2) for i in range(owners)])


def planes_of(boxes):
    planes = boxes.shape[0]
    plane = lax.axis_index("ep") // 2
    return [lax.dynamic_index_in_dim(boxes, (plane + i) % planes, 0, keepdims=False) for i in range(planes)]


def send_planes(parts):
    return [shift_z(part.astype(jnp.bfloat16), i) for i, part in enumerate(parts) if i]


def add_all(first, others):
    return first.astype(jnp.float32) + sum(part.astype(jnp.float32) for part in others)


def spread_planes(value):
    planes = lax.axis_size("ep") // 2
    return [value] + [shift_z(value, i) for i in range(1, planes)]


def join_planes(parts):
    planes, plane = len(parts), lax.axis_index("ep") // 2
    full = jnp.zeros((planes,) + parts[0].shape, parts[0].dtype)
    for i, part in enumerate(parts):
        full = lax.dynamic_update_index_in_dim(full, part, (plane - i) % planes, 0)
    return full


def sides_of(boxes):
    y = lax.axis_index("ep") % 2
    return [lax.dynamic_index_in_dim(boxes, i, 0, keepdims=False) for i in (y, 1 - y)]


def join_sides(own, other):
    y = lax.axis_index("ep") % 2
    full = jnp.zeros((2,) + own.shape, own.dtype)
    full = lax.dynamic_update_index_in_dim(full, own, y, 0)
    return lax.dynamic_update_index_in_dim(full, other, 1 - y, 0)


FIRST_HALF = ((0, 0), (2, 0), (0, 1), (2, 1))
LAST_HALF = ((1, 0), (1, 1), (3, 0), (3, 1))
NT = (((1,), (1,)), ((), ()))
TN = (((0,), (0,)), ((), ()))


def dot_f32(left, right, dims=None):
    if dims is None:
        return jnp.dot(left, right, preferred_element_type=jnp.float32)
    return lax.dot_general(left, right, dims, preferred_element_type=jnp.float32)


def choose(index, values):
    out = values[0]
    for i in range(1, len(values)):
        out = jnp.where(index == i, values[i], out)
    return out


def expert_kernel(sizes, *refs):
    experts, slots, blocks, rows, routed = sizes
    x_parts, g_ref = refs[:8], refs[8]
    base_ref, order_ref, router_ref, gate_ref, up_ref, down_ref = refs[9:15]
    own_ref, other_ref, xr_out, gr_out, dgu_ref, wh_ref, rg_ref = refs[15:22]
    xs, gs, xr, gr, wgu, wd, back, picks, probs, weight, d_weight, table, leaving, tables = refs[22:36]
    x_sem, g_sem, w_sem, out_sem, leave_sem, t_sem = refs[36:42]
    width = xs.shape[1]
    units = wd.shape[1]
    total = experts * slots
    depth = blocks * slots
    def source_rows(b):
        return pl.ds(pl.multiple_of(order_ref[b] * rows, rows), rows)

    for b in range(blocks):
        pltpu.make_async_copy(x_parts[b], xs.at[pl.ds(b * rows, rows)], x_sem.at[b]).start()
        pltpu.make_async_copy(g_ref.at[source_rows(b), pl.ds(width, tables.shape[2])], tables.at[b], t_sem.at[b]).start()
    rg_ref[...] = jnp.zeros_like(rg_ref)

    def block_rows(b):
        return pl.ds(pl.multiple_of(b * rows, rows), rows)

    def slot_rows(b):
        return pl.ds(pl.multiple_of(b * slots, slots), slots)

    def expand(values):
        return jnp.concatenate([jnp.broadcast_to(values[e], (slots, rows)) for e in range(experts)], axis=0)

    place = jnp.concatenate(
        [lax.broadcasted_iota(jnp.int32, (slots, rows), 0)] * experts, axis=0
    ).astype(jnp.float32)

    def gather_x(b, carry):
        pltpu.make_async_copy(xs.at[block_rows(b)], xs.at[block_rows(b)], x_sem.at[b]).wait()
        pltpu.make_async_copy(tables.at[b], tables.at[b], t_sem.at[b]).wait()
        pltpu.make_async_copy(g_ref.at[source_rows(b), pl.ds(0, width)], gs.at[block_rows(b)], g_sem.at[b]).start()

        @pl.when(b < experts)
        def _():
            pltpu.make_async_copy(gate_ref.at[b], wgu.at[b, :, pl.ds(0, units)], w_sem.at[0, b]).start()
            pltpu.make_async_copy(up_ref.at[b], wgu.at[b, :, pl.ds(units, units)], w_sem.at[1, b]).start()
            pltpu.make_async_copy(down_ref.at[b], wd.at[b], w_sem.at[2, b]).start()

        x_block = xs[block_rows(b), :]
        logits = dot_f32(router_ref[...], x_block, NT)
        lane = lax.broadcasted_iota(jnp.int32, logits.shape, 0)
        logits = jnp.where(lane < routed, logits, -1e30)
        expo = jnp.exp(logits - jnp.max(logits, axis=0, keepdims=True))
        prob = expo / jnp.sum(expo, axis=0, keepdims=True)
        probs[b] = prob
        table[...] = tables[b].astype(jnp.float32).T
        hit = expand([table[pl.ds(base_ref[0] + e, 1), :] for e in range(experts)]) == place
        prob_rows = expand([prob[e : e + 1, :] for e in range(experts)])
        chosen = jnp.sum(jnp.where(hit, prob_rows, 0.0), axis=1, keepdims=True)
        chosen = jnp.broadcast_to(chosen, (total, rows))
        one = hit.astype(jnp.float32).astype(jnp.bfloat16)
        picks[b] = one
        taken = dot_f32(one, x_block).astype(jnp.bfloat16)
        for e in range(experts):
            xr[e, slot_rows(b), :] = taken[e * slots : (e + 1) * slots]
            weight[e, slot_rows(b), :] = chosen[e * slots : (e + 1) * slots]
        back[b, pl.ds(total, router_ref.shape[0]), :width] = router_ref[...]
        back[b, pl.ds(total, router_ref.shape[0]), width:] = jnp.zeros_like(router_ref)
        return carry

    def gather_g(b, carry):
        pltpu.make_async_copy(gs.at[block_rows(b)], gs.at[block_rows(b)], g_sem.at[b]).wait()
        taken = dot_f32(picks[b], gs[block_rows(b), :]).astype(jnp.bfloat16)
        for e in range(experts):
            gr[e, slot_rows(b), :] = taken[e * slots : (e + 1) * slots]
        return carry

    lax.fori_loop(0, blocks, gather_x, 0)
    pltpu.make_async_copy(xr, xr_out, out_sem.at[0]).start()
    lax.fori_loop(0, blocks, gather_g, 0)
    pltpu.make_async_copy(gr, gr_out, out_sem.at[1]).start()

    def one_expert(e, carry):
        low, high = pl.ds(0, units), pl.ds(units, units)
        pltpu.make_async_copy(wgu.at[e, :, low], wgu.at[e, :, low], w_sem.at[0, e]).wait()
        pltpu.make_async_copy(wgu.at[e, :, high], wgu.at[e, :, high], w_sem.at[1, e]).wait()
        pltpu.make_async_copy(wd.at[e], wd.at[e], w_sem.at[2, e]).wait()
        both = dot_f32(xr[e], wgu[e])
        gate, up = both[:, :units], both[:, units:]
        back_hidden = dot_f32(gr[e], wd[e], NT)
        sig = 1.0 / (1.0 + jnp.exp(-gate))
        silu = gate * sig
        hidden = silu * up
        product = hidden.astype(jnp.bfloat16).astype(jnp.float32) * back_hidden
        d_weight[e] = jnp.broadcast_to(jnp.sum(product, axis=1, keepdims=True), (depth, rows))
        share = weight[e]
        d_hidden = share * back_hidden
        d_gate = d_hidden * up * (sig * (1.0 + gate * (1.0 - sig)))
        d_up = d_hidden * silu
        d_both = jnp.concatenate([d_gate, d_up], axis=1).astype(jnp.bfloat16)
        dgu_ref[e] = d_both
        weighted = (share * hidden).astype(jnp.bfloat16)
        wh_ref[e] = weighted
        d_rows = dot_f32(d_both, wgu[e], NT).astype(jnp.bfloat16)
        for b in range(blocks):
            back[b, slot_rows(e), :width] = d_rows[b * slots : (b + 1) * slots]
        out_rows = dot_f32(weighted, wd[e]).astype(jnp.bfloat16)
        for b in range(blocks):
            back[b, slot_rows(e), width:] = out_rows[b * slots : (b + 1) * slots]
        return carry

    lax.fori_loop(0, experts, one_expert, 0)

    half = rows // 2

    def left(turn):
        pltpu.make_async_copy(leaving.at[turn], leaving.at[turn], leave_sem.at[turn]).wait()

    def scatter(b, carry):
        one = picks[b]
        d_slot = jnp.concatenate([d_weight[e, slot_rows(b), :] for e in range(experts)], axis=0)
        spread = one.astype(jnp.float32) * d_slot
        d_prob = jnp.concatenate(
            [jnp.sum(spread[e * slots : (e + 1) * slots], axis=0, keepdims=True) for e in range(experts)]
            + [jnp.zeros((router_ref.shape[0] - experts, rows), jnp.float32)],
            axis=0,
        )
        prob = probs[b]
        centre = jnp.sum(prob * d_prob, axis=0, keepdims=True)
        d_logits = (prob * (d_prob - centre)).astype(jnp.bfloat16)
        rg_ref[...] += dot_f32(d_logits, xs[block_rows(b), :])
        turn = b % 2

        @pl.when(b >= 2)
        def _():
            left(turn)

        leaving[turn] = dot_f32(jnp.concatenate([one, d_logits], axis=0), back[b], TN).astype(jnp.bfloat16)
        for i, table_of in enumerate((FIRST_HALF, LAST_HALF)):
            part = choose(b % 4, [place[0] for place in table_of])
            row = choose(b % 4, [place[1] for place in table_of]) * half
            target = (part, pl.ds(pl.multiple_of(row, half), half))
            for ref, mine in ((own_ref, b < 4), (other_ref, b >= 4)):

                @pl.when(mine)
                def _(ref=ref, target=target, i=i):
                    pltpu.make_async_copy(
                        leaving.at[turn, pl.ds(i * half, half)], ref.at[target], leave_sem.at[turn]
                    ).start()

        return carry

    lax.fori_loop(0, blocks, scatter, 0)
    left(0)
    left(1)
    pltpu.make_async_copy(xr, xr_out, out_sem.at[0]).wait()
    pltpu.make_async_copy(gr, gr_out, out_sem.at[1]).wait()


def expert_call(x_parts, g_all, base, order, router_rows, gate_weight, up_weight, down_weight, routed, slots):
    blocks = len(x_parts)
    rows, width = x_parts[0].shape
    experts, _, units = gate_weight.shape
    depth = blocks * slots
    padded = router_rows.shape[0]
    extra = g_all.shape[1] - width
    low, full = jnp.bfloat16, jnp.float32
    any_spec = pl.BlockSpec(memory_space=pl.ANY)
    vmem_spec = pl.BlockSpec(memory_space=pltpu.VMEM)
    smem_spec = pl.BlockSpec(memory_space=pltpu.SMEM)
    return pl.pallas_call(
        lambda *refs: expert_kernel((experts, slots, blocks, rows, routed), *refs),
        out_shape=(
            jax.ShapeDtypeStruct((4, rows, 2 * width), low),
            jax.ShapeDtypeStruct((4, rows, 2 * width), low),
            jax.ShapeDtypeStruct((experts, depth, width), low),
            jax.ShapeDtypeStruct((experts, depth, width), low),
            jax.ShapeDtypeStruct((experts, depth, 2 * units), low),
            jax.ShapeDtypeStruct((experts, depth, units), low),
            jax.ShapeDtypeStruct((padded, width), full),
        ),
        in_specs=[any_spec] * 9 + [smem_spec, smem_spec, vmem_spec] + [any_spec] * 3,
        out_specs=(any_spec,) * 4 + (vmem_spec,) * 3,
        scratch_shapes=[
            pltpu.VMEM((blocks * rows, width), low),
            pltpu.VMEM((blocks * rows, width), low),
            pltpu.VMEM((experts, depth, width), low),
            pltpu.VMEM((experts, depth, width), low),
            pltpu.VMEM((experts, width, 2 * units), low),
            pltpu.VMEM((experts, units, width), low),
            pltpu.VMEM((blocks, experts * slots + padded, 2 * width), low),
            pltpu.VMEM((blocks, experts * slots, rows), low),
            pltpu.VMEM((blocks, padded, rows), full),
            pltpu.VMEM((experts, depth, rows), full),
            pltpu.VMEM((experts, depth, rows), full),
            pltpu.VMEM((extra, rows), full),
            pltpu.VMEM((2, rows, 2 * width), low),
            pltpu.VMEM((blocks, rows, extra), low),
            pltpu.SemaphoreType.DMA((blocks,)),
            pltpu.SemaphoreType.DMA((blocks,)),
            pltpu.SemaphoreType.DMA((3, experts)),
            pltpu.SemaphoreType.DMA((2,)),
            pltpu.SemaphoreType.DMA((2,)),
            pltpu.SemaphoreType.DMA((blocks,)),
        ],
        compiler_params=pltpu.CompilerParams(vmem_limit_bytes=58 * 2**20),
        cost_estimate=pl.CostEstimate(
            flops=2 * experts * depth * width * units * 40, bytes_accessed=60 * 2**20, transcendentals=0
        ),
        name="expert_chunk",
    )(*x_parts, g_all, base, order, router_rows, gate_weight, up_weight, down_weight)


def weight_kernel(count, *refs):
    xr, gr, dgu, wh = (refs[i * count : (i + 1) * count] for i in range(4))
    gate_ref, up_ref, down_ref = refs[4 * count :]
    units = gate_ref.shape[2]
    both = sum(dot_f32(x[0], d[0], TN) for x, d in zip(xr, dgu))
    gate_ref[0] = both[:, :units]
    up_ref[0] = both[:, units:]
    down_ref[0] = sum(dot_f32(h[0], g[0], TN) for h, g in zip(wh, gr))


def weight_call(xr, gr, dgu, wh):
    count = len(xr)
    experts, depth, width = xr[0].shape
    units = wh[0].shape[2]
    spec = lambda array: pl.BlockSpec((1,) + array.shape[1:], lambda e: (e, 0, 0))
    operands = [*xr, *gr, *dgu, *wh]
    up_like = jax.ShapeDtypeStruct((experts, width, units), jnp.float32)
    down_like = jax.ShapeDtypeStruct((experts, units, width), jnp.float32)
    return pl.pallas_call(
        lambda *refs: weight_kernel(count, *refs),
        grid=(experts,),
        out_shape=(up_like, up_like, down_like),
        in_specs=[spec(a) for a in operands],
        out_specs=(spec(up_like), spec(up_like), spec(down_like)),
        compiler_params=pltpu.CompilerParams(vmem_limit_bytes=50 * 2**20),
        cost_estimate=pl.CostEstimate(
            flops=2 * experts * depth * count * width * units * 3,
            bytes_accessed=60 * 2**20,
            transcendentals=0,
        ),
        name="expert_weights",
    )(*operands)


def swap_halves(values, half):
    lane = lax.broadcasted_iota(jnp.int32, values.shape, 1)
    size = values.shape[1]
    return jnp.where(
        lane % (2 * half) < half, pltpu.roll(values, size - half, 1), pltpu.roll(values, half, 1)
    )


def branch_back_kernel(*refs):
    parts, me_ref, att_ref, wo_ref, back_ref, out_ref, branch, sem = refs[:4], *refs[4:]
    rows = parts[0].shape[0]
    for flip, part in enumerate(parts):
        target = pl.ds(pl.multiple_of((me_ref[0] ^ flip) * rows, rows), rows)
        pltpu.make_async_copy(part, branch.at[target], sem.at[flip]).start()
    for flip, part in enumerate(parts):
        target = pl.ds(pl.multiple_of((me_ref[0] ^ flip) * rows, rows), rows)
        pltpu.make_async_copy(part, branch.at[target], sem.at[flip]).wait()
    out_part = dot_f32(att_ref[...], branch[...], TN).astype(jnp.bfloat16)
    _, planes, size, _ = out_ref.shape
    for i in range(2 * planes):
        out_ref[me_ref[1] ^ (i // planes), i % planes] = out_part[i * size : (i + 1) * size]
    back_ref[...] = dot_f32(branch[...], wo_ref[...], NT).astype(jnp.bfloat16)


def branch_back_call(parts, attended, wo):
    rows, width = parts[0].shape
    seq_len, q_width = attended.shape
    planes = lax.axis_size("ep") // 2
    me = jnp.stack([lax.axis_index("tp"), lax.axis_index("ep") % 2]).astype(jnp.int32)
    vmem_spec = pl.BlockSpec(memory_space=pltpu.VMEM)
    return pl.pallas_call(
        branch_back_kernel,
        out_shape=(
            jax.ShapeDtypeStruct((seq_len, q_width), jnp.bfloat16),
            jax.ShapeDtypeStruct((2, planes, q_width // planes // 2, width), jnp.bfloat16),
        ),
        in_specs=[pl.BlockSpec(memory_space=pl.ANY)] * 4 + [pl.BlockSpec(memory_space=pltpu.SMEM)] + [vmem_spec] * 2,
        out_specs=(vmem_spec,) * 2,
        scratch_shapes=[pltpu.VMEM((seq_len, width), jnp.bfloat16), pltpu.SemaphoreType.DMA((4,))],
        compiler_params=pltpu.CompilerParams(vmem_limit_bytes=24 * 2**20),
        cost_estimate=pl.CostEstimate(
            flops=4 * seq_len * width * q_width, bytes_accessed=8 * 2**20, transcendentals=0
        ),
        name="branch_back",
    )(*parts, me, attended, wo)


def attention_back_kernel(sizes, *refs):
    group_factor, head_size = sizes
    me_ref, back, q_ref, k_ref, v_ref, normed_ref, wq_ref, wk_ref, wv_ref = refs[:9]
    cos_ref, sin_ref, column_ref, row_ref, live_ref = refs[9:14]
    upper_ref, lower_ref, stay_ref, leave_ref = refs[14:18]
    d_q, d_k, d_v, d_all = refs[18:22]
    seq_len = q_ref.shape[0]
    rows = stay_ref.shape[1]
    factor = 1.0 / math.sqrt(head_size)
    me = me_ref[0]

    def place(flip):
        return pl.ds(pl.multiple_of((me ^ flip) * rows, rows), rows)

    d_k[...] = jnp.zeros_like(d_k)
    d_v[...] = jnp.zeros_like(d_v)
    step = seq_len // 2
    for start in (0, step):
        keys = start + step
        shape = (step, keys)
        query_place = start + lax.broadcasted_iota(jnp.int32, shape, 0)
        key_place = lax.broadcasted_iota(jnp.int32, shape, 1)
        same = column_ref[start : start + step, :] == row_ref[:, :keys]
        usable = (live_ref[:, :keys] > 0) | (key_place == query_place)
        allowed = same & (key_place <= query_place) & usable
        for head in range(q_ref.shape[1] // head_size):
            group = head // group_factor
            mine = slice(head * head_size, (head + 1) * head_size)
            shared = slice(group * head_size, (group + 1) * head_size)
            query = q_ref[start : start + step, mine]
            key, value = k_ref[:keys, shared], v_ref[:keys, shared]
            d_out = back[start : start + step, mine]
            scores = jnp.where(allowed, dot_f32(query, key, NT) * factor, -1e30)
            expo = jnp.exp(scores - jnp.max(scores, axis=1, keepdims=True))
            probs = expo * (1.0 / jnp.sum(expo, axis=1, keepdims=True))
            d_probs = dot_f32(d_out, value, NT)
            centre = jnp.sum(probs * d_probs, axis=1, keepdims=True)
            d_scores = (probs * (d_probs - centre)).astype(jnp.bfloat16)
            d_q[start : start + step, mine] = dot_f32(d_scores, key) * factor
            d_k[:keys, shared] += dot_f32(d_scores, query, TN) * factor
            d_v[:keys, shared] += dot_f32(probs.astype(jnp.bfloat16), d_out, TN)
    pair = 2 * head_size
    q_width = q_ref.shape[1]
    kv_width = k_ref.shape[1]
    for source, count, offset in ((d_q, q_width // pair, 0), (d_k, kv_width // pair, q_width)):
        for i in range(count):
            turned = source[:, i * pair : (i + 1) * pair]
            flat = turned * cos_ref[...] + swap_halves(turned, head_size // 2) * sin_ref[...]
            d_all[:, offset + i * pair : offset + (i + 1) * pair] = flat.astype(jnp.bfloat16)
    d_all[:, q_width + kv_width :] = d_v[...].astype(jnp.bfloat16)
    plane, side = me_ref[1], me_ref[2]
    planes, size = lower_ref.shape[0], lower_ref.shape[1]
    for i in range(3 * planes):
        features = slice(i * size, (i + 1) * size)
        part = dot_f32(normed_ref[:, features], d_all[...], TN).astype(jnp.bfloat16)
        if i < 2 * planes:
            upper_ref[side ^ (i // planes), i % planes] = part
        else:
            lower_ref[(i + planes - plane) % planes] = part
    for flip in range(4):
        values = d_all[place(flip), :]
        total = dot_f32(values[:, :q_width], wq_ref[...], NT)
        total += dot_f32(values[:, q_width : q_width + kv_width], wk_ref[...], NT)
        total += dot_f32(values[:, q_width + kv_width :], wv_ref[...], NT)
        if flip % 2:
            leave_ref[flip // 2] = total.astype(jnp.bfloat16)
        else:
            stay_ref[flip // 2] = total


def attention_back_call(back, query, key, value, normed, wq, wk, wv, cos, sin, segments, live, factor):
    seq_len, q_width = query.shape
    width, kv_width = wk.shape
    rows = seq_len // 4
    owner = lax.axis_index("ep")
    planes = lax.axis_size("ep") // 2
    size = width // (3 * planes)
    me = jnp.stack([lax.axis_index("tp"), owner // 2, owner % 2]).astype(jnp.int32)
    low, full = jnp.bfloat16, jnp.float32
    vmem_spec = pl.BlockSpec(memory_space=pltpu.VMEM)
    cos_pair = jnp.tile(cos, (1, 4))
    sin_pair = jnp.tile(jnp.concatenate([sin, -sin], axis=1), (1, 2))
    return pl.pallas_call(
        lambda *refs: attention_back_kernel((factor, HEAD_SIZE_DIM), *refs),
        out_shape=(
            jax.ShapeDtypeStruct((2, planes, size, q_width + 2 * kv_width), low),
            jax.ShapeDtypeStruct((planes, size, q_width + 2 * kv_width), low),
            jax.ShapeDtypeStruct((2, rows, width), full),
            jax.ShapeDtypeStruct((2, rows, width), low),
        ),
        in_specs=[pl.BlockSpec(memory_space=pltpu.SMEM)] + [vmem_spec] * 13,
        out_specs=(vmem_spec,) * 4,
        scratch_shapes=[
            pltpu.VMEM((seq_len, q_width), full),
            pltpu.VMEM((seq_len, kv_width), full),
            pltpu.VMEM((seq_len, kv_width), full),
            pltpu.VMEM((seq_len, q_width + 2 * kv_width), low),
        ],
        compiler_params=pltpu.CompilerParams(vmem_limit_bytes=48 * 2**20),
        cost_estimate=pl.CostEstimate(
            flops=2 * seq_len * width * (2 * q_width + 4 * kv_width) * 2 * 6,
            bytes_accessed=60 * 2**20,
            transcendentals=0,
        ),
        name="attention_back",
    )(
        me, back, query, key, value, normed, wq, wk, wv, cos_pair, sin_pair,
        segments.reshape(-1, 1), segments.reshape(1, -1), live.reshape(1, -1),
    )


def local_gathered(
    tokens,
    norm_gain,
    query_matrix,
    key_matrix,
    value_matrix,
    out_weight,
    moe_gain,
    router_weight,
    gate_weight,
    up_weight,
    down_weight,
    cotangent,
    expert_ids,
    segments,
    valid_mask,
):
    quarter = tokens.shape[0]
    width = tokens.shape[1]
    groups = lax.axis_size("tp")
    owners = lax.axis_size("ep")
    my_part = lax.axis_index("tp")
    seq_len = quarter * groups
    head_size = HEAD_SIZE_DIM
    kv_heads = key_matrix.shape[1] // head_size
    q_heads = query_matrix.shape[1] // head_size
    group_factor = q_heads // kv_heads
    local_experts = gate_weight.shape[0]
    experts_all = router_weight.shape[1]
    chosen_count = expert_ids.shape[1]
    slots = max(8, 3 * quarter * chosen_count // (2 * experts_all) // 8 * 8)
    factor = 1.0 / math.sqrt(head_size)
    segment_row = segments[0]
    live_row = valid_mask[0]
    x_float = tokens.astype(jnp.float32)
    planes = owners // 2
    owner = lax.axis_index("ep")
    my_valid = lax.dynamic_slice_in_dim(live_row, my_part * quarter, quarter, 0)
    padded = -(-experts_all // 16) * 16
    named = jnp.any(expert_ids[:, :, None] == jnp.arange(padded)[None, None, :], axis=1) & (my_valid[:, None] > 0)
    before = (jnp.arange(quarter)[None, :] < jnp.arange(quarter)[:, None]).astype(jnp.bfloat16)
    earlier = jnp.dot(before, named.astype(jnp.bfloat16), preferred_element_type=jnp.float32)
    slot = jnp.where(named, earlier, -1.0).astype(jnp.bfloat16)
    slot = jnp.pad(slot, ((0, 0), (0, -padded % 128)), constant_values=-1.0)
    sent = jnp.concatenate([cotangent, slot], axis=1)
    g_all = lax.all_gather(sent, ("ep", "tp"), axis=0, tiled=True)
    router_rows = jnp.roll(router_weight.T, -owner * local_experts, axis=0)
    router_rows = jnp.pad(router_rows, ((0, padded - experts_all), (0, 0)))
    base = (owner * local_experts).astype(jnp.int32)[None]
    step = jnp.arange(planes)[:, None]
    flip_y = jnp.array([0, 0, 1, 1, 0, 0, 1, 1])[None, :]
    flip_tp = jnp.array([0, 2, 0, 2, 1, 3, 1, 3])[None, :]
    order = (((owner // 2 - step) % planes) * 2 + (owner % 2 ^ flip_y)) * 4 + (my_part ^ flip_tp)
    order = order.astype(jnp.int32)
    tokens_all = gather_tp(tokens)
    normed_all = rms_norm(tokens_all.astype(jnp.float32), norm_gain).astype(jnp.bfloat16)
    query_unrotated = jnp.dot(normed_all, query_matrix, preferred_element_type=jnp.float32).reshape(
        seq_len, kv_heads, group_factor, head_size
    )
    key_unrotated = jnp.dot(normed_all, key_matrix, preferred_element_type=jnp.float32).reshape(
        seq_len, kv_heads, head_size
    )
    value_vectors = (
        jnp.dot(normed_all, value_matrix, preferred_element_type=jnp.float32)
        .astype(jnp.bfloat16)
        .reshape(seq_len, kv_heads, head_size)
    )
    cos_table, sin_table = angle_tables(seq_len, head_size)
    cos_query = cos_table[:, None, None, :]
    sin_query = sin_table[:, None, None, :]
    cos_key = cos_table[:, None, :]
    sin_key = sin_table[:, None, :]
    query_val = rotate(query_unrotated, cos_query, sin_query).astype(jnp.bfloat16)
    key_val = rotate(key_unrotated, cos_key, sin_key).astype(jnp.bfloat16)
    height = min(512, seq_len)
    offset = 0
    allowed = block_mask(segment_row, live_row, offset, height)
    scores = block_scores(query_val, key_val, allowed, factor)
    peak = jnp.max(scores, axis=-1, keepdims=True)
    expo = jnp.exp(scores - peak)
    denom = jnp.sum(expo, axis=-1, keepdims=True)
    weights = (expo / denom).astype(jnp.bfloat16)
    mixed = jnp.einsum("grqk,kgd->qgrd", weights, value_vectors, preferred_element_type=jnp.float32)
    outputs = mixed.reshape(height, q_heads * head_size)
    log_sums = [peak + jnp.log(denom)]
    attended = outputs.astype(jnp.bfloat16)
    branch, _ = scatter_tp(
        jnp.dot(attended, out_weight, preferred_element_type=jnp.float32), jnp.float32
    )
    middle = x_float + branch
    moe_in = rms_norm(middle, moe_gain).astype(jnp.bfloat16)
    barrier = lax.optimization_barrier
    columns, cross, diagonal, swapped, far = [moe_in], {}, {}, {}, {}

    def send_cross(step):
        cross[step] = (swap_x(columns[step]), swap_y(columns[step]))

    def send_diagonal(step):
        diagonal[step] = swap_x(cross[step][1]) if step % 2 else swap_y(cross[step][0])

    def send_swapped(step):
        swapped[step] = tuple(swap_core(part) for part in (columns[step], *cross[step]))

    send_cross(0)
    columns.append(shift_z(columns[0], 1))
    columns[1], cross = barrier((columns[1], cross))
    send_cross(1)
    columns.append(shift_z(columns[1], 1))
    columns[2], cross = barrier((columns[2], cross))
    send_diagonal(1)
    send_swapped(1)
    send_cross(2)
    columns.append(shift_z(columns[2], 1))
    columns[3], cross, diagonal, swapped = barrier((columns[3], cross, diagonal, swapped))
    far[1] = swap_core(diagonal[1])
    turns = [*range(1, planes), 0]
    kept, grad_parts = [], []
    own, other, arrived, from_x, from_y, halves, second, home = {}, {}, {}, {}, {}, {}, {}, {}
    for stage in range(planes + 4):
        ready, sends, joined = [], None, None
        a, b, c = stage - 2, stage - 3, stage - 4
        if a in arrived:
            sends = reduce_sends((own[a], arrived[a]))
            ready += sends
        if b in from_x:
            halves[b] = reduce_second((own[b], arrived[b]), from_x[b], from_y[b])
            ready += halves[b]
        if c in second:
            joined = reduce_home(halves[c][0], second[c][0], halves[c][2], second[c][1])
            ready += [joined]
            if turns[c] == 0:
                grad_parts.append(joined)
                joined = None
        came = {}
        if stage < planes:
            step = turns[stage]
            x_parts = (columns[step], *cross[step], diagonal[step], *swapped[step], far[step])
            if stage == 0:
                send_diagonal(2)
                send_cross(3)
                send_swapped(2)
                came["gather"] = (diagonal[2], cross[3], swapped[2])
            if stage == 1:
                send_diagonal(3)
                send_diagonal(0)
                send_swapped(3)
                came["gather"] = (diagonal[3], diagonal[0], swapped[3])
            if stage == 2:
                send_swapped(0)
                came["gather"] = (swapped[0],)
            own[stage], other[stage], *rest = expert_call(
                x_parts, g_all, base, order[step], after(router_rows, *ready),
                gate_weight, up_weight, down_weight, experts_all, slots,
            )
            kept.append(rest)
            came["kernel"] = (own[stage], other[stage])
        if stage == planes:
            xr, gr, dgu, wh, router_parts = zip(*kept)
            came["weights"] = weight_call(xr, gr, (after(dgu[0], *ready),) + dgu[1:], wh)
        if stage - 1 in other:
            came["core"] = swap_core(other[stage - 1])
        if sends:
            came["cross"] = (swap_x(sends[0]), swap_y(sends[1]))
        if b in halves:
            came["second"] = (swap_y(halves[b][1]), swap_x(halves[b][3]))
        if joined is not None:
            came["home"] = shift_z(joined, -turns[c])
        came = barrier(came)
        if stage == 0:
            diagonal[2], cross[3], swapped[2] = came["gather"]
            far[2] = swap_core(diagonal[2])
        if stage == 1:
            diagonal[3], diagonal[0], swapped[3] = came["gather"]
            far[3], far[0] = swap_core(diagonal[3]), swap_core(diagonal[0])
        if stage == 2:
            (swapped[0],) = came["gather"]
        if "kernel" in came:
            own[stage], other[stage] = came["kernel"]
        if "weights" in came:
            gate_grad, up_grad, down_grad = came["weights"]
        if "core" in came:
            arrived[stage - 1] = came["core"]
        if "cross" in came:
            from_x[a], from_y[a] = came["cross"]
        if "second" in came:
            second[b] = came["second"]
        if "home" in came:
            grad_parts.append(came["home"])
    grad_moe_in = sum(part[:, :width].astype(jnp.float32) for part in grad_parts)
    expert_sum = sum(part[:, width:].astype(jnp.float32) for part in grad_parts)
    output = (middle + expert_sum).astype(jnp.bfloat16)
    router_part = jnp.roll(sum(router_parts)[:experts_all], owner * local_experts, axis=0)
    grad_out = cotangent.astype(jnp.float32)
    _, norm_two_back = jax.vjp(rms_norm, middle, moe_gain)
    grad_mid_norm, moe_gain_grad = norm_two_back(grad_moe_in)
    grad_middle = grad_out + grad_mid_norm
    branch_parts = gather_pieces(grad_middle.astype(jnp.bfloat16))
    flat = lambda array: array.reshape(seq_len, -1)
    back, out_grad = branch_back_call(branch_parts, attended, out_weight)
    out_came = swap_y(out_grad[1])
    upper, lower, stay, leave = attention_back_call(
        back, flat(query_val), flat(key_val), flat(value_vectors), normed_all,
        query_matrix, key_matrix, value_matrix, cos_table, sin_table, segment_row, live_row, group_factor,
    )
    upper, lower, stay, leave, out_came = barrier((upper, lower, stay, leave, out_came))
    out_parts = planes_of(add_low(out_grad[0], out_came))
    out_came = send_planes(out_parts)
    small = jnp.concatenate([router_part, moe_gain_grad[None]], axis=0)
    upper_came = swap_y(upper[1])
    lower_came = send_planes(lower)
    both = stay + swap_core(leave).astype(jnp.float32)
    across_came = swap_x(both[1].astype(jnp.bfloat16))
    small = small + swap_core(small)
    upper_came, lower_came, across_came, small, out_came = barrier((upper_came, lower_came, across_came, small, out_came))
    out_sum = add_all(out_parts[0], out_came).astype(jnp.bfloat16)
    out_came = spread_planes(out_sum)
    upper_parts = planes_of(add_low(upper[0], upper_came))
    lower_parts = add_all(lower[0], lower_came).astype(jnp.bfloat16).reshape(2, -1, lower.shape[-1])
    lower_own, lower_leave = sides_of(lower_parts)
    grad_normed = both[0] + across_came.astype(jnp.float32)
    _, norm_one_back = jax.vjp(rms_norm, x_float, norm_gain)
    grad_x_norm, norm_gain_grad = norm_one_back(grad_normed)
    input_grad = grad_middle + grad_x_norm
    gain_part = norm_gain_grad[None]
    gain_part = gain_part + swap_core(gain_part)
    small = jnp.concatenate([small, gain_part], axis=0)
    small = small + swap_x(small)
    small = small + swap_y(small)
    upper_came = send_planes(upper_parts)
    lower_came = swap_y(lower_leave)
    upper_came, lower_came, small, out_came = barrier((upper_came, lower_came, small, out_came))
    out_half = join_planes(out_came)
    out_came = swap_y(out_half)
    upper_sum = add_all(upper_parts[0], upper_came).astype(jnp.bfloat16)
    lower_sum = add_low(lower_own, lower_came)
    upper_came = spread_planes(upper_sum)
    lower_came = swap_y(lower_sum)
    small_came = spread_planes(small)
    upper_came, lower_came, small_came, out_came = barrier((upper_came, lower_came, small_came, out_came))
    upper_half, lower_half = join_planes(upper_came), join_sides(lower_sum, lower_came)
    small = sum(small_came)
    upper_came = swap_y(upper_half)
    lower_came = spread_planes(lower_half)
    upper_came, lower_came = barrier((upper_came, lower_came))
    out_grad = join_sides(out_half, out_came).reshape(-1, width).astype(jnp.float32)
    columns = upper_half.shape[-1]
    upper = join_sides(upper_half, upper_came).reshape(-1, columns)
    lower = join_planes(lower_came).reshape(-1, columns)
    weights = jnp.concatenate([upper, lower], axis=0).astype(jnp.float32)
    q_width, kv_width = query_matrix.shape[1], key_matrix.shape[1]
    query_grad, key_grad, value_grad = jnp.split(weights, (q_width, q_width + kv_width), axis=1)
    router_grad, moe_gain_grad, norm_gain_grad = small[:experts_all].T, small[experts_all], small[experts_all + 1]
    return (
        output,
        input_grad,
        norm_gain_grad,
        query_grad,
        key_grad,
        value_grad,
        out_grad,
        moe_gain_grad,
        router_grad,
        gate_grad,
        up_grad,
        down_grad,
    )


def local(*operands):
    tokens, router_weight, gate_weight, expert_ids = operands[0], operands[7], operands[8], operands[12]
    quarter, experts_all = tokens.shape[0], router_weight.shape[1]
    slots = max(8, 3 * quarter * expert_ids.shape[1] // (2 * experts_all) // 8 * 8)
    gathers = lax.axis_size("tp") == 4 and lax.axis_size("ep") == 8 and gate_weight.shape[0] * slots >= quarter
    return (local_gathered if gathers else local_routed)(*operands)


def solution(mesh):
    in_specs = (
        P(("ep", "tp"), None),
        P(),
        P(None, "tp"),
        P(None, "tp"),
        P(None, "tp"),
        P("tp", None),
        P(),
        P(),
        P("ep", None, "tp"),
        P("ep", None, "tp"),
        P("ep", "tp", None),
        P(("ep", "tp"), None),
        P(("ep", "tp"), None),
        P("ep", None),
        P("ep", None),
    )
    out_specs = (
        P(("ep", "tp"), None),
        P(("ep", "tp"), None),
        P(),
        P(None, "tp"),
        P(None, "tp"),
        P(None, "tp"),
        P("tp", None),
        P(),
        P(),
        P("ep", None, "tp"),
        P("ep", None, "tp"),
        P("ep", "tp", None),
    )
    return jax.shard_map(local, mesh=mesh, in_specs=in_specs, out_specs=out_specs, check_vma=False)
```

```python
import math

import jax
import jax.numpy as jnp
from jax import lax
from jax.experimental import pallas as pl
from jax.experimental.pallas import tpu as pltpu
from jax.sharding import PartitionSpec as P

HEAD_SIZE_DIM = 64


EPS = 1e-06
HIGH_PRECISION = lax.Precision.HIGHEST


def rms_norm(activation, gain_vec):
    factor = lax.rsqrt(jnp.mean(activation * activation, axis=-1, keepdims=True) + EPS)
    return activation * factor * gain_vec


def rotate(vectors, cos_table, sin_table):
    half_size = vectors.shape[-1] // 2
    first_half = vectors[..., :half_size]
    second_half = vectors[..., half_size:]
    return jnp.concatenate(
        [
            first_half * cos_table - second_half * sin_table,
            second_half * cos_table + first_half * sin_table,
        ],
        axis=-1,
    )


def angle_tables(span_length, head_size):
    half_size = head_size // 2
    inverse = jnp.exp(
        -math.log(10000.0) * jnp.arange(half_size, dtype=jnp.float32) * 2.0 / head_size
    )
    angles = jnp.arange(span_length, dtype=jnp.float32)[:, None] * inverse[None, :]
    return (jnp.cos(angles), jnp.sin(angles))


def swiglu(gate_val, up_val):
    return jax.nn.silu(gate_val) * up_val


def softmax_rows(logits):
    return jax.nn.softmax(logits, axis=-1)


def block_mask(segment_row, live_row, offset, height):
    span_length = segment_row.shape[0]
    key_places = jnp.arange(span_length)
    query_places = offset + jnp.arange(height)
    same_doc = segment_row[:, None] == segment_row[None, :]
    causal = key_places[None, :] <= query_places[:, None]
    usable = (live_row[None, :] > 0) | (key_places[None, :] == query_places[:, None])
    return same_doc & causal & usable


def block_scores(query_block, key_val, allowed, factor):
    scores = (
        jnp.einsum("qgrd,kgd->grqk", query_block, key_val, preferred_element_type=jnp.float32)
        * factor
    )
    return jnp.where(allowed[None, None], scores, -1e30)


def group_rows(boxes):
    return lax.all_gather(boxes, "tp", axis=0, tiled=True)


def dispatch_rows(boxes):
    return lax.all_to_all(boxes, "ep", split_axis=1, concat_axis=1, tiled=True)


def return_rows(boxes):
    return lax.all_to_all(boxes, "ep", split_axis=1, concat_axis=1, tiled=True)


def local_routed(
    tokens,
    norm_gain,
    query_matrix,
    key_matrix,
    value_matrix,
    out_weight,
    moe_gain,
    router_weight,
    gate_weight,
    up_weight,
    down_weight,
    cotangent,
    expert_ids,
    segments,
    valid_mask,
):
    quarter = tokens.shape[0]
    width = tokens.shape[1]
    groups = lax.axis_size("tp")
    owners = lax.axis_size("ep")
    my_part = lax.axis_index("tp")
    seq_len = quarter * groups
    head_size = HEAD_SIZE_DIM
    kv_heads = key_matrix.shape[1] // head_size
    q_heads = query_matrix.shape[1] // head_size
    group_factor = q_heads // kv_heads
    local_experts = gate_weight.shape[0]
    experts_all = router_weight.shape[1]
    chosen_count = expert_ids.shape[1]
    slots = max(8, 3 * quarter * chosen_count // (2 * experts_all) // 8 * 8)
    factor = 1.0 / math.sqrt(head_size)
    segment_row = segments[0]
    live_row = valid_mask[0]
    x_float = tokens.astype(jnp.float32)
    normed = rms_norm(x_float, norm_gain).astype(jnp.bfloat16)
    normed_all = lax.all_gather(normed, "tp", axis=0, tiled=True)
    query_unrotated = jnp.dot(normed_all, query_matrix, preferred_element_type=jnp.float32).reshape(
        seq_len, kv_heads, group_factor, head_size
    )
    key_unrotated = jnp.dot(normed_all, key_matrix, preferred_element_type=jnp.float32).reshape(
        seq_len, kv_heads, head_size
    )
    value_vectors = (
        jnp.dot(normed_all, value_matrix, preferred_element_type=jnp.float32)
        .astype(jnp.bfloat16)
        .reshape(seq_len, kv_heads, head_size)
    )
    cos_table, sin_table = angle_tables(seq_len, head_size)
    cos_query = cos_table[:, None, None, :]
    sin_query = sin_table[:, None, None, :]
    cos_key = cos_table[:, None, :]
    sin_key = sin_table[:, None, :]
    query_val = rotate(query_unrotated, cos_query, sin_query).astype(jnp.bfloat16)
    key_val = rotate(key_unrotated, cos_key, sin_key).astype(jnp.bfloat16)
    height = min(512, seq_len)
    offset = 0
    allowed = block_mask(segment_row, live_row, offset, height)
    scores = block_scores(query_val, key_val, allowed, factor)
    peak = jnp.max(scores, axis=-1, keepdims=True)
    expo = jnp.exp(scores - peak)
    denom = jnp.sum(expo, axis=-1, keepdims=True)
    weights = (expo / denom).astype(jnp.bfloat16)
    mixed = jnp.einsum("grqk,kgd->qgrd", weights, value_vectors, preferred_element_type=jnp.float32)
    outputs = mixed.reshape(height, q_heads * head_size)
    log_sums = [peak + jnp.log(denom)]
    attended = outputs.astype(jnp.bfloat16)
    branch = lax.psum_scatter(
        jnp.dot(attended, out_weight, preferred_element_type=jnp.float32),
        "tp",
        scatter_dimension=0,
        tiled=True,
    )
    middle = x_float + branch
    moe_in = rms_norm(middle, moe_gain).astype(jnp.bfloat16)
    logits = jnp.dot(moe_in, router_weight, preferred_element_type=jnp.float32)
    router = softmax_rows(logits)
    my_valid = lax.dynamic_slice_in_dim(live_row, my_part * quarter, quarter, 0)
    valid_float = my_valid.astype(jnp.float32)
    picked = jnp.take_along_axis(router, expert_ids, axis=1) * valid_float[:, None]
    flat_ids = expert_ids.reshape(-1)
    flat_live = jnp.repeat(my_valid, chosen_count)
    named = (expert_ids[:, :, None] == jnp.arange(experts_all)[None, None, :]).astype(jnp.float32)
    chosen = (jnp.sum(named, axis=1) * valid_float[:, None]).astype(jnp.bfloat16)
    before = (jnp.arange(quarter)[None, :] < jnp.arange(quarter)[:, None]).astype(jnp.bfloat16)
    earlier = jnp.dot(before, chosen, preferred_element_type=jnp.float32)
    slot_of = jnp.sum(named * earlier[:, None, :], axis=2).astype(jnp.int32).reshape(-1)
    target = jnp.where(flat_live > 0, flat_ids, experts_all)
    safe_target = jnp.minimum(target, experts_all - 1)

    def pack(row_block):
        boxes = jnp.zeros((experts_all, slots, width), jnp.bfloat16)
        boxes = boxes.at[target, slot_of].set(row_block, mode="drop")
        return boxes.reshape(1, owners, local_experts * slots, width)

    def unpack(boxes):
        flat_boxes = boxes.reshape(experts_all, slots, width)
        taken = flat_boxes[safe_target, slot_of]
        taken = jnp.where(flat_live[:, None] > 0, taken, jnp.zeros_like(taken))
        return taken.reshape(quarter, chosen_count, width)

    sent = pack(jnp.repeat(moe_in, chosen_count, axis=0))
    full_gate, full_up, full_down = (gate_weight, up_weight, down_weight)
    arrived = group_rows(dispatch_rows(sent))
    expert_rows = arrived.reshape(groups, owners, local_experts, slots, width)
    gate_val = jnp.einsum(
        "tsecd,edf->tsecf", expert_rows, gate_weight, preferred_element_type=jnp.float32
    )
    up_val = jnp.einsum(
        "tsecd,edf->tsecf", expert_rows, up_weight, preferred_element_type=jnp.float32
    )
    hidden = swiglu(gate_val, up_val).astype(jnp.bfloat16)
    result = jnp.einsum("tsecf,efd->tsecd", hidden, down_weight, preferred_element_type=jnp.float32)
    finished = lax.psum_scatter(
        result.reshape(1 * lax.axis_size("tp"), owners, local_experts * slots, width).astype(
            jnp.bfloat16
        ),
        "tp",
        scatter_dimension=0,
        tiled=True,
    )
    returned = return_rows(finished)
    result_rows = unpack(returned).astype(jnp.float32)
    output = (middle + jnp.sum(picked[:, :, None] * result_rows, axis=1)).astype(jnp.bfloat16)
    grad_out = cotangent.astype(jnp.float32)
    grad_picked = jnp.einsum("tkd,td->tk", result_rows, grad_out, precision=HIGH_PRECISION)
    onehot_float = (expert_ids[:, :, None] == jnp.arange(experts_all)[None, None, :]).astype(
        jnp.float32
    )
    grad_router = jnp.sum(onehot_float * (grad_picked * valid_float[:, None])[:, :, None], axis=1)
    _, soft_back = jax.vjp(softmax_rows, logits)
    grad_logits = soft_back(grad_router)[0]
    grad_result = (
        (picked[:, :, None] * grad_out[:, None, :])
        .astype(jnp.bfloat16)
        .reshape(quarter * chosen_count, width)
    )
    grad_sent = pack(grad_result)
    grad_arrived = group_rows(dispatch_rows(grad_sent))
    grad_rows = grad_arrived.reshape(groups, owners, local_experts, slots, width)
    gate_all = jnp.einsum(
        "tsecd,edf->tsecf", expert_rows, full_gate, preferred_element_type=jnp.float32
    )
    up_all = jnp.einsum(
        "tsecd,edf->tsecf", expert_rows, full_up, preferred_element_type=jnp.float32
    )
    hidden_all, swiglu_back = jax.vjp(swiglu, gate_all, up_all)
    hidden_low = hidden_all.astype(jnp.bfloat16)
    grad_hidden = jnp.einsum(
        "tsecd,efd->tsecf", grad_rows, full_down, preferred_element_type=jnp.float32
    )
    grad_gate_f, grad_up_f = swiglu_back(grad_hidden)
    grad_gate_rows = grad_gate_f.astype(jnp.bfloat16)
    grad_up_rows = grad_up_f.astype(jnp.bfloat16)
    down_grad = jnp.einsum(
        "tsecf,tsecd->efd", hidden_low, grad_rows, preferred_element_type=jnp.float32
    )
    gate_grad = jnp.einsum(
        "tsecd,tsecf->edf", expert_rows, grad_gate_rows, preferred_element_type=jnp.float32
    )
    up_grad = jnp.einsum(
        "tsecd,tsecf->edf", expert_rows, grad_up_rows, preferred_element_type=jnp.float32
    )
    summed = jnp.einsum(
        "tsecf,edf->tsecd", grad_gate_rows, gate_weight, preferred_element_type=jnp.float32
    )
    summed = summed + jnp.einsum(
        "tsecf,edf->tsecd", grad_up_rows, up_weight, preferred_element_type=jnp.float32
    )
    grad_finished = lax.psum_scatter(
        summed.reshape(1 * lax.axis_size("tp"), owners, local_experts * slots, width).astype(
            jnp.bfloat16
        ),
        "tp",
        scatter_dimension=0,
        tiled=True,
    )
    grad_returned = return_rows(grad_finished)
    grad_copies = unpack(grad_returned).astype(jnp.float32)
    router_float = router_weight.astype(jnp.float32)
    grad_moe_in = jnp.sum(grad_copies, axis=1) + jnp.dot(
        grad_logits, router_float.T, precision=HIGH_PRECISION
    )
    router_grad = jnp.dot(moe_in.astype(jnp.float32).T, grad_logits, precision=HIGH_PRECISION)
    _, norm_two_back = jax.vjp(rms_norm, middle, moe_gain)
    grad_mid_norm, moe_gain_grad = norm_two_back(grad_moe_in)
    grad_middle = grad_out + grad_mid_norm
    grad_branch = lax.all_gather(grad_middle.astype(jnp.bfloat16), "tp", axis=0, tiled=True)
    out_grad = jnp.einsum("sh,sd->hd", attended, grad_branch, preferred_element_type=jnp.float32)
    grad_attended = jnp.einsum(
        "sd,hd->sh", grad_branch, out_weight, preferred_element_type=jnp.float32
    ).astype(jnp.bfloat16)
    grad_attended = grad_attended.reshape(seq_len, kv_heads, group_factor, head_size)
    query_parts = []
    key_total = jnp.zeros((seq_len, kv_heads, head_size), jnp.float32)
    value_total = jnp.zeros((seq_len, kv_heads, head_size), jnp.float32)
    for block_no, offset in enumerate(range(0, seq_len, height)):
        allowed = block_mask(segment_row, live_row, offset, height)
        scores = block_scores(query_val, key_val, allowed, factor)
        probs = jnp.where(allowed[None, None], jnp.exp(scores - log_sums[block_no]), 0.0)
        grad_probs = jnp.einsum(
            "qgrd,kgd->grqk", grad_attended, value_vectors, preferred_element_type=jnp.float32
        )
        centre = jnp.sum(probs * grad_probs, axis=-1, keepdims=True)
        grad_scores = (probs * (grad_probs - centre)).astype(jnp.bfloat16)
        query_parts.append(
            jnp.einsum("grqk,kgd->qgrd", grad_scores, key_val, preferred_element_type=jnp.float32)
            * factor
        )
        key_total = (
            jnp.einsum("grqk,qgrd->kgd", grad_scores, query_val, preferred_element_type=jnp.float32)
            * factor
        )
        value_total = jnp.einsum(
            "grqk,qgrd->kgd",
            probs.astype(jnp.bfloat16),
            grad_attended,
            preferred_element_type=jnp.float32,
        )
    grad_query_rot = query_parts[0]
    _, query_back = jax.vjp(lambda vectors: rotate(vectors, cos_query, sin_query), query_unrotated)
    _, key_back = jax.vjp(lambda vectors: rotate(vectors, cos_key, sin_key), key_unrotated)
    grad_q_pre = (
        query_back(grad_query_rot)[0].astype(jnp.bfloat16).reshape(seq_len, q_heads * head_size)
    )
    grad_k_pre = key_back(key_total)[0].astype(jnp.bfloat16).reshape(seq_len, kv_heads * head_size)
    grad_value = value_total.astype(jnp.bfloat16).reshape(seq_len, kv_heads * head_size)
    query_grad = jnp.einsum("sd,sh->dh", normed_all, grad_q_pre, preferred_element_type=jnp.float32)
    key_grad = jnp.einsum("sd,sh->dh", normed_all, grad_k_pre, preferred_element_type=jnp.float32)
    value_grad = jnp.einsum("sd,sh->dh", normed_all, grad_value, preferred_element_type=jnp.float32)
    summed = jnp.einsum("sh,dh->sd", grad_q_pre, query_matrix, preferred_element_type=jnp.float32)
    summed = summed + jnp.einsum(
        "sh,dh->sd", grad_k_pre, key_matrix, preferred_element_type=jnp.float32
    )
    summed = summed + jnp.einsum(
        "sh,dh->sd", grad_value, value_matrix, preferred_element_type=jnp.float32
    )
    grad_normed = lax.psum_scatter(
        summed.astype(jnp.bfloat16), "tp", scatter_dimension=0, tiled=True
    ).astype(jnp.float32)
    _, norm_one_back = jax.vjp(rms_norm, x_float, norm_gain)
    grad_x_norm, norm_gain_grad = norm_one_back(grad_normed)
    input_grad = grad_middle + grad_x_norm
    query_grad, key_grad, value_grad, out_grad = lax.psum(
        (query_grad, key_grad, value_grad, out_grad), "ep"
    )
    norm_gain_grad, moe_gain_grad, router_grad = lax.psum(
        (norm_gain_grad, moe_gain_grad, router_grad), ("ep", "tp")
    )
    return (
        output,
        input_grad,
        norm_gain_grad,
        query_grad,
        key_grad,
        value_grad,
        out_grad,
        moe_gain_grad,
        router_grad,
        gate_grad,
        up_grad,
        down_grad,
    )


def swap_core(value):
    return lax.ppermute(value, "tp", [(i, i ^ 1) for i in range(4)])


def swap_x(value):
    return lax.ppermute(value, "tp", [(i, i ^ 2) for i in range(4)])


def swap_y(value):
    owners = lax.axis_size("ep")
    return lax.ppermute(value, "ep", [(i, i ^ 1) for i in range(owners)])


def shift_z(value, step):
    owners = lax.axis_size("ep")
    return lax.ppermute(value, "ep", [(i, (i + 2 * step) % owners) for i in range(owners)])


def after(value, *others):
    return lax.optimization_barrier((value,) + others)[0]


def add_low(left, right):
    return (left.astype(jnp.float32) + right.astype(jnp.float32)).astype(jnp.bfloat16)


def gather_pieces(value):
    across = swap_x(value)
    other = swap_core(value)
    return value, other, across, swap_core(across)


def gather_tp(value):
    me = lax.axis_index("tp")
    rows = value.shape[0]
    full = jnp.zeros((4 * rows,) + value.shape[1:], value.dtype)
    for flip, part in enumerate(gather_pieces(value)):
        full = lax.dynamic_update_slice_in_dim(full, part, (me ^ flip) * rows, 0)
    return full


def scatter_tp(value, core_dtype):
    me = lax.axis_index("tp")
    core, across = me % 2, me // 2
    boxes = value.reshape((2, 2, value.shape[0] // 4) + value.shape[1:])
    leave = lax.dynamic_index_in_dim(boxes, 1 - core, 1, keepdims=False).astype(core_dtype)
    stay = lax.dynamic_index_in_dim(boxes, core, 1, keepdims=False)
    both = stay.astype(jnp.float32) + swap_core(leave).astype(jnp.float32)
    mine = lax.dynamic_index_in_dim(both, across, 0, keepdims=False)
    theirs = lax.dynamic_index_in_dim(both, 1 - across, 0, keepdims=False).astype(jnp.bfloat16)
    return mine + swap_x(theirs).astype(jnp.float32), theirs


def reduce_sends(own_core, arrived):
    return add_low(own_core[2], arrived[0]), add_low(own_core[3], arrived[1])


def reduce_second(boxes, from_x, from_y):
    own_core, arrived = boxes
    half = own_core.shape[1] // 2
    parts = []
    for part, extra in ((0, from_x), (1, from_y)):
        for rows in (slice(0, half), slice(half, 2 * half)):
            total = own_core[part, rows].astype(jnp.float32) + arrived[part, rows].astype(jnp.float32)
            parts.append((total + extra[rows].astype(jnp.float32)).astype(jnp.bfloat16))
    return parts


def join_kernel(first_ref, from_y_ref, last_ref, from_x_ref, out_ref):
    half = first_ref.shape[0]
    out_ref[:half] = add_low(first_ref[...], from_y_ref[...])
    out_ref[half:] = add_low(last_ref[...], from_x_ref[...])


def reduce_home(first, from_y, last, from_x):
    half, width = first.shape
    half_spec = pl.BlockSpec((half, width), lambda j: (0, 0))
    return pl.pallas_call(
        join_kernel,
        grid=(1,),
        in_specs=[half_spec] * 4,
        out_specs=pl.BlockSpec((2 * half, width), lambda j: (0, 0)),
        out_shape=jax.ShapeDtypeStruct((2 * half, width), first.dtype),
        name="join_halves",
    )(first, from_y, last, from_x)


def butterfly_sum(value):
    value = value + swap_core(value)
    value = value + swap_x(value)
    value = value + swap_y(value)
    value = value + shift_z(value, 2)
    owners = lax.axis_size("ep")
    return value + lax.ppermute(value, "ep", [(i, i ^ 2) for i in range(owners)])


def planes_of(boxes):
    planes = boxes.shape[0]
    plane = lax.axis_index("ep") // 2
    return [lax.dynamic_index_in_dim(boxes, (plane + i) % planes, 0, keepdims=False) for i in range(planes)]


def send_planes(parts):
    return [shift_z(part.astype(jnp.bfloat16), i) for i, part in enumerate(parts) if i]


def add_all(first, others):
    return first.astype(jnp.float32) + sum(part.astype(jnp.float32) for part in others)


def spread_planes(value):
    planes = lax.axis_size("ep") // 2
    return [value] + [shift_z(value, i) for i in range(1, planes)]


def join_planes(parts):
    planes, plane = len(parts), lax.axis_index("ep") // 2
    full = jnp.zeros((planes,) + parts[0].shape, parts[0].dtype)
    for i, part in enumerate(parts):
        full = lax.dynamic_update_index_in_dim(full, part, (plane - i) % planes, 0)
    return full


def sides_of(boxes):
    y = lax.axis_index("ep") % 2
    return [lax.dynamic_index_in_dim(boxes, i, 0, keepdims=False) for i in (y, 1 - y)]


def join_sides(own, other):
    y = lax.axis_index("ep") % 2
    full = jnp.zeros((2,) + own.shape, own.dtype)
    full = lax.dynamic_update_index_in_dim(full, own, y, 0)
    return lax.dynamic_update_index_in_dim(full, other, 1 - y, 0)


FIRST_HALF = ((0, 0), (2, 0), (0, 1), (2, 1))
LAST_HALF = ((1, 0), (1, 1), (3, 0), (3, 1))
NT = (((1,), (1,)), ((), ()))
TN = (((0,), (0,)), ((), ()))


def dot_f32(left, right, dims=None):
    if dims is None:
        return jnp.dot(left, right, preferred_element_type=jnp.float32)
    return lax.dot_general(left, right, dims, preferred_element_type=jnp.float32)


def choose(index, values):
    out = values[0]
    for i in range(1, len(values)):
        out = jnp.where(index == i, values[i], out)
    return out


def expert_kernel(sizes, *refs):
    experts, slots, blocks, rows, routed = sizes
    x_parts, g_ref = refs[:8], refs[8]
    base_ref, order_ref, router_ref, gate_ref, up_ref, down_ref = refs[9:15]
    own_ref, keep_ref, send_ref, xr_out, gr_out, dgu_ref, wh_ref, rg_ref = refs[15:23]
    xs, gs, xr, gr, wgu, wd, back, picks, probs, weight, d_weight, table, leaving, tables = refs[23:37]
    x_sem, g_sem, w_sem, out_sem, leave_sem, t_sem = refs[37:43]
    width = xs.shape[1]
    units = wd.shape[1]
    total = experts * slots
    depth = blocks * slots
    def source_rows(b):
        return pl.ds(pl.multiple_of(order_ref[b] * rows, rows), rows)

    for b in range(blocks):
        pltpu.make_async_copy(x_parts[b], xs.at[pl.ds(b * rows, rows)], x_sem.at[b]).start()
        pltpu.make_async_copy(g_ref.at[source_rows(b), pl.ds(width, tables.shape[2])], tables.at[b], t_sem.at[b]).start()
    rg_ref[...] = jnp.zeros_like(rg_ref)

    def block_rows(b):
        return pl.ds(pl.multiple_of(b * rows, rows), rows)

    def slot_rows(b):
        return pl.ds(pl.multiple_of(b * slots, slots), slots)

    def expand(values):
        return jnp.concatenate([jnp.broadcast_to(values[e], (slots, rows)) for e in range(experts)], axis=0)

    place = jnp.concatenate(
        [lax.broadcasted_iota(jnp.int32, (slots, rows), 0)] * experts, axis=0
    ).astype(jnp.float32)

    def gather_x(b, carry):
        pltpu.make_async_copy(xs.at[block_rows(b)], xs.at[block_rows(b)], x_sem.at[b]).wait()
        pltpu.make_async_copy(tables.at[b], tables.at[b], t_sem.at[b]).wait()
        pltpu.make_async_copy(g_ref.at[source_rows(b), pl.ds(0, width)], gs.at[block_rows(b)], g_sem.at[b]).start()

        @pl.when(b < experts)
        def _():
            pltpu.make_async_copy(gate_ref.at[b], wgu.at[b, :, pl.ds(0, units)], w_sem.at[0, b]).start()
            pltpu.make_async_copy(up_ref.at[b], wgu.at[b, :, pl.ds(units, units)], w_sem.at[1, b]).start()
            pltpu.make_async_copy(down_ref.at[b], wd.at[b], w_sem.at[2, b]).start()

        x_block = xs[block_rows(b), :]
        logits = dot_f32(router_ref[...], x_block, NT)
        lane = lax.broadcasted_iota(jnp.int32, logits.shape, 0)
        logits = jnp.where(lane < routed, logits, -1e30)
        expo = jnp.exp(logits - jnp.max(logits, axis=0, keepdims=True))
        prob = expo / jnp.sum(expo, axis=0, keepdims=True)
        probs[b] = prob
        table[...] = tables[b].astype(jnp.float32).T
        hit = expand([table[pl.ds(base_ref[0] + e, 1), :] for e in range(experts)]) == place
        prob_rows = expand([prob[e : e + 1, :] for e in range(experts)])
        chosen = jnp.sum(jnp.where(hit, prob_rows, 0.0), axis=1, keepdims=True)
        chosen = jnp.broadcast_to(chosen, (total, rows))
        one = hit.astype(jnp.float32).astype(jnp.bfloat16)
        picks[b] = one
        taken = dot_f32(one, x_block).astype(jnp.bfloat16)
        for e in range(experts):
            xr[e, slot_rows(b), :] = taken[e * slots : (e + 1) * slots]
            weight[e, slot_rows(b), :] = chosen[e * slots : (e + 1) * slots]
        back[b, pl.ds(total, router_ref.shape[0]), :width] = router_ref[...]
        back[b, pl.ds(total, router_ref.shape[0]), width:] = jnp.zeros_like(router_ref)
        return carry

    def gather_g(b, carry):
        pltpu.make_async_copy(gs.at[block_rows(b)], gs.at[block_rows(b)], g_sem.at[b]).wait()
        taken = dot_f32(picks[b], gs[block_rows(b), :]).astype(jnp.bfloat16)
        for e in range(experts):
            gr[e, slot_rows(b), :] = taken[e * slots : (e + 1) * slots]
        return carry

    lax.fori_loop(0, blocks, gather_x, 0)
    pltpu.make_async_copy(xr, xr_out, out_sem.at[0]).start()
    lax.fori_loop(0, blocks, gather_g, 0)
    pltpu.make_async_copy(gr, gr_out, out_sem.at[1]).start()

    def one_expert(e, carry):
        low, high = pl.ds(0, units), pl.ds(units, units)
        pltpu.make_async_copy(wgu.at[e, :, low], wgu.at[e, :, low], w_sem.at[0, e]).wait()
        pltpu.make_async_copy(wgu.at[e, :, high], wgu.at[e, :, high], w_sem.at[1, e]).wait()
        pltpu.make_async_copy(wd.at[e], wd.at[e], w_sem.at[2, e]).wait()
        both = dot_f32(xr[e], wgu[e])
        gate, up = both[:, :units], both[:, units:]
        back_hidden = dot_f32(gr[e], wd[e], NT)
        sig = 1.0 / (1.0 + jnp.exp(-gate))
        silu = gate * sig
        hidden = silu * up
        product = hidden.astype(jnp.bfloat16).astype(jnp.float32) * back_hidden
        d_weight[e] = jnp.broadcast_to(jnp.sum(product, axis=1, keepdims=True), (depth, rows))
        share = weight[e]
        d_hidden = share * back_hidden
        d_gate = d_hidden * up * (sig * (1.0 + gate * (1.0 - sig)))
        d_up = d_hidden * silu
        d_both = jnp.concatenate([d_gate, d_up], axis=1).astype(jnp.bfloat16)
        dgu_ref[e] = d_both
        weighted = (share * hidden).astype(jnp.bfloat16)
        wh_ref[e] = weighted
        d_rows = dot_f32(d_both, wgu[e], NT).astype(jnp.bfloat16)
        for b in range(blocks):
            back[b, slot_rows(e), :width] = d_rows[b * slots : (b + 1) * slots]
        out_rows = dot_f32(weighted, wd[e]).astype(jnp.bfloat16)
        for b in range(blocks):
            back[b, slot_rows(e), width:] = out_rows[b * slots : (b + 1) * slots]
        return carry

    lax.fori_loop(0, experts, one_expert, 0)

    half = rows // 2

    def left(turn):
        pltpu.make_async_copy(leaving.at[turn], leaving.at[turn], leave_sem.at[turn]).wait()

    def scatter(b, carry):
        one = picks[b]
        d_slot = jnp.concatenate([d_weight[e, slot_rows(b), :] for e in range(experts)], axis=0)
        spread = one.astype(jnp.float32) * d_slot
        d_prob = jnp.concatenate(
            [jnp.sum(spread[e * slots : (e + 1) * slots], axis=0, keepdims=True) for e in range(experts)]
            + [jnp.zeros((router_ref.shape[0] - experts, rows), jnp.float32)],
            axis=0,
        )
        prob = probs[b]
        centre = jnp.sum(prob * d_prob, axis=0, keepdims=True)
        d_logits = (prob * (d_prob - centre)).astype(jnp.bfloat16)
        rg_ref[...] += dot_f32(d_logits, xs[block_rows(b), :])
        turn = b % 2

        @pl.when(b >= 2)
        def _():
            left(turn)

        leaving[turn] = dot_f32(jnp.concatenate([one, d_logits], axis=0), back[b], TN).astype(jnp.bfloat16)
        for i, table_of in enumerate((FIRST_HALF, LAST_HALF)):
            part = choose(b % 4, [place[0] for place in table_of])
            row = choose(b % 4, [place[1] for place in table_of]) * half
            place_rows = pl.ds(pl.multiple_of(row, half), half)
            for ref, index, mine in (
                (own_ref, part, b < 4),
                (keep_ref, part, (b >= 4) & (part < 2)),
                (send_ref, part - 2, (b >= 4) & (part >= 2)),
            ):

                @pl.when(mine)
                def _(ref=ref, index=index, place_rows=place_rows, i=i):
                    pltpu.make_async_copy(
                        leaving.at[turn, pl.ds(i * half, half)], ref.at[index, place_rows], leave_sem.at[turn]
                    ).start()

        return carry

    lax.fori_loop(0, blocks, scatter, 0)
    left(0)
    left(1)
    pltpu.make_async_copy(xr, xr_out, out_sem.at[0]).wait()
    pltpu.make_async_copy(gr, gr_out, out_sem.at[1]).wait()


def expert_call(x_parts, g_all, base, order, router_rows, gate_weight, up_weight, down_weight, routed, slots):
    blocks = len(x_parts)
    rows, width = x_parts[0].shape
    experts, _, units = gate_weight.shape
    depth = blocks * slots
    padded = router_rows.shape[0]
    extra = g_all.shape[1] - width
    low, full = jnp.bfloat16, jnp.float32
    any_spec = pl.BlockSpec(memory_space=pl.ANY)
    vmem_spec = pl.BlockSpec(memory_space=pltpu.VMEM)
    smem_spec = pl.BlockSpec(memory_space=pltpu.SMEM)
    return pl.pallas_call(
        lambda *refs: expert_kernel((experts, slots, blocks, rows, routed), *refs),
        out_shape=(
            jax.ShapeDtypeStruct((4, rows, 2 * width), low),
            jax.ShapeDtypeStruct((2, rows, 2 * width), low),
            jax.ShapeDtypeStruct((2, rows, 2 * width), low),
            jax.ShapeDtypeStruct((experts, depth, width), low),
            jax.ShapeDtypeStruct((experts, depth, width), low),
            jax.ShapeDtypeStruct((experts, depth, 2 * units), low),
            jax.ShapeDtypeStruct((experts, depth, units), low),
            jax.ShapeDtypeStruct((padded, width), full),
        ),
        in_specs=[any_spec] * 9 + [smem_spec, smem_spec, vmem_spec] + [any_spec] * 3,
        out_specs=(any_spec,) * 5 + (vmem_spec,) * 3,
        scratch_shapes=[
            pltpu.VMEM((blocks * rows, width), low),
            pltpu.VMEM((blocks * rows, width), low),
            pltpu.VMEM((experts, depth, width), low),
            pltpu.VMEM((experts, depth, width), low),
            pltpu.VMEM((experts, width, 2 * units), low),
            pltpu.VMEM((experts, units, width), low),
            pltpu.VMEM((blocks, experts * slots + padded, 2 * width), low),
            pltpu.VMEM((blocks, experts * slots, rows), low),
            pltpu.VMEM((blocks, padded, rows), full),
            pltpu.VMEM((experts, depth, rows), full),
            pltpu.VMEM((experts, depth, rows), full),
            pltpu.VMEM((extra, rows), full),
            pltpu.VMEM((2, rows, 2 * width), low),
            pltpu.VMEM((blocks, rows, extra), low),
            pltpu.SemaphoreType.DMA((blocks,)),
            pltpu.SemaphoreType.DMA((blocks,)),
            pltpu.SemaphoreType.DMA((3, experts)),
            pltpu.SemaphoreType.DMA((2,)),
            pltpu.SemaphoreType.DMA((2,)),
            pltpu.SemaphoreType.DMA((blocks,)),
        ],
        compiler_params=pltpu.CompilerParams(vmem_limit_bytes=58 * 2**20),
        cost_estimate=pl.CostEstimate(
            flops=2 * experts * depth * width * units * 40, bytes_accessed=60 * 2**20, transcendentals=0
        ),
        name="expert_chunk",
    )(*x_parts, g_all, base, order, router_rows, gate_weight, up_weight, down_weight)


def weight_kernel(count, *refs):
    xr, gr, dgu, wh = (refs[i * count : (i + 1) * count] for i in range(4))
    gate_ref, up_ref, down_ref = refs[4 * count :]
    units = gate_ref.shape[2]
    both = sum(dot_f32(x[0], d[0], TN) for x, d in zip(xr, dgu))
    gate_ref[0] = both[:, :units]
    up_ref[0] = both[:, units:]
    down_ref[0] = sum(dot_f32(h[0], g[0], TN) for h, g in zip(wh, gr))


def weight_call(xr, gr, dgu, wh):
    count = len(xr)
    experts, depth, width = xr[0].shape
    units = wh[0].shape[2]
    spec = lambda array: pl.BlockSpec((1,) + array.shape[1:], lambda e: (e, 0, 0))
    operands = [*xr, *gr, *dgu, *wh]
    up_like = jax.ShapeDtypeStruct((experts, width, units), jnp.float32)
    down_like = jax.ShapeDtypeStruct((experts, units, width), jnp.float32)
    return pl.pallas_call(
        lambda *refs: weight_kernel(count, *refs),
        grid=(experts,),
        out_shape=(up_like, up_like, down_like),
        in_specs=[spec(a) for a in operands],
        out_specs=(spec(up_like), spec(up_like), spec(down_like)),
        compiler_params=pltpu.CompilerParams(vmem_limit_bytes=50 * 2**20),
        cost_estimate=pl.CostEstimate(
            flops=2 * experts * depth * count * width * units * 3,
            bytes_accessed=60 * 2**20,
            transcendentals=0,
        ),
        name="expert_weights",
    )(*operands)


def swap_halves(values, half):
    lane = lax.broadcasted_iota(jnp.int32, values.shape, 1)
    size = values.shape[1]
    return jnp.where(
        lane % (2 * half) < half, pltpu.roll(values, size - half, 1), pltpu.roll(values, half, 1)
    )


def branch_back_kernel(*refs):
    parts, me_ref, att_ref, wo_ref, back_ref, out_ref, branch, sem = refs[:4], *refs[4:]
    rows = parts[0].shape[0]
    for flip, part in enumerate(parts):
        target = pl.ds(pl.multiple_of((me_ref[0] ^ flip) * rows, rows), rows)
        pltpu.make_async_copy(part, branch.at[target], sem.at[flip]).start()
    for flip, part in enumerate(parts):
        target = pl.ds(pl.multiple_of((me_ref[0] ^ flip) * rows, rows), rows)
        pltpu.make_async_copy(part, branch.at[target], sem.at[flip]).wait()
    out_part = dot_f32(att_ref[...], branch[...], TN).astype(jnp.bfloat16)
    _, planes, size, _ = out_ref.shape
    for i in range(2 * planes):
        out_ref[me_ref[1] ^ (i // planes), i % planes] = out_part[i * size : (i + 1) * size]
    back_ref[...] = dot_f32(branch[...], wo_ref[...], NT).astype(jnp.bfloat16)


def branch_back_call(parts, attended, wo):
    rows, width = parts[0].shape
    seq_len, q_width = attended.shape
    planes = lax.axis_size("ep") // 2
    me = jnp.stack([lax.axis_index("tp"), lax.axis_index("ep") % 2]).astype(jnp.int32)
    vmem_spec = pl.BlockSpec(memory_space=pltpu.VMEM)
    return pl.pallas_call(
        branch_back_kernel,
        out_shape=(
            jax.ShapeDtypeStruct((seq_len, q_width), jnp.bfloat16),
            jax.ShapeDtypeStruct((2, planes, q_width // planes // 2, width), jnp.bfloat16),
        ),
        in_specs=[pl.BlockSpec(memory_space=pl.ANY)] * 4 + [pl.BlockSpec(memory_space=pltpu.SMEM)] + [vmem_spec] * 2,
        out_specs=(vmem_spec,) * 2,
        scratch_shapes=[pltpu.VMEM((seq_len, width), jnp.bfloat16), pltpu.SemaphoreType.DMA((4,))],
        compiler_params=pltpu.CompilerParams(vmem_limit_bytes=24 * 2**20),
        cost_estimate=pl.CostEstimate(
            flops=4 * seq_len * width * q_width, bytes_accessed=8 * 2**20, transcendentals=0
        ),
        name="branch_back",
    )(*parts, me, attended, wo)


def attention_back_kernel(sizes, *refs):
    group_factor, head_size = sizes
    me_ref, back, q_ref, k_ref, v_ref, normed_ref, wq_ref, wk_ref, wv_ref = refs[:9]
    cos_ref, sin_ref, column_ref, row_ref, live_ref = refs[9:14]
    weights_ref, stay_ref, leave_ref = refs[14:17]
    d_q, d_k, d_v, d_all = refs[17:21]
    seq_len = q_ref.shape[0]
    rows = stay_ref.shape[1]
    factor = 1.0 / math.sqrt(head_size)
    me = me_ref[0]

    def place(flip):
        return pl.ds(pl.multiple_of((me ^ flip) * rows, rows), rows)

    d_k[...] = jnp.zeros_like(d_k)
    d_v[...] = jnp.zeros_like(d_v)
    step = seq_len // 2
    for start in (0, step):
        keys = start + step
        shape = (step, keys)
        query_place = start + lax.broadcasted_iota(jnp.int32, shape, 0)
        key_place = lax.broadcasted_iota(jnp.int32, shape, 1)
        same = column_ref[start : start + step, :] == row_ref[:, :keys]
        usable = (live_ref[:, :keys] > 0) | (key_place == query_place)
        allowed = same & (key_place <= query_place) & usable
        for head in range(q_ref.shape[1] // head_size):
            group = head // group_factor
            mine = slice(head * head_size, (head + 1) * head_size)
            shared = slice(group * head_size, (group + 1) * head_size)
            query = q_ref[start : start + step, mine]
            key, value = k_ref[:keys, shared], v_ref[:keys, shared]
            d_out = back[start : start + step, mine]
            scores = jnp.where(allowed, dot_f32(query, key, NT) * factor, -1e30)
            expo = jnp.exp(scores - jnp.max(scores, axis=1, keepdims=True))
            probs = expo * (1.0 / jnp.sum(expo, axis=1, keepdims=True))
            d_probs = dot_f32(d_out, value, NT)
            centre = jnp.sum(probs * d_probs, axis=1, keepdims=True)
            d_scores = (probs * (d_probs - centre)).astype(jnp.bfloat16)
            d_q[start : start + step, mine] = dot_f32(d_scores, key) * factor
            d_k[:keys, shared] += dot_f32(d_scores, query, TN) * factor
            d_v[:keys, shared] += dot_f32(probs.astype(jnp.bfloat16), d_out, TN)
    pair = 2 * head_size
    q_width = q_ref.shape[1]
    kv_width = k_ref.shape[1]
    for source, count, offset in ((d_q, q_width // pair, 0), (d_k, kv_width // pair, q_width)):
        for i in range(count):
            turned = source[:, i * pair : (i + 1) * pair]
            flat = turned * cos_ref[...] + swap_halves(turned, head_size // 2) * sin_ref[...]
            d_all[:, offset + i * pair : offset + (i + 1) * pair] = flat.astype(jnp.bfloat16)
    d_all[:, q_width + kv_width :] = d_v[...].astype(jnp.bfloat16)
    size = weights_ref.shape[1] // 6
    for i in range(12):
        part = dot_f32(normed_ref[:, i * size : (i + 1) * size], d_all[...], TN).astype(jnp.bfloat16)
        weights_ref[me_ref[1] ^ (i // 6), i % 6 * size : (i % 6 + 1) * size] = part
    for flip in range(4):
        values = d_all[place(flip), :]
        total = dot_f32(values[:, :q_width], wq_ref[...], NT)
        total += dot_f32(values[:, q_width : q_width + kv_width], wk_ref[...], NT)
        total += dot_f32(values[:, q_width + kv_width :], wv_ref[...], NT)
        if flip % 2:
            leave_ref[flip // 2] = total.astype(jnp.bfloat16)
        else:
            stay_ref[flip // 2] = total


def attention_back_call(back, query, key, value, normed, wq, wk, wv, cos, sin, segments, live, factor):
    seq_len, q_width = query.shape
    width, kv_width = wk.shape
    rows = seq_len // 4
    me = jnp.stack([lax.axis_index("tp"), lax.axis_index("ep") % 2]).astype(jnp.int32)
    low, full = jnp.bfloat16, jnp.float32
    vmem_spec = pl.BlockSpec(memory_space=pltpu.VMEM)
    cos_pair = jnp.tile(cos, (1, 4))
    sin_pair = jnp.tile(jnp.concatenate([sin, -sin], axis=1), (1, 2))
    return pl.pallas_call(
        lambda *refs: attention_back_kernel((factor, HEAD_SIZE_DIM), *refs),
        out_shape=(
            jax.ShapeDtypeStruct((2, width // 2, q_width + 2 * kv_width), low),
            jax.ShapeDtypeStruct((2, rows, width), full),
            jax.ShapeDtypeStruct((2, rows, width), low),
        ),
        in_specs=[pl.BlockSpec(memory_space=pltpu.SMEM)] + [vmem_spec] * 13,
        out_specs=(vmem_spec,) * 3,
        scratch_shapes=[
            pltpu.VMEM((seq_len, q_width), full),
            pltpu.VMEM((seq_len, kv_width), full),
            pltpu.VMEM((seq_len, kv_width), full),
            pltpu.VMEM((seq_len, q_width + 2 * kv_width), low),
        ],
        compiler_params=pltpu.CompilerParams(vmem_limit_bytes=48 * 2**20),
        cost_estimate=pl.CostEstimate(
            flops=2 * seq_len * width * (2 * q_width + 4 * kv_width) * 2 * 6,
            bytes_accessed=60 * 2**20,
            transcendentals=0,
        ),
        name="attention_back",
    )(
        me, back, query, key, value, normed, wq, wk, wv, cos_pair, sin_pair,
        segments.reshape(-1, 1), segments.reshape(1, -1), live.reshape(1, -1),
    )


def local_gathered(
    tokens,
    norm_gain,
    query_matrix,
    key_matrix,
    value_matrix,
    out_weight,
    moe_gain,
    router_weight,
    gate_weight,
    up_weight,
    down_weight,
    cotangent,
    expert_ids,
    segments,
    valid_mask,
):
    quarter = tokens.shape[0]
    width = tokens.shape[1]
    groups = lax.axis_size("tp")
    owners = lax.axis_size("ep")
    my_part = lax.axis_index("tp")
    seq_len = quarter * groups
    head_size = HEAD_SIZE_DIM
    kv_heads = key_matrix.shape[1] // head_size
    q_heads = query_matrix.shape[1] // head_size
    group_factor = q_heads // kv_heads
    local_experts = gate_weight.shape[0]
    experts_all = router_weight.shape[1]
    chosen_count = expert_ids.shape[1]
    slots = max(8, 3 * quarter * chosen_count // (2 * experts_all) // 8 * 8)
    factor = 1.0 / math.sqrt(head_size)
    segment_row = segments[0]
    live_row = valid_mask[0]
    x_float = tokens.astype(jnp.float32)
    planes = owners // 2
    owner = lax.axis_index("ep")
    my_valid = lax.dynamic_slice_in_dim(live_row, my_part * quarter, quarter, 0)
    padded = -(-experts_all // 16) * 16
    named = jnp.any(expert_ids[:, :, None] == jnp.arange(padded)[None, None, :], axis=1) & (my_valid[:, None] > 0)
    before = (jnp.arange(quarter)[None, :] < jnp.arange(quarter)[:, None]).astype(jnp.bfloat16)
    earlier = jnp.dot(before, named.astype(jnp.bfloat16), preferred_element_type=jnp.float32)
    slot = jnp.where(named, earlier, -1.0).astype(jnp.bfloat16)
    slot = jnp.pad(slot, ((0, 0), (0, -padded % 128)), constant_values=-1.0)
    sent = jnp.concatenate([cotangent, slot], axis=1)
    g_all = lax.all_gather(sent, ("ep", "tp"), axis=0, tiled=True)
    router_rows = jnp.roll(router_weight.T, -owner * local_experts, axis=0)
    router_rows = jnp.pad(router_rows, ((0, padded - experts_all), (0, 0)))
    base = (owner * local_experts).astype(jnp.int32)[None]
    step = jnp.arange(planes)[:, None]
    flip_y = jnp.array([0, 0, 1, 1, 0, 0, 1, 1])[None, :]
    flip_tp = jnp.array([0, 2, 0, 2, 1, 3, 1, 3])[None, :]
    order = (((owner // 2 - step) % planes) * 2 + (owner % 2 ^ flip_y)) * 4 + (my_part ^ flip_tp)
    order = order.astype(jnp.int32)
    tokens_all = gather_tp(tokens)
    normed_all = rms_norm(tokens_all.astype(jnp.float32), norm_gain).astype(jnp.bfloat16)
    query_unrotated = jnp.dot(normed_all, query_matrix, preferred_element_type=jnp.float32).reshape(
        seq_len, kv_heads, group_factor, head_size
    )
    key_unrotated = jnp.dot(normed_all, key_matrix, preferred_element_type=jnp.float32).reshape(
        seq_len, kv_heads, head_size
    )
    value_vectors = (
        jnp.dot(normed_all, value_matrix, preferred_element_type=jnp.float32)
        .astype(jnp.bfloat16)
        .reshape(seq_len, kv_heads, head_size)
    )
    cos_table, sin_table = angle_tables(seq_len, head_size)
    cos_query = cos_table[:, None, None, :]
    sin_query = sin_table[:, None, None, :]
    cos_key = cos_table[:, None, :]
    sin_key = sin_table[:, None, :]
    query_val = rotate(query_unrotated, cos_query, sin_query).astype(jnp.bfloat16)
    key_val = rotate(key_unrotated, cos_key, sin_key).astype(jnp.bfloat16)
    height = min(512, seq_len)
    offset = 0
    allowed = block_mask(segment_row, live_row, offset, height)
    scores = block_scores(query_val, key_val, allowed, factor)
    peak = jnp.max(scores, axis=-1, keepdims=True)
    expo = jnp.exp(scores - peak)
    denom = jnp.sum(expo, axis=-1, keepdims=True)
    weights = (expo / denom).astype(jnp.bfloat16)
    mixed = jnp.einsum("grqk,kgd->qgrd", weights, value_vectors, preferred_element_type=jnp.float32)
    outputs = mixed.reshape(height, q_heads * head_size)
    log_sums = [peak + jnp.log(denom)]
    attended = outputs.astype(jnp.bfloat16)
    branch, _ = scatter_tp(
        jnp.dot(attended, out_weight, preferred_element_type=jnp.float32), jnp.float32
    )
    middle = x_float + branch
    moe_in = rms_norm(middle, moe_gain).astype(jnp.bfloat16)
    barrier = lax.optimization_barrier
    columns, cross, diagonal, swapped, far = [moe_in], {}, {}, {}, {}

    def send_cross(step):
        cross[step] = (swap_x(columns[step]), swap_y(columns[step]))

    def send_diagonal(step):
        diagonal[step] = swap_x(cross[step][1]) if step % 2 else swap_y(cross[step][0])

    def send_swapped(step):
        swapped[step] = tuple(swap_core(part) for part in (columns[step], *cross[step]))

    send_cross(0)
    columns.append(shift_z(columns[0], 1))
    columns[1], cross = barrier((columns[1], cross))
    send_cross(1)
    columns.append(shift_z(columns[1], 1))
    columns[2], cross = barrier((columns[2], cross))
    send_diagonal(1)
    send_swapped(1)
    send_cross(2)
    columns.append(shift_z(columns[2], 1))
    columns[3], cross, diagonal, swapped = barrier((columns[3], cross, diagonal, swapped))
    far[1] = swap_core(diagonal[1])
    turns = [*range(1, planes), 0]
    kept, grad_parts = [], []
    own, keep, send, arrived, from_x, from_y, halves, second = {}, {}, {}, {}, {}, {}, {}, {}
    for stage in range(planes + 3):
        ready, sends, joined = [], None, None
        a, b, c = stage - 1, stage - 2, stage - 3
        if a in send:
            sends = reduce_sends(own[a], swap_core(send[a]))
            ready += sends
            if stage >= 3:
                arrived[a] = swap_core(keep[a])
                ready += [arrived[a]]
        if b in from_x:
            halves[b] = reduce_second((own[b], arrived[b]), from_x[b], from_y[b])
            ready += halves[b]
        if c in second:
            joined = reduce_home(halves[c][0], second[c][0], halves[c][2], second[c][1])
            ready += [joined]
            if turns[c] == 0:
                grad_parts.append(joined)
                joined = None
        came = {}
        if stage < planes:
            step = turns[stage]
            x_parts = (columns[step], *cross[step], diagonal[step], *swapped[step], far[step])
            if stage == 0:
                send_diagonal(2)
                send_cross(3)
                send_swapped(2)
                came["gather"] = (diagonal[2], cross[3], swapped[2])
            if stage == 1:
                send_diagonal(3)
                send_diagonal(0)
                send_swapped(3)
                came["gather"] = (diagonal[3], diagonal[0], swapped[3])
            if stage == 2:
                send_swapped(0)
                came["gather"] = (swapped[0],)
            own[stage], keep[stage], send[stage], *rest = expert_call(
                x_parts, g_all, base, order[step], after(router_rows, *ready),
                gate_weight, up_weight, down_weight, experts_all, slots,
            )
            kept.append(rest)
            came["kernel"] = (own[stage], keep[stage], send[stage])
        if stage == planes:
            xr, gr, dgu, wh, router_parts = zip(*kept)
            came["weights"] = weight_call(xr, gr, (after(dgu[0], *ready),) + dgu[1:], wh)
        if sends:
            if stage < 3:
                came["core"] = swap_core(keep[a])
            came["cross"] = (swap_x(sends[0]), swap_y(sends[1]))
        if b in halves:
            came["second"] = (swap_y(halves[b][1]), swap_x(halves[b][3]))
        if joined is not None:
            came["home"] = shift_z(joined, -turns[c])
        came = barrier(came)
        if stage == 0:
            diagonal[2], cross[3], swapped[2] = came["gather"]
            far[2] = swap_core(diagonal[2])
        if stage == 1:
            diagonal[3], diagonal[0], swapped[3] = came["gather"]
            far[3], far[0] = swap_core(diagonal[3]), swap_core(diagonal[0])
        if stage == 2:
            (swapped[0],) = came["gather"]
        if "kernel" in came:
            own[stage], keep[stage], send[stage] = came["kernel"]
        if "weights" in came:
            gate_grad, up_grad, down_grad = came["weights"]
        if "core" in came:
            arrived[a] = came["core"]
        if "cross" in came:
            from_x[a], from_y[a] = came["cross"]
        if "second" in came:
            second[b] = came["second"]
        if "home" in came:
            grad_parts.append(came["home"])
    grad_moe_in = sum(part[:, :width].astype(jnp.float32) for part in grad_parts)
    expert_sum = sum(part[:, width:].astype(jnp.float32) for part in grad_parts)
    output = (middle + expert_sum).astype(jnp.bfloat16)
    router_part = jnp.roll(sum(router_parts)[:experts_all], owner * local_experts, axis=0)
    grad_out = cotangent.astype(jnp.float32)
    _, norm_two_back = jax.vjp(rms_norm, middle, moe_gain)
    grad_mid_norm, moe_gain_grad = norm_two_back(grad_moe_in)
    grad_middle = grad_out + grad_mid_norm
    branch_parts = gather_pieces(grad_middle.astype(jnp.bfloat16))
    flat = lambda array: array.reshape(seq_len, -1)
    back, out_grad = branch_back_call(branch_parts, attended, out_weight)
    out_came = swap_y(out_grad[1])
    weights, stay, leave = attention_back_call(
        back, flat(query_val), flat(key_val), flat(value_vectors), normed_all,
        query_matrix, key_matrix, value_matrix, cos_table, sin_table, segment_row, live_row, group_factor,
    )
    weights, stay, leave, out_came = barrier((weights, stay, leave, out_came))
    weights = weights.reshape(2, planes, -1, weights.shape[-1])
    weights_came = swap_y(weights[1])
    out_parts = planes_of(add_low(out_grad[0], out_came))
    out_came = send_planes(out_parts)
    both = stay + swap_core(leave).astype(jnp.float32)
    out_came, both = barrier((out_came, both))
    across_came = swap_x(both[1].astype(jnp.bfloat16))
    out_sum = add_all(out_parts[0], out_came).astype(jnp.bfloat16)
    out_came = spread_planes(out_sum)
    weights_came, across_came, out_came = barrier((weights_came, across_came, out_came))
    weights_parts = planes_of(add_low(weights[0], weights_came))
    weights_came = send_planes(weights_parts)
    out_half = join_planes(out_came)
    out_came = swap_y(out_half)
    grad_normed = both[0] + across_came.astype(jnp.float32)
    _, norm_one_back = jax.vjp(rms_norm, x_float, norm_gain)
    grad_x_norm, norm_gain_grad = norm_one_back(grad_normed)
    input_grad = grad_middle + grad_x_norm
    small = jnp.concatenate([router_part, moe_gain_grad[None], norm_gain_grad[None]], axis=0)
    small = small + swap_core(small)
    small_came = swap_x(small)
    weights_came, small_came, out_came = barrier((weights_came, small_came, out_came))
    small = small + small_came
    small_came = swap_y(small)
    weights_sum = add_all(weights_parts[0], weights_came).astype(jnp.bfloat16)
    weights_came = spread_planes(weights_sum)
    weights_came, small_came = barrier((weights_came, small_came))
    small = small + small_came
    weights_half = join_planes(weights_came)
    weights_came = swap_y(weights_half)
    small_came = send_planes([small] * planes)
    weights_came, small_came = barrier((weights_came, small_came))
    small = add_all(small, small_came)
    out_grad = join_sides(out_half, out_came).reshape(-1, width).astype(jnp.float32)
    weights = join_sides(weights_half, weights_came).reshape(width, -1).astype(jnp.float32)
    q_width, kv_width = query_matrix.shape[1], key_matrix.shape[1]
    query_grad, key_grad, value_grad = jnp.split(weights, (q_width, q_width + kv_width), axis=1)
    router_grad, moe_gain_grad, norm_gain_grad = small[:experts_all].T, small[experts_all], small[experts_all + 1]
    return (
        output,
        input_grad,
        norm_gain_grad,
        query_grad,
        key_grad,
        value_grad,
        out_grad,
        moe_gain_grad,
        router_grad,
        gate_grad,
        up_grad,
        down_grad,
    )


def local(*operands):
    tokens, router_weight, gate_weight, expert_ids = operands[0], operands[7], operands[8], operands[12]
    quarter, experts_all = tokens.shape[0], router_weight.shape[1]
    slots = max(8, 3 * quarter * expert_ids.shape[1] // (2 * experts_all) // 8 * 8)
    gathers = lax.axis_size("tp") == 4 and lax.axis_size("ep") == 8 and gate_weight.shape[0] * slots >= quarter
    return (local_gathered if gathers else local_routed)(*operands)


def solution(mesh):
    in_specs = (
        P(("ep", "tp"), None),
        P(),
        P(None, "tp"),
        P(None, "tp"),
        P(None, "tp"),
        P("tp", None),
        P(),
        P(),
        P("ep", None, "tp"),
        P("ep", None, "tp"),
        P("ep", "tp", None),
        P(("ep", "tp"), None),
        P(("ep", "tp"), None),
        P("ep", None),
        P("ep", None),
    )
    out_specs = (
        P(("ep", "tp"), None),
        P(("ep", "tp"), None),
        P(),
        P(None, "tp"),
        P(None, "tp"),
        P(None, "tp"),
        P("tp", None),
        P(),
        P(),
        P("ep", None, "tp"),
        P("ep", None, "tp"),
        P("ep", "tp", None),
    )
    return jax.shard_map(local, mesh=mesh, in_specs=in_specs, out_specs=out_specs, check_vma=False)
```

```python
import math

import jax
import jax.numpy as jnp
from jax import lax
from jax.experimental import pallas as pl
from jax.experimental.pallas import tpu as pltpu
from jax.sharding import PartitionSpec as P

HEAD_SIZE_DIM = 64


EPS = 1e-06
HIGH_PRECISION = lax.Precision.HIGHEST


def rms_norm(activation, gain_vec):
    factor = lax.rsqrt(jnp.mean(activation * activation, axis=-1, keepdims=True) + EPS)
    return activation * factor * gain_vec


def rotate(vectors, cos_table, sin_table):
    half_size = vectors.shape[-1] // 2
    first_half = vectors[..., :half_size]
    second_half = vectors[..., half_size:]
    return jnp.concatenate(
        [
            first_half * cos_table - second_half * sin_table,
            second_half * cos_table + first_half * sin_table,
        ],
        axis=-1,
    )


def angle_tables(span_length, head_size):
    half_size = head_size // 2
    inverse = jnp.exp(
        -math.log(10000.0) * jnp.arange(half_size, dtype=jnp.float32) * 2.0 / head_size
    )
    angles = jnp.arange(span_length, dtype=jnp.float32)[:, None] * inverse[None, :]
    return (jnp.cos(angles), jnp.sin(angles))


def swiglu(gate_val, up_val):
    return jax.nn.silu(gate_val) * up_val


def softmax_rows(logits):
    return jax.nn.softmax(logits, axis=-1)


def block_mask(segment_row, live_row, offset, height):
    span_length = segment_row.shape[0]
    key_places = jnp.arange(span_length)
    query_places = offset + jnp.arange(height)
    same_doc = segment_row[:, None] == segment_row[None, :]
    causal = key_places[None, :] <= query_places[:, None]
    usable = (live_row[None, :] > 0) | (key_places[None, :] == query_places[:, None])
    return same_doc & causal & usable


def block_scores(query_block, key_val, allowed, factor):
    scores = (
        jnp.einsum("qgrd,kgd->grqk", query_block, key_val, preferred_element_type=jnp.float32)
        * factor
    )
    return jnp.where(allowed[None, None], scores, -1e30)


def group_rows(boxes):
    return lax.all_gather(boxes, "tp", axis=0, tiled=True)


def dispatch_rows(boxes):
    return lax.all_to_all(boxes, "ep", split_axis=1, concat_axis=1, tiled=True)


def return_rows(boxes):
    return lax.all_to_all(boxes, "ep", split_axis=1, concat_axis=1, tiled=True)


def local_routed(
    tokens,
    norm_gain,
    query_matrix,
    key_matrix,
    value_matrix,
    out_weight,
    moe_gain,
    router_weight,
    gate_weight,
    up_weight,
    down_weight,
    cotangent,
    expert_ids,
    segments,
    valid_mask,
):
    quarter = tokens.shape[0]
    width = tokens.shape[1]
    groups = lax.axis_size("tp")
    owners = lax.axis_size("ep")
    my_part = lax.axis_index("tp")
    seq_len = quarter * groups
    head_size = HEAD_SIZE_DIM
    kv_heads = key_matrix.shape[1] // head_size
    q_heads = query_matrix.shape[1] // head_size
    group_factor = q_heads // kv_heads
    local_experts = gate_weight.shape[0]
    experts_all = router_weight.shape[1]
    chosen_count = expert_ids.shape[1]
    slots = max(8, 3 * quarter * chosen_count // (2 * experts_all) // 8 * 8)
    factor = 1.0 / math.sqrt(head_size)
    segment_row = segments[0]
    live_row = valid_mask[0]
    x_float = tokens.astype(jnp.float32)
    normed = rms_norm(x_float, norm_gain).astype(jnp.bfloat16)
    normed_all = lax.all_gather(normed, "tp", axis=0, tiled=True)
    query_unrotated = jnp.dot(normed_all, query_matrix, preferred_element_type=jnp.float32).reshape(
        seq_len, kv_heads, group_factor, head_size
    )
    key_unrotated = jnp.dot(normed_all, key_matrix, preferred_element_type=jnp.float32).reshape(
        seq_len, kv_heads, head_size
    )
    value_vectors = (
        jnp.dot(normed_all, value_matrix, preferred_element_type=jnp.float32)
        .astype(jnp.bfloat16)
        .reshape(seq_len, kv_heads, head_size)
    )
    cos_table, sin_table = angle_tables(seq_len, head_size)
    cos_query = cos_table[:, None, None, :]
    sin_query = sin_table[:, None, None, :]
    cos_key = cos_table[:, None, :]
    sin_key = sin_table[:, None, :]
    query_val = rotate(query_unrotated, cos_query, sin_query).astype(jnp.bfloat16)
    key_val = rotate(key_unrotated, cos_key, sin_key).astype(jnp.bfloat16)
    height = min(512, seq_len)
    offset = 0
    allowed = block_mask(segment_row, live_row, offset, height)
    scores = block_scores(query_val, key_val, allowed, factor)
    peak = jnp.max(scores, axis=-1, keepdims=True)
    expo = jnp.exp(scores - peak)
    denom = jnp.sum(expo, axis=-1, keepdims=True)
    weights = (expo / denom).astype(jnp.bfloat16)
    mixed = jnp.einsum("grqk,kgd->qgrd", weights, value_vectors, preferred_element_type=jnp.float32)
    outputs = mixed.reshape(height, q_heads * head_size)
    log_sums = [peak + jnp.log(denom)]
    attended = outputs.astype(jnp.bfloat16)
    branch = lax.psum_scatter(
        jnp.dot(attended, out_weight, preferred_element_type=jnp.float32),
        "tp",
        scatter_dimension=0,
        tiled=True,
    )
    middle = x_float + branch
    moe_in = rms_norm(middle, moe_gain).astype(jnp.bfloat16)
    logits = jnp.dot(moe_in, router_weight, preferred_element_type=jnp.float32)
    router = softmax_rows(logits)
    my_valid = lax.dynamic_slice_in_dim(live_row, my_part * quarter, quarter, 0)
    valid_float = my_valid.astype(jnp.float32)
    picked = jnp.take_along_axis(router, expert_ids, axis=1) * valid_float[:, None]
    flat_ids = expert_ids.reshape(-1)
    flat_live = jnp.repeat(my_valid, chosen_count)
    named = (expert_ids[:, :, None] == jnp.arange(experts_all)[None, None, :]).astype(jnp.float32)
    chosen = (jnp.sum(named, axis=1) * valid_float[:, None]).astype(jnp.bfloat16)
    before = (jnp.arange(quarter)[None, :] < jnp.arange(quarter)[:, None]).astype(jnp.bfloat16)
    earlier = jnp.dot(before, chosen, preferred_element_type=jnp.float32)
    slot_of = jnp.sum(named * earlier[:, None, :], axis=2).astype(jnp.int32).reshape(-1)
    target = jnp.where(flat_live > 0, flat_ids, experts_all)
    safe_target = jnp.minimum(target, experts_all - 1)

    def pack(row_block):
        boxes = jnp.zeros((experts_all, slots, width), jnp.bfloat16)
        boxes = boxes.at[target, slot_of].set(row_block, mode="drop")
        return boxes.reshape(1, owners, local_experts * slots, width)

    def unpack(boxes):
        flat_boxes = boxes.reshape(experts_all, slots, width)
        taken = flat_boxes[safe_target, slot_of]
        taken = jnp.where(flat_live[:, None] > 0, taken, jnp.zeros_like(taken))
        return taken.reshape(quarter, chosen_count, width)

    sent = pack(jnp.repeat(moe_in, chosen_count, axis=0))
    full_gate, full_up, full_down = (gate_weight, up_weight, down_weight)
    arrived = group_rows(dispatch_rows(sent))
    expert_rows = arrived.reshape(groups, owners, local_experts, slots, width)
    gate_val = jnp.einsum(
        "tsecd,edf->tsecf", expert_rows, gate_weight, preferred_element_type=jnp.float32
    )
    up_val = jnp.einsum(
        "tsecd,edf->tsecf", expert_rows, up_weight, preferred_element_type=jnp.float32
    )
    hidden = swiglu(gate_val, up_val).astype(jnp.bfloat16)
    result = jnp.einsum("tsecf,efd->tsecd", hidden, down_weight, preferred_element_type=jnp.float32)
    finished = lax.psum_scatter(
        result.reshape(1 * lax.axis_size("tp"), owners, local_experts * slots, width).astype(
            jnp.bfloat16
        ),
        "tp",
        scatter_dimension=0,
        tiled=True,
    )
    returned = return_rows(finished)
    result_rows = unpack(returned).astype(jnp.float32)
    output = (middle + jnp.sum(picked[:, :, None] * result_rows, axis=1)).astype(jnp.bfloat16)
    grad_out = cotangent.astype(jnp.float32)
    grad_picked = jnp.einsum("tkd,td->tk", result_rows, grad_out, precision=HIGH_PRECISION)
    onehot_float = (expert_ids[:, :, None] == jnp.arange(experts_all)[None, None, :]).astype(
        jnp.float32
    )
    grad_router = jnp.sum(onehot_float * (grad_picked * valid_float[:, None])[:, :, None], axis=1)
    _, soft_back = jax.vjp(softmax_rows, logits)
    grad_logits = soft_back(grad_router)[0]
    grad_result = (
        (picked[:, :, None] * grad_out[:, None, :])
        .astype(jnp.bfloat16)
        .reshape(quarter * chosen_count, width)
    )
    grad_sent = pack(grad_result)
    grad_arrived = group_rows(dispatch_rows(grad_sent))
    grad_rows = grad_arrived.reshape(groups, owners, local_experts, slots, width)
    gate_all = jnp.einsum(
        "tsecd,edf->tsecf", expert_rows, full_gate, preferred_element_type=jnp.float32
    )
    up_all = jnp.einsum(
        "tsecd,edf->tsecf", expert_rows, full_up, preferred_element_type=jnp.float32
    )
    hidden_all, swiglu_back = jax.vjp(swiglu, gate_all, up_all)
    hidden_low = hidden_all.astype(jnp.bfloat16)
    grad_hidden = jnp.einsum(
        "tsecd,efd->tsecf", grad_rows, full_down, preferred_element_type=jnp.float32
    )
    grad_gate_f, grad_up_f = swiglu_back(grad_hidden)
    grad_gate_rows = grad_gate_f.astype(jnp.bfloat16)
    grad_up_rows = grad_up_f.astype(jnp.bfloat16)
    down_grad = jnp.einsum(
        "tsecf,tsecd->efd", hidden_low, grad_rows, preferred_element_type=jnp.float32
    )
    gate_grad = jnp.einsum(
        "tsecd,tsecf->edf", expert_rows, grad_gate_rows, preferred_element_type=jnp.float32
    )
    up_grad = jnp.einsum(
        "tsecd,tsecf->edf", expert_rows, grad_up_rows, preferred_element_type=jnp.float32
    )
    summed = jnp.einsum(
        "tsecf,edf->tsecd", grad_gate_rows, gate_weight, preferred_element_type=jnp.float32
    )
    summed = summed + jnp.einsum(
        "tsecf,edf->tsecd", grad_up_rows, up_weight, preferred_element_type=jnp.float32
    )
    grad_finished = lax.psum_scatter(
        summed.reshape(1 * lax.axis_size("tp"), owners, local_experts * slots, width).astype(
            jnp.bfloat16
        ),
        "tp",
        scatter_dimension=0,
        tiled=True,
    )
    grad_returned = return_rows(grad_finished)
    grad_copies = unpack(grad_returned).astype(jnp.float32)
    router_float = router_weight.astype(jnp.float32)
    grad_moe_in = jnp.sum(grad_copies, axis=1) + jnp.dot(
        grad_logits, router_float.T, precision=HIGH_PRECISION
    )
    router_grad = jnp.dot(moe_in.astype(jnp.float32).T, grad_logits, precision=HIGH_PRECISION)
    _, norm_two_back = jax.vjp(rms_norm, middle, moe_gain)
    grad_mid_norm, moe_gain_grad = norm_two_back(grad_moe_in)
    grad_middle = grad_out + grad_mid_norm
    grad_branch = lax.all_gather(grad_middle.astype(jnp.bfloat16), "tp", axis=0, tiled=True)
    out_grad = jnp.einsum("sh,sd->hd", attended, grad_branch, preferred_element_type=jnp.float32)
    grad_attended = jnp.einsum(
        "sd,hd->sh", grad_branch, out_weight, preferred_element_type=jnp.float32
    ).astype(jnp.bfloat16)
    grad_attended = grad_attended.reshape(seq_len, kv_heads, group_factor, head_size)
    query_parts = []
    key_total = jnp.zeros((seq_len, kv_heads, head_size), jnp.float32)
    value_total = jnp.zeros((seq_len, kv_heads, head_size), jnp.float32)
    for block_no, offset in enumerate(range(0, seq_len, height)):
        allowed = block_mask(segment_row, live_row, offset, height)
        scores = block_scores(query_val, key_val, allowed, factor)
        probs = jnp.where(allowed[None, None], jnp.exp(scores - log_sums[block_no]), 0.0)
        grad_probs = jnp.einsum(
            "qgrd,kgd->grqk", grad_attended, value_vectors, preferred_element_type=jnp.float32
        )
        centre = jnp.sum(probs * grad_probs, axis=-1, keepdims=True)
        grad_scores = (probs * (grad_probs - centre)).astype(jnp.bfloat16)
        query_parts.append(
            jnp.einsum("grqk,kgd->qgrd", grad_scores, key_val, preferred_element_type=jnp.float32)
            * factor
        )
        key_total = (
            jnp.einsum("grqk,qgrd->kgd", grad_scores, query_val, preferred_element_type=jnp.float32)
            * factor
        )
        value_total = jnp.einsum(
            "grqk,qgrd->kgd",
            probs.astype(jnp.bfloat16),
            grad_attended,
            preferred_element_type=jnp.float32,
        )
    grad_query_rot = query_parts[0]
    _, query_back = jax.vjp(lambda vectors: rotate(vectors, cos_query, sin_query), query_unrotated)
    _, key_back = jax.vjp(lambda vectors: rotate(vectors, cos_key, sin_key), key_unrotated)
    grad_q_pre = (
        query_back(grad_query_rot)[0].astype(jnp.bfloat16).reshape(seq_len, q_heads * head_size)
    )
    grad_k_pre = key_back(key_total)[0].astype(jnp.bfloat16).reshape(seq_len, kv_heads * head_size)
    grad_value = value_total.astype(jnp.bfloat16).reshape(seq_len, kv_heads * head_size)
    query_grad = jnp.einsum("sd,sh->dh", normed_all, grad_q_pre, preferred_element_type=jnp.float32)
    key_grad = jnp.einsum("sd,sh->dh", normed_all, grad_k_pre, preferred_element_type=jnp.float32)
    value_grad = jnp.einsum("sd,sh->dh", normed_all, grad_value, preferred_element_type=jnp.float32)
    summed = jnp.einsum("sh,dh->sd", grad_q_pre, query_matrix, preferred_element_type=jnp.float32)
    summed = summed + jnp.einsum(
        "sh,dh->sd", grad_k_pre, key_matrix, preferred_element_type=jnp.float32
    )
    summed = summed + jnp.einsum(
        "sh,dh->sd", grad_value, value_matrix, preferred_element_type=jnp.float32
    )
    grad_normed = lax.psum_scatter(
        summed.astype(jnp.bfloat16), "tp", scatter_dimension=0, tiled=True
    ).astype(jnp.float32)
    _, norm_one_back = jax.vjp(rms_norm, x_float, norm_gain)
    grad_x_norm, norm_gain_grad = norm_one_back(grad_normed)
    input_grad = grad_middle + grad_x_norm
    query_grad, key_grad, value_grad, out_grad = lax.psum(
        (query_grad, key_grad, value_grad, out_grad), "ep"
    )
    norm_gain_grad, moe_gain_grad, router_grad = lax.psum(
        (norm_gain_grad, moe_gain_grad, router_grad), ("ep", "tp")
    )
    return (
        output,
        input_grad,
        norm_gain_grad,
        query_grad,
        key_grad,
        value_grad,
        out_grad,
        moe_gain_grad,
        router_grad,
        gate_grad,
        up_grad,
        down_grad,
    )


def swap_core(value):
    return lax.ppermute(value, "tp", [(i, i ^ 1) for i in range(4)])


def swap_x(value):
    return lax.ppermute(value, "tp", [(i, i ^ 2) for i in range(4)])


def swap_y(value):
    owners = lax.axis_size("ep")
    return lax.ppermute(value, "ep", [(i, i ^ 1) for i in range(owners)])


def shift_z(value, step):
    owners = lax.axis_size("ep")
    return lax.ppermute(value, "ep", [(i, (i + 2 * step) % owners) for i in range(owners)])


def after(value, *others):
    return lax.optimization_barrier((value,) + others)[0]


def add_low(left, right):
    return (left.astype(jnp.float32) + right.astype(jnp.float32)).astype(jnp.bfloat16)


def gather_pieces(value):
    across = swap_x(value)
    other = swap_core(value)
    return value, other, across, swap_core(across)


def gather_tp(value):
    me = lax.axis_index("tp")
    rows = value.shape[0]
    full = jnp.zeros((4 * rows,) + value.shape[1:], value.dtype)
    for flip, part in enumerate(gather_pieces(value)):
        full = lax.dynamic_update_slice_in_dim(full, part, (me ^ flip) * rows, 0)
    return full


def scatter_tp(value, core_dtype):
    me = lax.axis_index("tp")
    core, across = me % 2, me // 2
    boxes = value.reshape((2, 2, value.shape[0] // 4) + value.shape[1:])
    leave = lax.dynamic_index_in_dim(boxes, 1 - core, 1, keepdims=False).astype(core_dtype)
    stay = lax.dynamic_index_in_dim(boxes, core, 1, keepdims=False)
    both = stay.astype(jnp.float32) + swap_core(leave).astype(jnp.float32)
    mine = lax.dynamic_index_in_dim(both, across, 0, keepdims=False)
    theirs = lax.dynamic_index_in_dim(both, 1 - across, 0, keepdims=False).astype(jnp.bfloat16)
    return mine + swap_x(theirs).astype(jnp.float32), theirs


def reduce_sends(own_core, arrived):
    return add_low(own_core[2], arrived[0]), add_low(own_core[3], arrived[1])


def reduce_second(boxes, from_x, from_y):
    own_core, arrived = boxes
    half = own_core.shape[1] // 2
    parts = []
    for part, extra in ((0, from_x), (1, from_y)):
        for rows in (slice(0, half), slice(half, 2 * half)):
            total = own_core[part, rows].astype(jnp.float32) + arrived[part, rows].astype(jnp.float32)
            parts.append((total + extra[rows].astype(jnp.float32)).astype(jnp.bfloat16))
    return parts


def join_kernel(first_ref, from_y_ref, last_ref, from_x_ref, grad_ref, out_ref):
    half, width = grad_ref.shape[0] // 2, grad_ref.shape[1]
    for ref, columns in ((grad_ref, slice(0, width)), (out_ref, slice(width, 2 * width))):
        ref[:half] = add_low(first_ref[:, columns], from_y_ref[:, columns])
        ref[half:] = add_low(last_ref[:, columns], from_x_ref[:, columns])


def reduce_home(first, from_y, last, from_x):
    half, width = first.shape
    like = jax.ShapeDtypeStruct((2 * half, width // 2), first.dtype)
    return pl.pallas_call(
        join_kernel,
        grid=(1,),
        in_specs=[pl.BlockSpec((half, width), lambda j: (0, 0))] * 4,
        out_specs=(pl.BlockSpec(like.shape, lambda j: (0, 0)),) * 2,
        out_shape=(like, like),
        name="join_halves",
    )(first, from_y, last, from_x)


def butterfly_sum(value):
    value = value + swap_core(value)
    value = value + swap_x(value)
    value = value + swap_y(value)
    value = value + shift_z(value, 2)
    owners = lax.axis_size("ep")
    return value + lax.ppermute(value, "ep", [(i, i ^ 2) for i in range(owners)])


def planes_of(boxes):
    planes = boxes.shape[0]
    plane = lax.axis_index("ep") // 2
    return [lax.dynamic_index_in_dim(boxes, (plane + i) % planes, 0, keepdims=False) for i in range(planes)]


def send_planes(parts):
    return [shift_z(part.astype(jnp.bfloat16), i) for i, part in enumerate(parts) if i]


def add_all(first, others):
    return first.astype(jnp.float32) + sum(part.astype(jnp.float32) for part in others)


def spread_planes(value):
    planes = lax.axis_size("ep") // 2
    return [value] + [shift_z(value, i) for i in range(1, planes)]


def join_planes(parts):
    planes, plane = len(parts), lax.axis_index("ep") // 2
    full = jnp.zeros((planes,) + parts[0].shape, parts[0].dtype)
    for i, part in enumerate(parts):
        full = lax.dynamic_update_index_in_dim(full, part, (plane - i) % planes, 0)
    return full


def sides_of(boxes):
    y = lax.axis_index("ep") % 2
    return [lax.dynamic_index_in_dim(boxes, i, 0, keepdims=False) for i in (y, 1 - y)]


def join_sides(own, other):
    y = lax.axis_index("ep") % 2
    full = jnp.zeros((2,) + own.shape, own.dtype)
    full = lax.dynamic_update_index_in_dim(full, own, y, 0)
    return lax.dynamic_update_index_in_dim(full, other, 1 - y, 0)


FIRST_HALF = ((0, 0), (2, 0), (0, 1), (2, 1))
LAST_HALF = ((1, 0), (1, 1), (3, 0), (3, 1))
NT = (((1,), (1,)), ((), ()))
TN = (((0,), (0,)), ((), ()))


def dot_f32(left, right, dims=None):
    if dims is None:
        return jnp.dot(left, right, preferred_element_type=jnp.float32)
    return lax.dot_general(left, right, dims, preferred_element_type=jnp.float32)


def choose(index, values):
    out = values[0]
    for i in range(1, len(values)):
        out = jnp.where(index == i, values[i], out)
    return out


def expert_kernel(sizes, *refs):
    experts, slots, blocks, rows, routed = sizes
    x_parts, g_ref = refs[:8], refs[8]
    base_ref, order_ref, router_ref, gate_ref, up_ref, down_ref = refs[9:15]
    own_ref, keep_ref, send_ref, xr_out, gr_out, dgu_ref, wh_ref, rg_ref = refs[15:23]
    xs, gs, xr, gr, wgu, wd, back, picks, probs, weight, d_weight, table, leaving, tables = refs[23:37]
    x_sem, g_sem, w_sem, out_sem, leave_sem, t_sem = refs[37:43]
    width = xs.shape[1]
    units = wd.shape[1]
    total = experts * slots
    depth = blocks * slots
    def source_rows(b):
        return pl.ds(pl.multiple_of(order_ref[b] * rows, rows), rows)

    for b in range(blocks):
        pltpu.make_async_copy(x_parts[b], xs.at[pl.ds(b * rows, rows)], x_sem.at[b]).start()
        pltpu.make_async_copy(g_ref.at[source_rows(b), pl.ds(width, tables.shape[2])], tables.at[b], t_sem.at[b]).start()
    rg_ref[...] = jnp.zeros_like(rg_ref)

    def block_rows(b):
        return pl.ds(pl.multiple_of(b * rows, rows), rows)

    def slot_rows(b):
        return pl.ds(pl.multiple_of(b * slots, slots), slots)

    def expand(values):
        return jnp.concatenate([jnp.broadcast_to(values[e], (slots, rows)) for e in range(experts)], axis=0)

    place = jnp.concatenate(
        [lax.broadcasted_iota(jnp.int32, (slots, rows), 0)] * experts, axis=0
    ).astype(jnp.float32)

    def gather_x(b, carry):
        pltpu.make_async_copy(xs.at[block_rows(b)], xs.at[block_rows(b)], x_sem.at[b]).wait()
        pltpu.make_async_copy(tables.at[b], tables.at[b], t_sem.at[b]).wait()
        pltpu.make_async_copy(g_ref.at[source_rows(b), pl.ds(0, width)], gs.at[block_rows(b)], g_sem.at[b]).start()

        @pl.when(b < experts)
        def _():
            pltpu.make_async_copy(gate_ref.at[b], wgu.at[b, :, pl.ds(0, units)], w_sem.at[0, b]).start()
            pltpu.make_async_copy(up_ref.at[b], wgu.at[b, :, pl.ds(units, units)], w_sem.at[1, b]).start()
            pltpu.make_async_copy(down_ref.at[b], wd.at[b], w_sem.at[2, b]).start()

        x_block = xs[block_rows(b), :]
        logits = dot_f32(router_ref[...], x_block, NT)
        lane = lax.broadcasted_iota(jnp.int32, logits.shape, 0)
        logits = jnp.where(lane < routed, logits, -1e30)
        expo = jnp.exp(logits - jnp.max(logits, axis=0, keepdims=True))
        prob = expo / jnp.sum(expo, axis=0, keepdims=True)
        probs[b] = prob
        table[...] = tables[b].astype(jnp.float32).T
        hit = expand([table[pl.ds(base_ref[0] + e, 1), :] for e in range(experts)]) == place
        prob_rows = expand([prob[e : e + 1, :] for e in range(experts)])
        chosen = jnp.sum(jnp.where(hit, prob_rows, 0.0), axis=1, keepdims=True)
        chosen = jnp.broadcast_to(chosen, (total, rows))
        one = hit.astype(jnp.float32).astype(jnp.bfloat16)
        picks[b] = one
        taken = dot_f32(one, x_block).astype(jnp.bfloat16)
        for e in range(experts):
            xr[e, slot_rows(b), :] = taken[e * slots : (e + 1) * slots]
            weight[e, slot_rows(b), :] = chosen[e * slots : (e + 1) * slots]
        back[b, pl.ds(total, router_ref.shape[0]), :width] = router_ref[...]
        back[b, pl.ds(total, router_ref.shape[0]), width:] = jnp.zeros_like(router_ref)
        return carry

    def gather_g(b, carry):
        pltpu.make_async_copy(gs.at[block_rows(b)], gs.at[block_rows(b)], g_sem.at[b]).wait()
        taken = dot_f32(picks[b], gs[block_rows(b), :]).astype(jnp.bfloat16)
        for e in range(experts):
            gr[e, slot_rows(b), :] = taken[e * slots : (e + 1) * slots]
        return carry

    lax.fori_loop(0, blocks, gather_x, 0)
    pltpu.make_async_copy(xr, xr_out, out_sem.at[0]).start()
    lax.fori_loop(0, blocks, gather_g, 0)
    pltpu.make_async_copy(gr, gr_out, out_sem.at[1]).start()

    def one_expert(e, carry):
        low, high = pl.ds(0, units), pl.ds(units, units)
        pltpu.make_async_copy(wgu.at[e, :, low], wgu.at[e, :, low], w_sem.at[0, e]).wait()
        pltpu.make_async_copy(wgu.at[e, :, high], wgu.at[e, :, high], w_sem.at[1, e]).wait()
        pltpu.make_async_copy(wd.at[e], wd.at[e], w_sem.at[2, e]).wait()
        both = dot_f32(xr[e], wgu[e])
        gate, up = both[:, :units], both[:, units:]
        back_hidden = dot_f32(gr[e], wd[e], NT)
        sig = 1.0 / (1.0 + jnp.exp(-gate))
        silu = gate * sig
        hidden = silu * up
        product = hidden.astype(jnp.bfloat16).astype(jnp.float32) * back_hidden
        d_weight[e] = jnp.broadcast_to(jnp.sum(product, axis=1, keepdims=True), (depth, rows))
        share = weight[e]
        d_hidden = share * back_hidden
        d_gate = d_hidden * up * (sig * (1.0 + gate * (1.0 - sig)))
        d_up = d_hidden * silu
        d_both = jnp.concatenate([d_gate, d_up], axis=1).astype(jnp.bfloat16)
        dgu_ref[e] = d_both
        weighted = (share * hidden).astype(jnp.bfloat16)
        wh_ref[e] = weighted
        d_rows = dot_f32(d_both, wgu[e], NT).astype(jnp.bfloat16)
        for b in range(blocks):
            back[b, slot_rows(e), :width] = d_rows[b * slots : (b + 1) * slots]
        out_rows = dot_f32(weighted, wd[e]).astype(jnp.bfloat16)
        for b in range(blocks):
            back[b, slot_rows(e), width:] = out_rows[b * slots : (b + 1) * slots]
        return carry

    lax.fori_loop(0, experts, one_expert, 0)

    half = rows // 2

    def left(turn):
        pltpu.make_async_copy(leaving.at[turn], leaving.at[turn], leave_sem.at[turn]).wait()

    def scatter(b, carry):
        one = picks[b]
        d_slot = jnp.concatenate([d_weight[e, slot_rows(b), :] for e in range(experts)], axis=0)
        spread = one.astype(jnp.float32) * d_slot
        d_prob = jnp.concatenate(
            [jnp.sum(spread[e * slots : (e + 1) * slots], axis=0, keepdims=True) for e in range(experts)]
            + [jnp.zeros((router_ref.shape[0] - experts, rows), jnp.float32)],
            axis=0,
        )
        prob = probs[b]
        centre = jnp.sum(prob * d_prob, axis=0, keepdims=True)
        d_logits = (prob * (d_prob - centre)).astype(jnp.bfloat16)
        rg_ref[...] += dot_f32(d_logits, xs[block_rows(b), :])
        turn = b % 2

        @pl.when(b >= 2)
        def _():
            left(turn)

        leaving[turn] = dot_f32(jnp.concatenate([one, d_logits], axis=0), back[b], TN).astype(jnp.bfloat16)
        for i, table_of in enumerate((FIRST_HALF, LAST_HALF)):
            part = choose(b % 4, [place[0] for place in table_of])
            row = choose(b % 4, [place[1] for place in table_of]) * half
            place_rows = pl.ds(pl.multiple_of(row, half), half)
            for ref, index, mine in (
                (own_ref, part, b < 4),
                (keep_ref, part, (b >= 4) & (part < 2)),
                (send_ref, part - 2, (b >= 4) & (part >= 2)),
            ):

                @pl.when(mine)
                def _(ref=ref, index=index, place_rows=place_rows, i=i):
                    pltpu.make_async_copy(
                        leaving.at[turn, pl.ds(i * half, half)], ref.at[index, place_rows], leave_sem.at[turn]
                    ).start()

        return carry

    lax.fori_loop(0, blocks, scatter, 0)
    left(0)
    left(1)
    pltpu.make_async_copy(xr, xr_out, out_sem.at[0]).wait()
    pltpu.make_async_copy(gr, gr_out, out_sem.at[1]).wait()


def expert_call(x_parts, g_all, base, order, router_rows, gate_weight, up_weight, down_weight, routed, slots):
    blocks = len(x_parts)
    rows, width = x_parts[0].shape
    experts, _, units = gate_weight.shape
    depth = blocks * slots
    padded = router_rows.shape[0]
    extra = g_all.shape[1] - width
    low, full = jnp.bfloat16, jnp.float32
    any_spec = pl.BlockSpec(memory_space=pl.ANY)
    vmem_spec = pl.BlockSpec(memory_space=pltpu.VMEM)
    smem_spec = pl.BlockSpec(memory_space=pltpu.SMEM)
    return pl.pallas_call(
        lambda *refs: expert_kernel((experts, slots, blocks, rows, routed), *refs),
        out_shape=(
            jax.ShapeDtypeStruct((4, rows, 2 * width), low),
            jax.ShapeDtypeStruct((2, rows, 2 * width), low),
            jax.ShapeDtypeStruct((2, rows, 2 * width), low),
            jax.ShapeDtypeStruct((experts, depth, width), low),
            jax.ShapeDtypeStruct((experts, depth, width), low),
            jax.ShapeDtypeStruct((experts, depth, 2 * units), low),
            jax.ShapeDtypeStruct((experts, depth, units), low),
            jax.ShapeDtypeStruct((padded, width), full),
        ),
        in_specs=[any_spec] * 9 + [smem_spec, smem_spec, vmem_spec] + [any_spec] * 3,
        out_specs=(any_spec,) * 5 + (vmem_spec,) * 3,
        scratch_shapes=[
            pltpu.VMEM((blocks * rows, width), low),
            pltpu.VMEM((blocks * rows, width), low),
            pltpu.VMEM((experts, depth, width), low),
            pltpu.VMEM((experts, depth, width), low),
            pltpu.VMEM((experts, width, 2 * units), low),
            pltpu.VMEM((experts, units, width), low),
            pltpu.VMEM((blocks, experts * slots + padded, 2 * width), low),
            pltpu.VMEM((blocks, experts * slots, rows), low),
            pltpu.VMEM((blocks, padded, rows), full),
            pltpu.VMEM((experts, depth, rows), full),
            pltpu.VMEM((experts, depth, rows), full),
            pltpu.VMEM((extra, rows), full),
            pltpu.VMEM((2, rows, 2 * width), low),
            pltpu.VMEM((blocks, rows, extra), low),
            pltpu.SemaphoreType.DMA((blocks,)),
            pltpu.SemaphoreType.DMA((blocks,)),
            pltpu.SemaphoreType.DMA((3, experts)),
            pltpu.SemaphoreType.DMA((2,)),
            pltpu.SemaphoreType.DMA((2,)),
            pltpu.SemaphoreType.DMA((blocks,)),
        ],
        compiler_params=pltpu.CompilerParams(vmem_limit_bytes=58 * 2**20),
        cost_estimate=pl.CostEstimate(
            flops=2 * experts * depth * width * units * 40, bytes_accessed=60 * 2**20, transcendentals=0
        ),
        name="expert_chunk",
    )(*x_parts, g_all, base, order, router_rows, gate_weight, up_weight, down_weight)


def weight_kernel(count, *refs):
    xr, gr, dgu, wh = (refs[i * count : (i + 1) * count] for i in range(4))
    gate_ref, up_ref, down_ref = refs[4 * count :]
    units = gate_ref.shape[2]
    both = sum(dot_f32(x[0], d[0], TN) for x, d in zip(xr, dgu))
    gate_ref[0] = both[:, :units]
    up_ref[0] = both[:, units:]
    down_ref[0] = sum(dot_f32(h[0], g[0], TN) for h, g in zip(wh, gr))


def weight_call(xr, gr, dgu, wh):
    count = len(xr)
    experts, depth, width = xr[0].shape
    units = wh[0].shape[2]
    spec = lambda array: pl.BlockSpec((1,) + array.shape[1:], lambda e: (e, 0, 0))
    operands = [*xr, *gr, *dgu, *wh]
    up_like = jax.ShapeDtypeStruct((experts, width, units), jnp.float32)
    down_like = jax.ShapeDtypeStruct((experts, units, width), jnp.float32)
    return pl.pallas_call(
        lambda *refs: weight_kernel(count, *refs),
        grid=(experts,),
        out_shape=(up_like, up_like, down_like),
        in_specs=[spec(a) for a in operands],
        out_specs=(spec(up_like), spec(up_like), spec(down_like)),
        compiler_params=pltpu.CompilerParams(vmem_limit_bytes=50 * 2**20),
        cost_estimate=pl.CostEstimate(
            flops=2 * experts * depth * count * width * units * 3,
            bytes_accessed=60 * 2**20,
            transcendentals=0,
        ),
        name="expert_weights",
    )(*operands)


def swap_halves(values, half):
    lane = lax.broadcasted_iota(jnp.int32, values.shape, 1)
    size = values.shape[1]
    return jnp.where(
        lane % (2 * half) < half, pltpu.roll(values, size - half, 1), pltpu.roll(values, half, 1)
    )


def branch_back_kernel(*refs):
    parts, me_ref, att_ref, wo_ref, back_ref, out_ref, branch, sem = refs[:4], *refs[4:]
    rows = parts[0].shape[0]
    for flip, part in enumerate(parts):
        target = pl.ds(pl.multiple_of((me_ref[0] ^ flip) * rows, rows), rows)
        pltpu.make_async_copy(part, branch.at[target], sem.at[flip]).start()
    for flip, part in enumerate(parts):
        target = pl.ds(pl.multiple_of((me_ref[0] ^ flip) * rows, rows), rows)
        pltpu.make_async_copy(part, branch.at[target], sem.at[flip]).wait()
    out_part = dot_f32(att_ref[...], branch[...], TN).astype(jnp.bfloat16)
    _, planes, size, _ = out_ref.shape
    for i in range(2 * planes):
        out_ref[me_ref[1] ^ (i // planes), i % planes] = out_part[i * size : (i + 1) * size]
    back_ref[...] = dot_f32(branch[...], wo_ref[...], NT).astype(jnp.bfloat16)


def branch_back_call(parts, attended, wo):
    rows, width = parts[0].shape
    seq_len, q_width = attended.shape
    planes = lax.axis_size("ep") // 2
    me = jnp.stack([lax.axis_index("tp"), lax.axis_index("ep") % 2]).astype(jnp.int32)
    vmem_spec = pl.BlockSpec(memory_space=pltpu.VMEM)
    return pl.pallas_call(
        branch_back_kernel,
        out_shape=(
            jax.ShapeDtypeStruct((seq_len, q_width), jnp.bfloat16),
            jax.ShapeDtypeStruct((2, planes, q_width // planes // 2, width), jnp.bfloat16),
        ),
        in_specs=[pl.BlockSpec(memory_space=pl.ANY)] * 4 + [pl.BlockSpec(memory_space=pltpu.SMEM)] + [vmem_spec] * 2,
        out_specs=(vmem_spec,) * 2,
        scratch_shapes=[pltpu.VMEM((seq_len, width), jnp.bfloat16), pltpu.SemaphoreType.DMA((4,))],
        compiler_params=pltpu.CompilerParams(vmem_limit_bytes=24 * 2**20),
        cost_estimate=pl.CostEstimate(
            flops=4 * seq_len * width * q_width, bytes_accessed=8 * 2**20, transcendentals=0
        ),
        name="branch_back",
    )(*parts, me, attended, wo)


def attention_back_kernel(sizes, *refs):
    group_factor, head_size = sizes
    me_ref, back, q_ref, k_ref, v_ref, normed_ref, wq_ref, wk_ref, wv_ref = refs[:9]
    cos_ref, sin_ref, column_ref, row_ref, live_ref = refs[9:14]
    weights_ref, stay_ref, leave_ref = refs[14:17]
    d_q, d_k, d_v, d_all = refs[17:21]
    seq_len = q_ref.shape[0]
    rows = stay_ref.shape[1]
    factor = 1.0 / math.sqrt(head_size)
    me = me_ref[0]

    def place(flip):
        return pl.ds(pl.multiple_of((me ^ flip) * rows, rows), rows)

    d_k[...] = jnp.zeros_like(d_k)
    d_v[...] = jnp.zeros_like(d_v)
    step = seq_len // 2
    for start in (0, step):
        keys = start + step
        shape = (step, keys)
        query_place = start + lax.broadcasted_iota(jnp.int32, shape, 0)
        key_place = lax.broadcasted_iota(jnp.int32, shape, 1)
        same = column_ref[start : start + step, :] == row_ref[:, :keys]
        usable = (live_ref[:, :keys] > 0) | (key_place == query_place)
        allowed = same & (key_place <= query_place) & usable
        for head in range(q_ref.shape[1] // head_size):
            group = head // group_factor
            mine = slice(head * head_size, (head + 1) * head_size)
            shared = slice(group * head_size, (group + 1) * head_size)
            query = q_ref[start : start + step, mine]
            key, value = k_ref[:keys, shared], v_ref[:keys, shared]
            d_out = back[start : start + step, mine]
            scores = jnp.where(allowed, dot_f32(query, key, NT) * factor, -1e30)
            expo = jnp.exp(scores - jnp.max(scores, axis=1, keepdims=True))
            probs = expo * (1.0 / jnp.sum(expo, axis=1, keepdims=True))
            d_probs = dot_f32(d_out, value, NT)
            centre = jnp.sum(probs * d_probs, axis=1, keepdims=True)
            d_scores = (probs * (d_probs - centre)).astype(jnp.bfloat16)
            d_q[start : start + step, mine] = dot_f32(d_scores, key) * factor
            d_k[:keys, shared] += dot_f32(d_scores, query, TN) * factor
            d_v[:keys, shared] += dot_f32(probs.astype(jnp.bfloat16), d_out, TN)
    pair = 2 * head_size
    q_width = q_ref.shape[1]
    kv_width = k_ref.shape[1]
    for source, count, offset in ((d_q, q_width // pair, 0), (d_k, kv_width // pair, q_width)):
        for i in range(count):
            turned = source[:, i * pair : (i + 1) * pair]
            flat = turned * cos_ref[...] + swap_halves(turned, head_size // 2) * sin_ref[...]
            d_all[:, offset + i * pair : offset + (i + 1) * pair] = flat.astype(jnp.bfloat16)
    d_all[:, q_width + kv_width :] = d_v[...].astype(jnp.bfloat16)
    size = weights_ref.shape[1] // 6
    for i in range(12):
        part = dot_f32(normed_ref[:, i * size : (i + 1) * size], d_all[...], TN).astype(jnp.bfloat16)
        weights_ref[me_ref[1] ^ (i // 6), i % 6 * size : (i % 6 + 1) * size] = part
    for flip in range(4):
        values = d_all[place(flip), :]
        total = dot_f32(values[:, :q_width], wq_ref[...], NT)
        total += dot_f32(values[:, q_width : q_width + kv_width], wk_ref[...], NT)
        total += dot_f32(values[:, q_width + kv_width :], wv_ref[...], NT)
        if flip % 2:
            leave_ref[flip // 2] = total.astype(jnp.bfloat16)
        else:
            stay_ref[flip // 2] = total


def attention_back_call(back, query, key, value, normed, wq, wk, wv, cos, sin, segments, live, factor):
    seq_len, q_width = query.shape
    width, kv_width = wk.shape
    rows = seq_len // 4
    me = jnp.stack([lax.axis_index("tp"), lax.axis_index("ep") % 2]).astype(jnp.int32)
    low, full = jnp.bfloat16, jnp.float32
    vmem_spec = pl.BlockSpec(memory_space=pltpu.VMEM)
    cos_pair = jnp.tile(cos, (1, 4))
    sin_pair = jnp.tile(jnp.concatenate([sin, -sin], axis=1), (1, 2))
    return pl.pallas_call(
        lambda *refs: attention_back_kernel((factor, HEAD_SIZE_DIM), *refs),
        out_shape=(
            jax.ShapeDtypeStruct((2, width // 2, q_width + 2 * kv_width), low),
            jax.ShapeDtypeStruct((2, rows, width), full),
            jax.ShapeDtypeStruct((2, rows, width), low),
        ),
        in_specs=[pl.BlockSpec(memory_space=pltpu.SMEM)] + [vmem_spec] * 13,
        out_specs=(vmem_spec,) * 3,
        scratch_shapes=[
            pltpu.VMEM((seq_len, q_width), full),
            pltpu.VMEM((seq_len, kv_width), full),
            pltpu.VMEM((seq_len, kv_width), full),
            pltpu.VMEM((seq_len, q_width + 2 * kv_width), low),
        ],
        compiler_params=pltpu.CompilerParams(vmem_limit_bytes=48 * 2**20),
        cost_estimate=pl.CostEstimate(
            flops=2 * seq_len * width * (2 * q_width + 4 * kv_width) * 2 * 6,
            bytes_accessed=60 * 2**20,
            transcendentals=0,
        ),
        name="attention_back",
    )(
        me, back, query, key, value, normed, wq, wk, wv, cos_pair, sin_pair,
        segments.reshape(-1, 1), segments.reshape(1, -1), live.reshape(1, -1),
    )


def local_gathered(
    tokens,
    norm_gain,
    query_matrix,
    key_matrix,
    value_matrix,
    out_weight,
    moe_gain,
    router_weight,
    gate_weight,
    up_weight,
    down_weight,
    cotangent,
    expert_ids,
    segments,
    valid_mask,
):
    quarter = tokens.shape[0]
    width = tokens.shape[1]
    groups = lax.axis_size("tp")
    owners = lax.axis_size("ep")
    my_part = lax.axis_index("tp")
    seq_len = quarter * groups
    head_size = HEAD_SIZE_DIM
    kv_heads = key_matrix.shape[1] // head_size
    q_heads = query_matrix.shape[1] // head_size
    group_factor = q_heads // kv_heads
    local_experts = gate_weight.shape[0]
    experts_all = router_weight.shape[1]
    chosen_count = expert_ids.shape[1]
    slots = max(8, 3 * quarter * chosen_count // (2 * experts_all) // 8 * 8)
    factor = 1.0 / math.sqrt(head_size)
    segment_row = segments[0]
    live_row = valid_mask[0]
    x_float = tokens.astype(jnp.float32)
    planes = owners // 2
    owner = lax.axis_index("ep")
    my_valid = lax.dynamic_slice_in_dim(live_row, my_part * quarter, quarter, 0)
    padded = -(-experts_all // 16) * 16
    named = jnp.any(expert_ids[:, :, None] == jnp.arange(padded)[None, None, :], axis=1) & (my_valid[:, None] > 0)
    before = (jnp.arange(quarter)[None, :] < jnp.arange(quarter)[:, None]).astype(jnp.bfloat16)
    earlier = jnp.dot(before, named.astype(jnp.bfloat16), preferred_element_type=jnp.float32)
    slot = jnp.where(named, earlier, -1.0).astype(jnp.bfloat16)
    slot = jnp.pad(slot, ((0, 0), (0, -padded % 128)), constant_values=-1.0)
    sent = jnp.concatenate([cotangent, slot], axis=1)
    g_all = lax.all_gather(sent, ("ep", "tp"), axis=0, tiled=True)
    router_rows = jnp.roll(router_weight.T, -owner * local_experts, axis=0)
    router_rows = jnp.pad(router_rows, ((0, padded - experts_all), (0, 0)))
    base = (owner * local_experts).astype(jnp.int32)[None]
    step = jnp.arange(planes)[:, None]
    flip_y = jnp.array([0, 0, 1, 1, 0, 0, 1, 1])[None, :]
    flip_tp = jnp.array([0, 2, 0, 2, 1, 3, 1, 3])[None, :]
    order = (((owner // 2 - step) % planes) * 2 + (owner % 2 ^ flip_y)) * 4 + (my_part ^ flip_tp)
    order = order.astype(jnp.int32)
    tokens_all = gather_tp(tokens)
    normed_all = rms_norm(tokens_all.astype(jnp.float32), norm_gain).astype(jnp.bfloat16)
    query_unrotated = jnp.dot(normed_all, query_matrix, preferred_element_type=jnp.float32).reshape(
        seq_len, kv_heads, group_factor, head_size
    )
    key_unrotated = jnp.dot(normed_all, key_matrix, preferred_element_type=jnp.float32).reshape(
        seq_len, kv_heads, head_size
    )
    value_vectors = (
        jnp.dot(normed_all, value_matrix, preferred_element_type=jnp.float32)
        .astype(jnp.bfloat16)
        .reshape(seq_len, kv_heads, head_size)
    )
    cos_table, sin_table = angle_tables(seq_len, head_size)
    cos_query = cos_table[:, None, None, :]
    sin_query = sin_table[:, None, None, :]
    cos_key = cos_table[:, None, :]
    sin_key = sin_table[:, None, :]
    query_val = rotate(query_unrotated, cos_query, sin_query).astype(jnp.bfloat16)
    key_val = rotate(key_unrotated, cos_key, sin_key).astype(jnp.bfloat16)
    height = min(512, seq_len)
    offset = 0
    allowed = block_mask(segment_row, live_row, offset, height)
    scores = block_scores(query_val, key_val, allowed, factor)
    peak = jnp.max(scores, axis=-1, keepdims=True)
    expo = jnp.exp(scores - peak)
    denom = jnp.sum(expo, axis=-1, keepdims=True)
    weights = (expo / denom).astype(jnp.bfloat16)
    mixed = jnp.einsum("grqk,kgd->qgrd", weights, value_vectors, preferred_element_type=jnp.float32)
    outputs = mixed.reshape(height, q_heads * head_size)
    log_sums = [peak + jnp.log(denom)]
    attended = outputs.astype(jnp.bfloat16)
    branch, _ = scatter_tp(
        jnp.dot(attended, out_weight, preferred_element_type=jnp.float32), jnp.float32
    )
    middle = x_float + branch
    moe_in = rms_norm(middle, moe_gain).astype(jnp.bfloat16)
    barrier = lax.optimization_barrier
    columns, cross, diagonal, swapped, far = [moe_in], {}, {}, {}, {}

    def send_cross(step):
        cross[step] = (swap_x(columns[step]), swap_y(columns[step]))

    def send_diagonal(step):
        diagonal[step] = swap_x(cross[step][1]) if step % 2 else swap_y(cross[step][0])

    def send_swapped(step):
        swapped[step] = tuple(swap_core(part) for part in (columns[step], *cross[step]))

    send_cross(0)
    columns.append(shift_z(columns[0], 1))
    columns[1], cross = barrier((columns[1], cross))
    send_cross(1)
    columns.append(shift_z(columns[1], 1))
    columns[2], cross = barrier((columns[2], cross))
    send_diagonal(1)
    send_swapped(1)
    send_cross(2)
    columns.append(shift_z(columns[2], 1))
    columns[3], cross, diagonal, swapped = barrier((columns[3], cross, diagonal, swapped))
    far[1] = swap_core(diagonal[1])
    turns = [*range(1, planes), 0]
    kept, grad_parts, out_joined = [], [], []
    own, keep, send, arrived, from_x, from_y, halves, second = {}, {}, {}, {}, {}, {}, {}, {}
    for stage in range(planes + 3):
        ready, sends, joined = [], None, None
        a, b, c = stage - 1, stage - 2, stage - 3
        if a in send:
            sends = reduce_sends(own[a], swap_core(send[a]))
            ready += sends
            if stage >= 3:
                arrived[a] = swap_core(keep[a])
                ready += [arrived[a]]
        if b in from_x:
            halves[b] = reduce_second((own[b], arrived[b]), from_x[b], from_y[b])
            ready += halves[b]
        if c in second:
            joined = reduce_home(halves[c][0], second[c][0], halves[c][2], second[c][1])
            joined, out_part = joined
            out_joined.append(out_part)
            ready += [joined]
            if turns[c] == 0:
                grad_parts.append(joined)
                joined = None
        came = {}
        if stage < planes:
            step = turns[stage]
            x_parts = (columns[step], *cross[step], diagonal[step], *swapped[step], far[step])
            if stage == 0:
                send_diagonal(2)
                send_cross(3)
                send_swapped(2)
                came["gather"] = (diagonal[2], cross[3], swapped[2])
            if stage == 1:
                send_diagonal(3)
                send_diagonal(0)
                send_swapped(3)
                came["gather"] = (diagonal[3], diagonal[0], swapped[3])
            if stage == 2:
                send_swapped(0)
                came["gather"] = (swapped[0],)
            own[stage], keep[stage], send[stage], *rest = expert_call(
                x_parts, g_all, base, order[step], after(router_rows, *ready),
                gate_weight, up_weight, down_weight, experts_all, slots,
            )
            kept.append(rest)
            came["kernel"] = (own[stage], keep[stage], send[stage])
        if stage == planes:
            out_home = {0: shift_z(out_joined[0], -turns[0])}
            came["output"] = out_home[0]
            xr, gr, dgu, wh, router_parts = zip(*kept)
            came["weights"] = weight_call(xr, gr, (after(dgu[0], *ready),) + dgu[1:], wh)
        if sends:
            if stage < 3:
                came["core"] = swap_core(keep[a])
            came["cross"] = (swap_x(sends[0]), swap_y(sends[1]))
        if b in halves:
            came["second"] = (swap_y(halves[b][1]), swap_x(halves[b][3]))
        if joined is not None:
            came["home"] = shift_z(joined, -turns[c])
        came = barrier(came)
        if stage == 0:
            diagonal[2], cross[3], swapped[2] = came["gather"]
            far[2] = swap_core(diagonal[2])
        if stage == 1:
            diagonal[3], diagonal[0], swapped[3] = came["gather"]
            far[3], far[0] = swap_core(diagonal[3]), swap_core(diagonal[0])
        if stage == 2:
            (swapped[0],) = came["gather"]
        if "kernel" in came:
            own[stage], keep[stage], send[stage] = came["kernel"]
        if "weights" in came:
            out_home[0] = came["output"]
            gate_grad, up_grad, down_grad = came["weights"]
        if "core" in came:
            arrived[a] = came["core"]
        if "cross" in came:
            from_x[a], from_y[a] = came["cross"]
        if "second" in came:
            second[b] = came["second"]
        if "home" in came:
            grad_parts.append(came["home"])
    grad_moe_in = sum(part.astype(jnp.float32) for part in grad_parts)
    router_part = jnp.roll(sum(router_parts)[:experts_all], owner * local_experts, axis=0)
    grad_out = cotangent.astype(jnp.float32)
    _, norm_two_back = jax.vjp(rms_norm, middle, moe_gain)
    grad_mid_norm, moe_gain_grad = norm_two_back(grad_moe_in)
    grad_middle = grad_out + grad_mid_norm
    branch_parts = gather_pieces(grad_middle.astype(jnp.bfloat16))
    out_home[1] = shift_z(out_joined[1], -turns[1])
    flat = lambda array: array.reshape(seq_len, -1)
    back, out_grad = branch_back_call(branch_parts, attended, out_weight)
    out_came = swap_y(out_grad[1])
    weights, stay, leave = attention_back_call(
        back, flat(query_val), flat(key_val), flat(value_vectors), normed_all,
        query_matrix, key_matrix, value_matrix, cos_table, sin_table, segment_row, live_row, group_factor,
    )
    weights, stay, leave, out_came, out_home[1] = barrier((weights, stay, leave, out_came, out_home[1]))
    weights = weights.reshape(2, planes, -1, weights.shape[-1])
    weights_came = swap_y(weights[1])
    out_parts = planes_of(add_low(out_grad[0], out_came))
    out_came = send_planes(out_parts)
    both = stay + swap_core(leave).astype(jnp.float32)
    out_came, both = barrier((out_came, both))
    across_came = swap_x(both[1].astype(jnp.bfloat16))
    out_sum = add_all(out_parts[0], out_came).astype(jnp.bfloat16)
    out_came = spread_planes(out_sum)
    weights_came, across_came, out_came = barrier((weights_came, across_came, out_came))
    weights_parts = planes_of(add_low(weights[0], weights_came))
    weights_came = send_planes(weights_parts)
    out_half = join_planes(out_came)
    out_came = swap_y(out_half)
    grad_normed = both[0] + across_came.astype(jnp.float32)
    _, norm_one_back = jax.vjp(rms_norm, x_float, norm_gain)
    grad_x_norm, norm_gain_grad = norm_one_back(grad_normed)
    input_grad = grad_middle + grad_x_norm
    small = jnp.concatenate([router_part, moe_gain_grad[None], norm_gain_grad[None]], axis=0)
    small = small + swap_core(small)
    small_came = swap_x(small)
    weights_came, small_came, out_came = barrier((weights_came, small_came, out_came))
    small = small + small_came
    small_came = swap_y(small)
    weights_sum = add_all(weights_parts[0], weights_came).astype(jnp.bfloat16)
    weights_came = spread_planes(weights_sum)
    weights_came, small_came = barrier((weights_came, small_came))
    small = small + small_came
    weights_half = join_planes(weights_came)
    weights_came = swap_y(weights_half)
    small_came = send_planes([small] * planes)
    out_home[2] = shift_z(after(out_joined[2], weights_half), -turns[2])
    weights_came, small_came, out_home[2] = barrier((weights_came, small_came, out_home[2]))
    small = add_all(small, small_came)
    expert_sum = sum(out_home[i].astype(jnp.float32) for i in range(planes - 1))
    expert_sum = expert_sum + out_joined[planes - 1].astype(jnp.float32)
    output = (middle + expert_sum).astype(jnp.bfloat16)
    out_grad = join_sides(out_half, out_came).reshape(-1, width).astype(jnp.float32)
    weights = join_sides(weights_half, weights_came).reshape(width, -1).astype(jnp.float32)
    q_width, kv_width = query_matrix.shape[1], key_matrix.shape[1]
    query_grad, key_grad, value_grad = jnp.split(weights, (q_width, q_width + kv_width), axis=1)
    router_grad, moe_gain_grad, norm_gain_grad = small[:experts_all].T, small[experts_all], small[experts_all + 1]
    return (
        output,
        input_grad,
        norm_gain_grad,
        query_grad,
        key_grad,
        value_grad,
        out_grad,
        moe_gain_grad,
        router_grad,
        gate_grad,
        up_grad,
        down_grad,
    )


def local(*operands):
    tokens, router_weight, gate_weight, expert_ids = operands[0], operands[7], operands[8], operands[12]
    quarter, experts_all = tokens.shape[0], router_weight.shape[1]
    slots = max(8, 3 * quarter * expert_ids.shape[1] // (2 * experts_all) // 8 * 8)
    gathers = lax.axis_size("tp") == 4 and lax.axis_size("ep") == 8 and gate_weight.shape[0] * slots >= quarter
    return (local_gathered if gathers else local_routed)(*operands)


def solution(mesh):
    in_specs = (
        P(("ep", "tp"), None),
        P(),
        P(None, "tp"),
        P(None, "tp"),
        P(None, "tp"),
        P("tp", None),
        P(),
        P(),
        P("ep", None, "tp"),
        P("ep", None, "tp"),
        P("ep", "tp", None),
        P(("ep", "tp"), None),
        P(("ep", "tp"), None),
        P("ep", None),
        P("ep", None),
    )
    out_specs = (
        P(("ep", "tp"), None),
        P(("ep", "tp"), None),
        P(),
        P(None, "tp"),
        P(None, "tp"),
        P(None, "tp"),
        P("tp", None),
        P(),
        P(),
        P("ep", None, "tp"),
        P("ep", None, "tp"),
        P("ep", "tp", None),
    )
    return jax.shard_map(local, mesh=mesh, in_specs=in_specs, out_specs=out_specs, check_vma=False)
```
